32 devices in a mesh: dp: 4 (over x, core), tensor: 8 (over z, y).
Axes of the slice: x: 2, y: 2, z: 4, core: 2. Of those that a mesh axis runs over, the one named last changes fastest.
Arguments:
- tokens: bfloat16 [12288, 1024], P(('dp', 'tensor')), may hold values from -6 to 6, as said below
- memory: bfloat16 [12288, 1024], P(('dp', 'tensor')), may hold values from -6 to 6, as said below
- self_qkv: bfloat16 [1024, 3, 1024], P(None, None, 'tensor'), may hold values from -1 to 1, as said below
- self_out: bfloat16 [1024, 1024], P('tensor'), may hold values from -3 to 3
- cross_q: bfloat16 [1024, 1024], P(None, 'tensor'), may hold values from -1 to 1, as said below
- cross_kv: bfloat16 [1024, 2, 1024], P(None, None, 'tensor'), may hold values from -1 to 1, as said below
- cross_out: bfloat16 [1024, 1024], P('tensor'), may hold values from -6 to 6
- hidden_weight: bfloat16 [1024, 4096], P(None, 'tensor'), may hold values from -0.1875 to 0.1875
- hidden_bias: bfloat16 [4096], P('tensor'), may hold values from -3 to 3
- output_weight: bfloat16 [4096, 1024], P('tensor'), may hold values from -0.75 to 0.75
- output_bias: float32 [1024], replicated, may hold values from -5 to 5
- norm_gain: float32 [3, 1024], replicated, may hold values from 0.25 to 1.75
- norm_shift: float32 [3, 1024], replicated, may hold values from -3 to 3
- grad_output: bfloat16 [12288, 1024], P(('dp', 'tensor')), may hold values from -6 to 6
Outputs:
- layer_output: bfloat16 [12288, 1024], P(('dp', 'tensor'))
- grad_tokens: float32 [12288, 1024], P(('dp', 'tensor'))
- grad_memory: float32 [12288, 1024], P(('dp', 'tensor'))
- grad_self_qkv: float32 [1024, 3, 1024], P(None, None, 'tensor')
- grad_self_out: float32 [1024, 1024], P('tensor')
- grad_cross_q: float32 [1024, 1024], P(None, 'tensor')
- grad_cross_kv: float32 [1024, 2, 1024], P(None, None, 'tensor')
- grad_cross_out: float32 [1024, 1024], P('tensor')
- grad_hidden_weight: float32 [1024, 4096], P(None, 'tensor')
- grad_hidden_bias: float32 [4096], P('tensor')
- grad_output_weight: float32 [4096, 1024], P('tensor')
- grad_output_bias: float32 [1024], replicated
- grad_norm_gain: float32 [3, 1024], replicated
- grad_norm_shift: float32 [3, 1024], replicated
The draws below stay inside these ranges and needn't reach their ends.
Inputs may be any that keep to these rules, and one draw needn't show every extreme that they name: `tokens`: independent entries of mean zero and deviation one. `memory`: independent entries of mean zero and deviation one. `self_qkv`: independent entries of mean zero and deviation 1 / sqrt(1024). `cross_q`: independent entries of mean zero and deviation 1 / sqrt(1024). `cross_kv`: independent entries of mean zero and deviation 1 / sqrt(1024).
All inputs are finite; a program needn't handle non-finite values.
Results may differ from the reference program's by a relative error of at most 0.023.
Values may be sent and summed in bfloat16 or wider, within the bound.
A program may use at most 256 MiB of HBM per device.

```python
import math
import jax
import jax.numpy as jnp
from jax import lax

D = 1024
H = 16
DH = 64
FF = 4096
LEN = 1024
MEM = 1024
NSEQ = 12
TOKENS = 12288
MTOKENS = 12288


def normal_part(key, shape, factor):
    return jnp.clip(jax.random.normal(key, shape, jnp.float32), -6.0, 6.0) * factor


def draw_tokens(key, part):
    key = jax.random.fold_in(key, 11)
    values = normal_part(key, (TOKENS, D), 1.0)
    return values.astype(jnp.bfloat16)


def draw_memory(key, part):
    key = jax.random.fold_in(key, 12)
    values = normal_part(key, (MTOKENS, D), 1.0)
    return values.astype(jnp.bfloat16)


def draw_self_qkv(key, part):
    key = jax.random.fold_in(key, 13)
    values = normal_part(key, (D, 3, D), D ** (-0.5))
    return values.astype(jnp.bfloat16)


def draw_cross_q(key, part):
    key = jax.random.fold_in(key, 14)
    values = normal_part(key, (D, D), D ** (-0.5))
    return values.astype(jnp.bfloat16)


def draw_cross_kv(key, part):
    key = jax.random.fold_in(key, 15)
    values = normal_part(key, (D, 2, D), D ** (-0.5))
    return values.astype(jnp.bfloat16)


def block_scale(key, extent, split, least, high):
    def one(dim, shards_of):
        steps = jax.random.uniform(jax.random.fold_in(jax.random.fold_in(key, 6), dim), (shards_of,), jnp.float32, least / len(split), high / len(split))
        return jnp.repeat(jnp.exp(steps), extent[dim] // shards_of).reshape((-1,) + (1,) * (len(extent) - dim - 1))

    loudness = one(*split[0])
    for cut in split[1:]:
        loudness = loudness * one(*cut)
    return loudness


def noise(key, extent, spread, bound, pieces=(), held_as=jnp.bfloat16):
    drawn = jax.random.normal(key, extent, jnp.float32) * spread
    if len(pieces) > 0:
        drawn = block_scale(key, extent, pieces, -0.22, 0.18) * drawn
    return jnp.clip(drawn, min=-bound, max=bound).astype(held_as)


def setup_inputs(seed: int = 0) -> dict:
    key_list = jax.random.split(jax.random.key(seed), 15)
    tokens = draw_tokens(jax.random.fold_in(key_list[14], 71), 0)
    memory = draw_memory(jax.random.fold_in(key_list[14], 71), 0)
    self_qkv = draw_self_qkv(jax.random.fold_in(key_list[14], 71), 0)
    self_out = noise(key_list[3], (D, D), (max(D // 256, 1)) ** -0.5, 3.0, ((0, 8),))
    cross_q = draw_cross_q(jax.random.fold_in(key_list[14], 71), 0)
    cross_kv = draw_cross_kv(jax.random.fold_in(key_list[14], 71), 0)
    cross_out = noise(key_list[6], (D, D), (max(D // 1024, 1)) ** -0.5, 6.0, ((0, 8),))
    hidden_weight = noise(key_list[7], (D, FF), D ** -0.5, 0.1875, ((1, 8),))
    hidden_bias = noise(key_list[8], (FF,), 0.5, 3.0, ((0, 8),))
    output_weight = noise(key_list[9], (FF, D), (max(FF // 64, 1)) ** -0.5, 0.75, ((0, 8),))
    output_bias = noise(key_list[10], (D,), 1.0, 5.0, (), jnp.float32)
    norm_gain = jnp.clip(1.0 + 0.15 * jax.random.normal(key_list[11], (3, D), jnp.float32), 0.25, 1.75)
    norm_shift = noise(key_list[12], (3, D), 0.5, 3.0, (), jnp.float32)
    grad_output = noise(key_list[13], (TOKENS, D), 1.0, 6.0, ((0, 32),))
    return dict(tokens=tokens, memory=memory, self_qkv=self_qkv, self_out=self_out, cross_q=cross_q, cross_kv=cross_kv, cross_out=cross_out, hidden_weight=hidden_weight, hidden_bias=hidden_bias, output_weight=output_weight, output_bias=output_bias, norm_gain=norm_gain, norm_shift=norm_shift, grad_output=grad_output)


residual_alpha = 300.0 ** 0.25
norm_eps = 1e-05
masked_score = -1e+30
highest = lax.Precision.HIGHEST

@jax.custom_vjp
def low(v):
    return lax.optimization_barrier(v.astype(jnp.bfloat16)).astype(jnp.float32)

@jax.custom_vjp
def low_back(v):
    return v

def low_keep(v):
    return (low(v), None)

def low_pass(kept, grad):
    return (grad,)

def back_keep(v):
    return (v, None)

def back_low(kept, grad):
    return (low(grad),)
low.defvjp(low_keep, low_pass)
low_back.defvjp(back_keep, back_low)

def both_ways(values):
    return low(low_back(values))

def normalize(rows_in, gain_row, shift_row):
    row_mean = lax.optimization_barrier(jnp.mean(rows_in, axis=-1, keepdims=True))
    centered = rows_in - row_mean
    variance = lax.optimization_barrier(jnp.mean(centered * centered, axis=-1, keepdims=True))
    return centered * lax.rsqrt(variance + norm_eps) * gain_row + shift_row

def split_heads(tensor_in, which):
    picked = tensor_in[:, :, which]
    return picked.reshape(picked.shape[0], picked.shape[1], H, DH)

def attend(queries, keys_in, values_in, causal):
    batch_seqs, length = (queries.shape[0], queries.shape[1])
    block_rows = min(512, length)
    block_count = length // block_rows
    width_keys = keys_in.shape[1]
    blocked = queries.reshape(batch_seqs, block_count, block_rows, H, DH).transpose(1, 0, 2, 3, 4)
    offsets = jnp.arange(block_count, dtype=jnp.int32) * block_rows

    def one_block(inputs):
        query_block, offset = inputs
        scores = low_back(jnp.einsum('bqhd,bkhd->bhqk', query_block, keys_in, precision=highest) * DH ** (-0.5))
        if causal:
            row_pos = offset + jnp.arange(block_rows, dtype=jnp.int32)[:, None]
            col_pos = jnp.arange(width_keys, dtype=jnp.int32)[None, :]
            scores = jnp.where(col_pos <= row_pos, scores, masked_score)
        row_top = lax.optimization_barrier(jnp.max(scores, axis=-1, keepdims=True))
        exp_scores = jnp.exp(scores - row_top)
        probs_low = low(exp_scores / lax.optimization_barrier(jnp.sum(exp_scores, axis=-1, keepdims=True)))
        return jnp.einsum('bhqk,bkhd->bqhd', probs_low, values_in, precision=highest)
    result = lax.map(jax.checkpoint(one_block), (blocked, offsets))
    return result.transpose(1, 0, 2, 3, 4).reshape(batch_seqs, length, H * DH)

def project(values, weight):
    return jnp.einsum('bnd,de->bne', values, weight, precision=highest)

def layer(params, seq_tokens, seq_memory):
    self_qkv, self_out, cross_q, cross_kv, cross_out, hidden_weight, hidden_bias, output_weight, output_bias, norm_gain, norm_shift = params
    batch_seqs = seq_tokens.shape[0]
    mixed = project(seq_tokens, self_qkv.reshape(D, 3 * D))
    mixed = both_ways(mixed.reshape(batch_seqs, LEN, 3, D))
    self_heads = both_ways(attend(split_heads(mixed, 0), split_heads(mixed, 1), split_heads(mixed, 2), True))
    branch_one = low_back(project(self_heads, self_out))
    normed_one = normalize(residual_alpha * seq_tokens + branch_one, norm_gain[0], norm_shift[0])
    normed_one_low = low(normed_one)
    cross_queries = both_ways(project(normed_one_low, cross_q))
    cross_queries = cross_queries.reshape(batch_seqs, -1, H, DH)
    memory_mixed = project(seq_memory, cross_kv.reshape(D, 2 * D))
    memory_mixed = both_ways(memory_mixed.reshape(batch_seqs, MEM, 2, D))
    cross_heads = both_ways(attend(cross_queries, split_heads(memory_mixed, 0), split_heads(memory_mixed, 1), False))
    branch_two = low_back(project(cross_heads, cross_out))
    normed_two = normalize(residual_alpha * normed_one + branch_two, norm_gain[1], norm_shift[1])
    normed_two_low = low(normed_two)
    hidden_pre = low_back(project(normed_two_low, hidden_weight) + hidden_bias)
    activated = low(jax.nn.gelu(hidden_pre, approximate=True))
    branch_three = low_back(project(activated, output_weight))
    return normalize(residual_alpha * normed_two + branch_three + output_bias, norm_gain[2], norm_shift[2])

def reference(tokens, memory, self_qkv, self_out, cross_q, cross_kv, cross_out, hidden_weight, hidden_bias, output_weight, output_bias, norm_gain, norm_shift, grad_output):
    per_step = math.gcd(NSEQ, max(1, 4096 // LEN))
    step_count = NSEQ // per_step
    params = tuple((argument.astype(jnp.float32) for argument in (self_qkv, self_out, cross_q, cross_kv, cross_out, hidden_weight, hidden_bias, output_weight, output_bias, norm_gain, norm_shift)))
    seq_tokens = tokens.astype(jnp.float32).reshape(step_count, per_step, LEN, D)
    seq_memory = memory.astype(jnp.float32).reshape(step_count, per_step, MEM, D)
    seq_grads = grad_output.astype(jnp.float32).reshape(step_count, per_step, LEN, D)

    def one_step(totals, inputs):
        tokens_now, memory_now, grads_now = inputs
        outputs_now, pull_back = jax.vjp(layer, params, tokens_now, memory_now)
        param_grads, token_grads, memory_grads = pull_back(grads_now)
        totals = jax.tree.map(lambda first_tree, second_tree: first_tree + second_tree, totals, param_grads)
        return (totals, (outputs_now, token_grads, memory_grads))
    zero_grads = jax.tree.map(jnp.zeros_like, params)
    totals, (outputs_all, token_grads, memory_grads) = lax.scan(one_step, zero_grads, (seq_tokens, seq_memory, seq_grads))
    return (outputs_all.reshape(TOKENS, D).astype(jnp.bfloat16), token_grads.reshape(TOKENS, D), memory_grads.reshape(MTOKENS, D), totals[0], totals[1], totals[2], totals[3], totals[4], totals[5], totals[6], totals[7], totals[8], totals[9], totals[10])
```

```python
import functools
import math

import jax
import jax.numpy as jnp
from jax import lax
from jax.experimental import pallas as pl
from jax.experimental.pallas import tpu as pltpu
from jax.sharding import PartitionSpec as P

MESH = pl.DeviceIdType.MESH
DH = 64
LANES = 128
LEN = 1024

residual_alpha = 300.0**0.25
norm_eps = 1e-05

def greet(peers):
    barrier = pltpu.get_barrier_semaphore()
    for p in peers:
        pl.semaphore_signal(barrier, inc=1, device_id={"tensor": p}, device_id_type=MESH)
    pl.semaphore_wait(barrier, len(peers))

def to_heads_kernel(count, tsize, pairs, block, *refs):
    ins, outs = refs[:count], refs[count:2*count]
    send_sem, recv_sem = refs[2*count:]
    me = lax.axis_index("tensor")
    blocks = ins[0].shape[0] // block
    per_seq = LEN // block
    wide = ins[0].shape[1] // LANES
    seqs = tsize * blocks // per_seq
    greet([lax.rem(me + i, tsize) for i in range(1, tsize)])
    def unit(a, u):
        j, p = u // wide, u % wide
        g = me * blocks + j
        q = (g // per_seq) * wide + p
        dst, slot, k = q // pairs, q % pairs, g % per_seq
        src = ins[a].at[pl.ds(pl.multiple_of(j * block, block), block), pl.ds(pl.multiple_of(p * LANES, LANES), LANES)]
        to = outs[a].at[slot, pl.ds(pl.multiple_of(k * block, block), block), :]
        return dst, src, to, send_sem.at[a, u], recv_sem.at[a, slot * per_seq + k]
    for a in range(count):
        def start(u, _):
            dst, src, to, ss, rs = unit(a, u)
            @pl.when(dst == me)
            def _():
                pltpu.make_async_copy(src, to, rs).start()
            @pl.when(dst != me)
            def _():
                pltpu.make_async_remote_copy(src, to, ss, rs, device_id={"tensor": dst}, device_id_type=MESH).start()
            return 0
        lax.fori_loop(0, blocks * wide, start, 0)
    for a in range(count):
        def done(u, _):
            dst, src, to, ss, rs = unit(a, u)
            @pl.when(dst != me)
            def _():
                pltpu.make_async_remote_copy(src, to, ss, rs, device_id={"tensor": dst}, device_id_type=MESH).wait_send()
            return 0
        lax.fori_loop(0, blocks * wide, done, 0)
        def got(r, _):
            slot, k = r // per_seq, r % per_seq
            @pl.when(me * pairs + slot < seqs * wide)
            def _():
                to = outs[a].at[slot, pl.ds(pl.multiple_of(k * block, block), block), :]
                pltpu.make_async_copy(to, to, recv_sem.at[a, r]).wait()
            return 0
        lax.fori_loop(0, pairs * per_seq, got, 0)

def to_heads(arrays, tsize, cid):
    n, d = arrays[0].shape
    block = math.gcd(n, LEN)
    wide = d // LANES
    seqs = n * tsize // LEN
    pairs = -(-seqs * wide // tsize)
    count = len(arrays)
    return pl.pallas_call(
        functools.partial(to_heads_kernel, count, tsize, pairs, block),
        out_shape=[jax.ShapeDtypeStruct((pairs, LEN, LANES), jnp.bfloat16)] * count,
        in_specs=[pl.BlockSpec(memory_space=pl.ANY)] * count,
        out_specs=[pl.BlockSpec(memory_space=pl.ANY)] * count,
        scratch_shapes=[pltpu.SemaphoreType.DMA((count, n // block * wide)), pltpu.SemaphoreType.DMA((count, pairs * LEN // block))],
        compiler_params=pltpu.CompilerParams(collective_id=cid, has_side_effects=True),
    )(*arrays)

def to_tokens_kernel(count, tsize, pairs, block, *refs):
    ins, outs = refs[:count], refs[count:2*count]
    send_sem, recv_sem = refs[2*count:]
    me = lax.axis_index("tensor")
    blocks = outs[0].shape[0] // block
    per_seq = LEN // block
    wide = outs[0].shape[1] // LANES
    seqs = tsize * blocks // per_seq
    greet([lax.rem(me + i, tsize) for i in range(1, tsize)])
    def unit(a, u):
        slot, k = u // per_seq, u % per_seq
        q = me * pairs + slot
        g = (q // wide) * per_seq + k
        dst, j, p = g // blocks, g % blocks, q % wide
        src = ins[a].at[slot, pl.ds(pl.multiple_of(k * block, block), block), :]
        to = outs[a].at[pl.ds(pl.multiple_of(j * block, block), block), pl.ds(pl.multiple_of(p * LANES, LANES), LANES)]
        return q < seqs * wide, dst, src, to, send_sem.at[a, u], recv_sem.at[a, j * wide + p]
    for a in range(count):
        def start(u, _):
            real, dst, src, to, ss, rs = unit(a, u)
            @pl.when(real & (dst == me))
            def _():
                pltpu.make_async_copy(src, to, rs).start()
            @pl.when(real & (dst != me))
            def _():
                pltpu.make_async_remote_copy(src, to, ss, rs, device_id={"tensor": dst}, device_id_type=MESH).start()
            return 0
        lax.fori_loop(0, pairs * per_seq, start, 0)
    for a in range(count):
        def done(u, _):
            real, dst, src, to, ss, rs = unit(a, u)
            @pl.when(real & (dst != me))
            def _():
                pltpu.make_async_remote_copy(src, to, ss, rs, device_id={"tensor": dst}, device_id_type=MESH).wait_send()
            return 0
        lax.fori_loop(0, pairs * per_seq, done, 0)
        def got(r, _):
            j, p = r // wide, r % wide
            to = outs[a].at[pl.ds(pl.multiple_of(j * block, block), block), pl.ds(pl.multiple_of(p * LANES, LANES), LANES)]
            pltpu.make_async_copy(to, to, recv_sem.at[a, r]).wait()
            return 0
        lax.fori_loop(0, blocks * wide, got, 0)

def to_tokens(arrays, n, d, tsize, cid):
    pairs = arrays[0].shape[0]
    block = math.gcd(n, LEN)
    wide = d // LANES
    count = len(arrays)
    return pl.pallas_call(
        functools.partial(to_tokens_kernel, count, tsize, pairs, block),
        out_shape=[jax.ShapeDtypeStruct((n, d), jnp.bfloat16)] * count,
        in_specs=[pl.BlockSpec(memory_space=pl.ANY)] * count,
        out_specs=[pl.BlockSpec(memory_space=pl.ANY)] * count,
        scratch_shapes=[pltpu.SemaphoreType.DMA((count, pairs * LEN // block)), pltpu.SemaphoreType.DMA((count, n // block * wide))],
        compiler_params=pltpu.CompilerParams(collective_id=cid, has_side_effects=True),
    )(*arrays)

def lane_half(shape, h):
    return (lax.broadcasted_iota(jnp.int32, shape, len(shape)-1) // 64) == h

NT = (((1,), (1,)), ((), ()))
NN = (((1,), (0,)), ((), ()))
LOG2E = math.log2(math.e)
def dot(a, b, dims):
    return lax.dot_general(a, b, dims, preferred_element_type=jnp.float32)

def fwd_kernel(causal, bq, q_ref, k_ref, v_ref, o_ref, lse_ref):
    def block(i):
        keys = bq * (i + 1) if causal else LEN
        rows = pl.ds(i * bq, bq)
        q = q_ref[0, rows, :] * jnp.bfloat16(0.125)
        k = k_ref[0, :keys, :]
        total = None
        for h in (0, 1):
            qh = jnp.where(lane_half(q.shape, h), q, jnp.bfloat16(0))
            s = dot(qh, k, NT)
            if causal:
                tail = s[:, keys - bq:]
                r = lax.broadcasted_iota(jnp.int32, tail.shape, 0)
                c = lax.broadcasted_iota(jnp.int32, tail.shape, 1)
                tail = jnp.where(c <= r, tail, -1e30)
                s = tail if keys == bq else jnp.concatenate([s[:, :keys - bq], tail], 1)
            m = jnp.max(s, axis=-1, keepdims=True)
            e = jnp.exp2((s - m) * LOG2E)
            l = jnp.sum(e, axis=-1, keepdims=True)
            v = v_ref[0, :keys, :]
            o = dot(e.astype(jnp.bfloat16), v, NN) / l
            total = o if h == 0 else jnp.where(lane_half(o.shape, 0), total, o)
            lse = m * LOG2E + jnp.log2(l)
            lse_ref[0, h:h+1, rows] = jnp.transpose(jnp.broadcast_to(lse, (bq, 128)))[0:1]
        o_ref[0, rows, :] = total.astype(jnp.bfloat16)
    for i in range(LEN // bq):
        block(i)

def attend_fwd(q, k, v, causal, bq=256):
    pairs = q.shape[0]
    spec = pl.BlockSpec((1, LEN, LANES), lambda i: (i, 0, 0))
    return pl.pallas_call(
        functools.partial(fwd_kernel, causal, bq),
        grid=(pairs,),
        out_shape=[jax.ShapeDtypeStruct(q.shape, jnp.bfloat16), jax.ShapeDtypeStruct((pairs, 8, LEN), jnp.float32)],
        in_specs=[spec] * 3,
        out_specs=[spec, pl.BlockSpec((1, 8, LEN), lambda i: (i, 0, 0))],
        compiler_params=pltpu.CompilerParams(vmem_limit_bytes=48 << 20),
        cost_estimate=pl.CostEstimate(flops=pairs * 2 * 2 * 2 * LEN * LEN * 64, bytes_accessed=pairs * LEN * LANES * 8, transcendentals=pairs * 2 * LEN * LEN),
    )(q, k, v)

def bwd_kernel(causal, bq, q_ref, k_ref, v_ref, o_ref, lse_ref, do_ref, dq_ref, dk_ref, dv_ref, dk_acc, dv_acc):
    dk_acc[...] = jnp.zeros_like(dk_acc)
    dv_acc[...] = jnp.zeros_like(dv_acc)
    kt = jnp.transpose(k_ref[0])
    for i in range(LEN // bq):
        keys = bq * (i + 1) if causal else LEN
        rows = pl.ds(i * bq, bq)
        q = q_ref[0, rows, :] * jnp.bfloat16(0.125)
        do = do_ref[0, rows, :]
        prod = jnp.transpose(do.astype(jnp.float32) * o_ref[0, rows, :].astype(jnp.float32))
        k = k_ref[0, :keys, :]
        v = v_ref[0, :keys, :]
        dqt = None
        for h in (0, 1):
            mask = lane_half(q.shape, h)
            qh = jnp.where(mask, q, jnp.bfloat16(0))
            doh = jnp.where(mask, do, jnp.bfloat16(0))
            delta = jnp.sum(prod[64 * h:64 * h + 64], axis=0, keepdims=True)
            s = dot(k, qh, NT)
            p = jnp.exp2(s * LOG2E - lse_ref[0, h:h+1, rows])
            if causal:
                tail = p[keys - bq:, :]
                r = lax.broadcasted_iota(jnp.int32, tail.shape, 1)
                c = lax.broadcasted_iota(jnp.int32, tail.shape, 0)
                tail = jnp.where(c <= r, tail, 0.0)
                p = tail if keys == bq else jnp.concatenate([p[:keys - bq], tail], 0)
            dp = dot(v, doh, NT)
            ds = (p * (dp - delta)).astype(jnp.bfloat16)
            dv_acc[:keys, :] += dot(p.astype(jnp.bfloat16), doh, NN)
            dk_acc[:keys, :] += dot(ds, qh, NN)
            part = dot(kt[64 * h:64 * h + 64, :keys], ds, NN)
            dqt = part if h == 0 else jnp.concatenate([dqt, part], 0)
        dq_ref[0, rows, :] = (jnp.transpose(dqt) * 0.125).astype(jnp.bfloat16)
    dk_ref[0] = dk_acc[...].astype(jnp.bfloat16)
    dv_ref[0] = dv_acc[...].astype(jnp.bfloat16)

def attend_bwd(q, k, v, o, lse, do, causal, bq=256):
    pairs = q.shape[0]
    spec = pl.BlockSpec((1, LEN, LANES), lambda i: (i, 0, 0))
    return pl.pallas_call(
        functools.partial(bwd_kernel, causal, bq),
        grid=(pairs,),
        out_shape=[jax.ShapeDtypeStruct(q.shape, jnp.bfloat16)] * 3,
        in_specs=[spec] * 4 + [pl.BlockSpec((1, 8, LEN), lambda i: (i, 0, 0)), spec],
        out_specs=[spec] * 3,
        scratch_shapes=[pltpu.VMEM((LEN, LANES), jnp.float32)] * 2,
        compiler_params=pltpu.CompilerParams(vmem_limit_bytes=48 << 20),
        cost_estimate=pl.CostEstimate(flops=pairs * 5 * 2 * 2 * LEN * LEN * 64, bytes_accessed=pairs * LEN * LANES * 16, transcendentals=pairs * 2 * LEN * LEN),
    )(q, k, v, o, lse, do)


def cols_kernel(count, x_ref, w_ref, *outs):
    out = dot(x_ref[...], w_ref[0], NN)
    width = out.shape[1] // count
    for i, o_ref in enumerate(outs):
        o_ref[...] = out[:, i * width : (i + 1) * width].astype(o_ref.dtype)


def cols_product(x, weight, count, dtype=jnp.bfloat16):
    n, d = x.shape
    t, _, c = weight.shape
    width = c // count
    return pl.pallas_call(
        functools.partial(cols_kernel, count),
        grid=(t,),
        out_shape=[jax.ShapeDtypeStruct((n, t * width), dtype)] * count,
        in_specs=[
            pl.BlockSpec((n, d), lambda i: (0, 0)),
            pl.BlockSpec((1, d, c), lambda i: (i, 0, 0)),
        ],
        out_specs=[pl.BlockSpec((n, width), lambda i: (0, i))] * count,
        compiler_params=pltpu.CompilerParams(vmem_limit_bytes=48 << 20),
        cost_estimate=pl.CostEstimate(
            flops=2 * n * d * t * c, bytes_accessed=2 * (t * d * c + n * d + n * t * c), transcendentals=0
        ),
    )(x, weight)


def back_kernel(count, *refs):
    ys, w_ref, o_ref = refs[:count], refs[count], refs[count + 1]
    y = jnp.concatenate([y_ref[...] for y_ref in ys], 1) if count > 1 else ys[0][...]
    term = dot(y, w_ref[0], NT)

    @pl.when(pl.program_id(0) == 0)
    def _():
        o_ref[...] = term

    @pl.when(pl.program_id(0) != 0)
    def _():
        o_ref[...] += term


def back_product(ys, weight):
    count = len(ys)
    n = ys[0].shape[0]
    t, d, c = weight.shape
    width = c // count
    return pl.pallas_call(
        functools.partial(back_kernel, count),
        grid=(t,),
        out_shape=jax.ShapeDtypeStruct((n, d), jnp.float32),
        in_specs=[pl.BlockSpec((n, width), lambda i: (0, i))] * count
        + [pl.BlockSpec((1, d, c), lambda i: (i, 0, 0))],
        out_specs=pl.BlockSpec((n, d), lambda i: (0, 0)),
        compiler_params=pltpu.CompilerParams(vmem_limit_bytes=48 << 20),
        cost_estimate=pl.CostEstimate(
            flops=2 * n * d * t * c, bytes_accessed=2 * (t * d * c + 2 * n * d + n * t * c), transcendentals=0
        ),
    )(*ys, weight)


def grad_kernel(count, x_ref, *refs):
    ys, o_ref, xt_ref = refs[:count], refs[count], refs[count + 1]

    @pl.when(pl.program_id(0) == 0)
    def _():
        xt_ref[...] = jnp.transpose(x_ref[...])

    y = jnp.concatenate([y_ref[...] for y_ref in ys], 1) if count > 1 else ys[0][...]
    o_ref[0] = dot(xt_ref[...], y, NN).astype(o_ref.dtype)


def cols_grad(x, ys, t):
    count = len(ys)
    n, d = x.shape
    width = max(ys[0].shape[1] // t, LANES)
    blocks = ys[0].shape[1] // width
    c = width * count
    out = pl.pallas_call(
        functools.partial(grad_kernel, count),
        grid=(blocks,),
        out_shape=jax.ShapeDtypeStruct((blocks, d, c), jnp.bfloat16),
        in_specs=[pl.BlockSpec((n, d), lambda i: (0, 0))]
        + [pl.BlockSpec((n, width), lambda i: (0, i))] * count,
        out_specs=pl.BlockSpec((1, d, c), lambda i: (i, 0, 0)),
        scratch_shapes=[pltpu.VMEM((d, n), jnp.bfloat16)],
        compiler_params=pltpu.CompilerParams(vmem_limit_bytes=48 << 20),
        cost_estimate=pl.CostEstimate(
            flops=2 * n * d * t * c, bytes_accessed=2 * (t * d * c + n * d + n * t * c), transcendentals=0
        ),
    )(x, *ys)
    return narrow(out, count, t)


def gather_weight(weight):
    dp, t = lax.axis_size("dp"), lax.axis_size("tensor")
    rows = weight.shape[0] // dp
    share = lax.dynamic_slice_in_dim(weight, lax.axis_index("dp") * rows, rows, 0)
    whole = lax.all_gather(share, ("tensor", "dp"), axis=0, tiled=True)
    return whole.reshape(t, weight.shape[0], weight.shape[1])


def widen(weight, count):
    t, r, c = weight.shape
    width = c // count
    if width % LANES == 0:
        return weight
    m = LANES // width
    parts = weight.reshape(t // m, m, r, count, width).transpose(0, 2, 3, 1, 4)
    return parts.reshape(t // m, r, count * LANES)


def narrow(grad, count, t):
    blocks, r, c = grad.shape
    if blocks == t:
        return grad
    m = t // blocks
    parts = grad.reshape(blocks, r, count, m, c // count // m).transpose(0, 3, 1, 2, 4)
    return parts.reshape(t, r, c // m)


def swap(value, axis, bit):
    size = lax.axis_size(axis)
    return lax.ppermute(value, axis, [(i, i ^ bit) for i in range(size)])


def pick(value, index, axis):
    return lax.dynamic_index_in_dim(value, index, axis, keepdims=False)


def reduce_grad(grad):
    dp, t = lax.axis_size("dp"), lax.axis_size("tensor")
    own_dp, own_t = lax.axis_index("dp"), lax.axis_index("tensor")
    _, r, c = grad.shape
    core, side, line, depth = own_dp % 2, own_t % 2, own_t // 2, t // 2
    halves = grad.reshape(t, 2, r // 2, c)
    total = pick(halves, core, 1) + swap(pick(halves, 1 - core, 1), "dp", 1)
    pairs = total.reshape(depth, 2, r // 2, c)
    total = pick(pairs, side, 1) + swap(pick(pairs, 1 - side, 1), "tensor", 1)
    result = pick(total, line, 0)
    for sign in (1, -1):
        passed = None
        for step in range(depth - 1):
            far = line + sign * (depth - 1 - step)
            part = pick(total, jnp.clip(far, 0, depth - 1), 0)
            passed = part if passed is None else part + passed
            lines = range(step + 1) if sign == 1 else range(depth - 1 - step, depth)
            passed = lax.ppermute(
                passed, "tensor", [(2 * i + j, 2 * (i + sign) + j) for i in lines for j in range(2)]
            )
        result = result + passed
    bit = 2
    while bit < dp:
        result = result + swap(result, "dp", bit)
        bit *= 2
    other = swap(result, "dp", 1)
    first = jnp.where(core == 0, result, other)
    second = jnp.where(core == 0, other, result)
    return jnp.concatenate([first, second], 0).astype(jnp.float32)


def normalize(rows_in, gain_row, shift_row):
    row_mean = jnp.mean(rows_in, axis=-1, keepdims=True)
    centered = rows_in - row_mean
    variance = jnp.mean(centered * centered, axis=-1, keepdims=True)
    return centered * lax.rsqrt(variance + norm_eps) * gain_row + shift_row


def gelu_tanh(values):
    return jax.nn.gelu(values, approximate=True)


def product(values, weight):
    return jnp.dot(values, weight, preferred_element_type=jnp.float32)


def rows_grad(left, right, t):
    out = lax.dot_general(left, right, (((0,), (0,)), ((), ())), preferred_element_type=jnp.float32)
    return out.astype(jnp.bfloat16).reshape(t, -1, right.shape[1])


def per_device(
    tokens,
    memory,
    self_qkv,
    self_out,
    cross_q,
    cross_kv,
    cross_out,
    hidden_weight,
    hidden_bias,
    output_weight,
    output_bias,
    norm_gain,
    norm_shift,
    grad_output,
):
    low = jnp.bfloat16
    t = lax.axis_size("tensor")
    n, d = tokens.shape
    w_qkv = widen(gather_weight(self_qkv.reshape(d, -1)), 3)
    w_kv = widen(gather_weight(cross_kv.reshape(d, -1)), 2)
    w_so = gather_weight(self_out).reshape(d, d)
    w_cq = widen(gather_weight(cross_q), 1)
    w_co = gather_weight(cross_out).reshape(d, d)
    w_hid = gather_weight(hidden_weight)
    w_out = gather_weight(output_weight).reshape(-1, d)
    bias_all = lax.all_gather(hidden_bias, "tensor", axis=0, tiled=True)

    qkv = cols_product(tokens, w_qkv, 3)
    sq, sk, sv = to_heads(qkv, t, 0)
    so, s_lse = attend_fwd(sq, sk, sv, True, 512)
    (self_heads,) = to_tokens([so], n, d, t, 1)
    branch_one = product(self_heads, w_so)
    normed_one, pull_one = jax.vjp(
        normalize, residual_alpha * tokens.astype(jnp.float32) + branch_one, norm_gain[0], norm_shift[0]
    )
    normed_one_low = normed_one.astype(low)
    kv = cols_product(memory, w_kv, 2)
    cq = cols_product(normed_one_low, w_cq, 1)
    cq, ck, cv = to_heads([*cq, *kv], t, 2)
    co, c_lse = attend_fwd(cq, ck, cv, False, 512)
    (cross_heads,) = to_tokens([co], n, d, t, 3)
    branch_two = product(cross_heads, w_co)
    normed_two, pull_two = jax.vjp(
        normalize, residual_alpha * normed_one + branch_two, norm_gain[1], norm_shift[1]
    )
    normed_two_low = normed_two.astype(low)
    (hidden_low,) = cols_product(normed_two_low, w_hid, 1, jnp.float32)
    hidden_pre = hidden_low + bias_all
    activated, gelu_pull = jax.vjp(gelu_tanh, hidden_pre)
    activated_low = activated.astype(low)
    branch_three = product(activated_low, w_out)
    layer_out, pull_three = jax.vjp(
        normalize, residual_alpha * normed_two + branch_three + output_bias, norm_gain[2], norm_shift[2]
    )
    grad_three, gain_three, shift_three = pull_three(grad_output.astype(jnp.float32))
    bias_out_grad = jnp.sum(grad_three, axis=0)
    grad_three_low = grad_three.astype(low)
    out_weight_grad = reduce_grad(rows_grad(activated_low, grad_three_low, t))
    grad_act = lax.dot_general(grad_three_low, w_out, NT, preferred_element_type=jnp.float32)
    grad_hidden = gelu_pull(grad_act)[0].astype(low)
    hidden_bias_grad = jnp.sum(grad_hidden, axis=0, dtype=jnp.float32)
    hidden_weight_grad = reduce_grad(cols_grad(normed_two_low, [grad_hidden], t))
    grad_two, gain_two, shift_two = pull_two(
        residual_alpha * grad_three + back_product([grad_hidden], w_hid)
    )
    grad_two_low = grad_two.astype(low)
    cross_out_grad = reduce_grad(rows_grad(cross_heads, grad_two_low, t))
    grad_co = lax.dot_general(grad_two_low, w_co, NT, preferred_element_type=jnp.float32).astype(low)
    (grad_co,) = to_heads([grad_co], t, 4)
    cross_grads = attend_bwd(cq, ck, cv, co, c_lse, grad_co, False, 256)
    g_cq, g_ck, g_cv = to_tokens(cross_grads, n, d, t, 5)
    cross_q_grad = reduce_grad(cols_grad(normed_one_low, [g_cq], t))
    cross_kv_grad = reduce_grad(cols_grad(memory, [g_ck, g_cv], t)).reshape(cross_kv.shape)
    grad_memory = back_product([g_ck, g_cv], w_kv)
    grad_one, gain_one, shift_one = pull_one(residual_alpha * grad_two + back_product([g_cq], w_cq))
    grad_one_low = grad_one.astype(low)
    self_out_grad = reduce_grad(rows_grad(self_heads, grad_one_low, t))
    grad_so = lax.dot_general(grad_one_low, w_so, NT, preferred_element_type=jnp.float32).astype(low)
    (grad_so,) = to_heads([grad_so], t, 6)
    self_grads = attend_bwd(sq, sk, sv, so, s_lse, grad_so, True, 256)
    g_qkv = to_tokens(self_grads, n, d, t, 7)
    self_qkv_grad = reduce_grad(cols_grad(tokens, g_qkv, t)).reshape(self_qkv.shape)
    grad_tokens = residual_alpha * grad_one + back_product(g_qkv, w_qkv)
    gain_total, shift_total, bias_total, hidden_bias_total = lax.psum(
        (
            jnp.stack([gain_one, gain_two, gain_three]),
            jnp.stack([shift_one, shift_two, shift_three]),
            bias_out_grad,
            hidden_bias_grad,
        ),
        ("dp", "tensor"),
    )
    units = hidden_bias.shape[0]
    hidden_bias_total = lax.dynamic_slice_in_dim(hidden_bias_total, lax.axis_index("tensor") * units, units, 0)
    return (
        layer_out.astype(low),
        grad_tokens,
        grad_memory,
        self_qkv_grad,
        self_out_grad,
        cross_q_grad,
        cross_kv_grad,
        cross_out_grad,
        hidden_weight_grad,
        hidden_bias_total,
        out_weight_grad,
        bias_total,
        gain_total,
        shift_total,
    )


def solution(mesh):
    return jax.shard_map(
        per_device,
        mesh=mesh,
        in_specs=(
            P(("dp", "tensor"), None),
            P(("dp", "tensor"), None),
            P(None, None, "tensor"),
            P("tensor", None),
            P(None, "tensor"),
            P(None, None, "tensor"),
            P("tensor", None),
            P(None, "tensor"),
            P("tensor"),
            P("tensor", None),
            P(),
            P(),
            P(),
            P(("dp", "tensor"), None),
        ),
        out_specs=(
            P(("dp", "tensor"), None),
            P(("dp", "tensor"), None),
            P(("dp", "tensor"), None),
            P(None, None, "tensor"),
            P("tensor", None),
            P(None, "tensor"),
            P(None, None, "tensor"),
            P("tensor", None),
            P(None, "tensor"),
            P("tensor"),
            P("tensor", None),
            P(),
            P(),
            P(),
        ),
        check_vma=False,
    )
```

```python
import functools
import math

import jax
import jax.numpy as jnp
from jax import lax
from jax.experimental import pallas as pl
from jax.experimental.pallas import tpu as pltpu
from jax.sharding import PartitionSpec as P

MESH = pl.DeviceIdType.MESH
DH = 64
LANES = 128
LEN = 1024

residual_alpha = 300.0**0.25
norm_eps = 1e-05

def greet(peers):
    barrier = pltpu.get_barrier_semaphore()
    for p in peers:
        pl.semaphore_signal(barrier, inc=1, device_id={"tensor": p}, device_id_type=MESH)
    pl.semaphore_wait(barrier, len(peers))

def to_heads_kernel(count, tsize, pairs, block, *refs):
    ins, outs = refs[:count], refs[count:2*count]
    send_sem, recv_sem = refs[2*count:]
    me = lax.axis_index("tensor")
    blocks = ins[0].shape[0] // block
    per_seq = LEN // block
    wide = ins[0].shape[1] // LANES
    seqs = tsize * blocks // per_seq
    greet([lax.rem(me + i, tsize) for i in range(1, tsize)])
    def unit(a, u):
        j, p = u // wide, u % wide
        g = me * blocks + j
        q = (g // per_seq) * wide + p
        dst, slot, k = q // pairs, q % pairs, g % per_seq
        src = ins[a].at[pl.ds(pl.multiple_of(j * block, block), block), pl.ds(pl.multiple_of(p * LANES, LANES), LANES)]
        to = outs[a].at[slot, pl.ds(pl.multiple_of(k * block, block), block), :]
        return dst, src, to, send_sem.at[a, u], recv_sem.at[a, slot * per_seq + k]
    for a in range(count):
        def start(u, _):
            dst, src, to, ss, rs = unit(a, u)
            @pl.when(dst == me)
            def _():
                pltpu.make_async_copy(src, to, rs).start()
            @pl.when(dst != me)
            def _():
                pltpu.make_async_remote_copy(src, to, ss, rs, device_id={"tensor": dst}, device_id_type=MESH).start()
            return 0
        lax.fori_loop(0, blocks * wide, start, 0)
    for a in range(count):
        def done(u, _):
            dst, src, to, ss, rs = unit(a, u)
            @pl.when(dst != me)
            def _():
                pltpu.make_async_remote_copy(src, to, ss, rs, device_id={"tensor": dst}, device_id_type=MESH).wait_send()
            return 0
        lax.fori_loop(0, blocks * wide, done, 0)
        def got(r, _):
            slot, k = r // per_seq, r % per_seq
            @pl.when(me * pairs + slot < seqs * wide)
            def _():
                to = outs[a].at[slot, pl.ds(pl.multiple_of(k * block, block), block), :]
                pltpu.make_async_copy(to, to, recv_sem.at[a, r]).wait()
            return 0
        lax.fori_loop(0, pairs * per_seq, got, 0)

def to_heads(arrays, tsize, cid):
    n, d = arrays[0].shape
    block = math.gcd(n, LEN)
    wide = d // LANES
    seqs = n * tsize // LEN
    pairs = -(-seqs * wide // tsize)
    count = len(arrays)
    return pl.pallas_call(
        functools.partial(to_heads_kernel, count, tsize, pairs, block),
        out_shape=[jax.ShapeDtypeStruct((pairs, LEN, LANES), jnp.bfloat16)] * count,
        in_specs=[pl.BlockSpec(memory_space=pl.ANY)] * count,
        out_specs=[pl.BlockSpec(memory_space=pl.ANY)] * count,
        scratch_shapes=[pltpu.SemaphoreType.DMA((count, n // block * wide)), pltpu.SemaphoreType.DMA((count, pairs * LEN // block))],
        compiler_params=pltpu.CompilerParams(collective_id=cid, has_side_effects=True),
    )(*arrays)

def to_tokens_kernel(count, tsize, pairs, block, *refs):
    ins, outs = refs[:count], refs[count:2*count]
    send_sem, recv_sem = refs[2*count:]
    me = lax.axis_index("tensor")
    blocks = outs[0].shape[0] // block
    per_seq = LEN // block
    wide = outs[0].shape[1] // LANES
    seqs = tsize * blocks // per_seq
    greet([lax.rem(me + i, tsize) for i in range(1, tsize)])
    def unit(a, u):
        slot, k = u // per_seq, u % per_seq
        q = me * pairs + slot
        g = (q // wide) * per_seq + k
        dst, j, p = g // blocks, g % blocks, q % wide
        src = ins[a].at[slot, pl.ds(pl.multiple_of(k * block, block), block), :]
        to = outs[a].at[pl.ds(pl.multiple_of(j * block, block), block), pl.ds(pl.multiple_of(p * LANES, LANES), LANES)]
        return q < seqs * wide, dst, src, to, send_sem.at[a, u], recv_sem.at[a, j * wide + p]
    for a in range(count):
        def start(u, _):
            real, dst, src, to, ss, rs = unit(a, u)
            @pl.when(real & (dst == me))
            def _():
                pltpu.make_async_copy(src, to, rs).start()
            @pl.when(real & (dst != me))
            def _():
                pltpu.make_async_remote_copy(src, to, ss, rs, device_id={"tensor": dst}, device_id_type=MESH).start()
            return 0
        lax.fori_loop(0, pairs * per_seq, start, 0)
    for a in range(count):
        def done(u, _):
            real, dst, src, to, ss, rs = unit(a, u)
            @pl.when(real & (dst != me))
            def _():
                pltpu.make_async_remote_copy(src, to, ss, rs, device_id={"tensor": dst}, device_id_type=MESH).wait_send()
            return 0
        lax.fori_loop(0, pairs * per_seq, done, 0)
        def got(r, _):
            j, p = r // wide, r % wide
            to = outs[a].at[pl.ds(pl.multiple_of(j * block, block), block), pl.ds(pl.multiple_of(p * LANES, LANES), LANES)]
            pltpu.make_async_copy(to, to, recv_sem.at[a, r]).wait()
            return 0
        lax.fori_loop(0, blocks * wide, got, 0)

def to_tokens(arrays, n, d, tsize, cid):
    pairs = arrays[0].shape[0]
    block = math.gcd(n, LEN)
    wide = d // LANES
    count = len(arrays)
    return pl.pallas_call(
        functools.partial(to_tokens_kernel, count, tsize, pairs, block),
        out_shape=[jax.ShapeDtypeStruct((n, d), jnp.bfloat16)] * count,
        in_specs=[pl.BlockSpec(memory_space=pl.ANY)] * count,
        out_specs=[pl.BlockSpec(memory_space=pl.ANY)] * count,
        scratch_shapes=[pltpu.SemaphoreType.DMA((count, pairs * LEN // block)), pltpu.SemaphoreType.DMA((count, n // block * wide))],
        compiler_params=pltpu.CompilerParams(collective_id=cid, has_side_effects=True),
    )(*arrays)

def lane_half(shape, h):
    return (lax.broadcasted_iota(jnp.int32, shape, len(shape)-1) // 64) == h

NT = (((1,), (1,)), ((), ()))
NN = (((1,), (0,)), ((), ()))
LOG2E = math.log2(math.e)
def dot(a, b, dims):
    return lax.dot_general(a, b, dims, preferred_element_type=jnp.float32)

def fwd_kernel(causal, bq, q_ref, k_ref, v_ref, o_ref, lse_ref):
    def block(i):
        keys = bq * (i + 1) if causal else LEN
        rows = pl.ds(i * bq, bq)
        q = q_ref[0, rows, :] * jnp.bfloat16(0.125)
        k = k_ref[0, :keys, :]
        total = None
        for h in (0, 1):
            qh = jnp.where(lane_half(q.shape, h), q, jnp.bfloat16(0))
            s = dot(qh, k, NT)
            if causal:
                tail = s[:, keys - bq:]
                r = lax.broadcasted_iota(jnp.int32, tail.shape, 0)
                c = lax.broadcasted_iota(jnp.int32, tail.shape, 1)
                tail = jnp.where(c <= r, tail, -1e30)
                s = tail if keys == bq else jnp.concatenate([s[:, :keys - bq], tail], 1)
            m = jnp.max(s, axis=-1, keepdims=True)
            e = jnp.exp2((s - m) * LOG2E)
            l = jnp.sum(e, axis=-1, keepdims=True)
            v = v_ref[0, :keys, :]
            o = dot(e.astype(jnp.bfloat16), v, NN) / l
            total = o if h == 0 else jnp.where(lane_half(o.shape, 0), total, o)
            lse = m * LOG2E + jnp.log2(l)
            lse_ref[0, h:h+1, rows] = jnp.transpose(jnp.broadcast_to(lse, (bq, 128)))[0:1]
        o_ref[0, rows, :] = total.astype(jnp.bfloat16)
    for i in range(LEN // bq):
        block(i)

def attend_fwd(q, k, v, causal, bq=256):
    pairs = q.shape[0]
    spec = pl.BlockSpec((1, LEN, LANES), lambda i: (i, 0, 0))
    return pl.pallas_call(
        functools.partial(fwd_kernel, causal, bq),
        grid=(pairs,),
        out_shape=[jax.ShapeDtypeStruct(q.shape, jnp.bfloat16), jax.ShapeDtypeStruct((pairs, 8, LEN), jnp.float32)],
        in_specs=[spec] * 3,
        out_specs=[spec, pl.BlockSpec((1, 8, LEN), lambda i: (i, 0, 0))],
        compiler_params=pltpu.CompilerParams(vmem_limit_bytes=48 << 20),
        cost_estimate=pl.CostEstimate(flops=pairs * 2 * 2 * 2 * LEN * LEN * 64, bytes_accessed=pairs * LEN * LANES * 8, transcendentals=pairs * 2 * LEN * LEN),
    )(q, k, v)

def bwd_kernel(causal, bq, q_ref, k_ref, v_ref, o_ref, lse_ref, do_ref, dq_ref, dk_ref, dv_ref, dk_acc, dv_acc):
    dk_acc[...] = jnp.zeros_like(dk_acc)
    dv_acc[...] = jnp.zeros_like(dv_acc)
    kt = jnp.transpose(k_ref[0])
    for i in range(LEN // bq):
        keys = bq * (i + 1) if causal else LEN
        rows = pl.ds(i * bq, bq)
        q = q_ref[0, rows, :] * jnp.bfloat16(0.125)
        do = do_ref[0, rows, :]
        prod = jnp.transpose(do.astype(jnp.float32) * o_ref[0, rows, :].astype(jnp.float32))
        k = k_ref[0, :keys, :]
        v = v_ref[0, :keys, :]
        dqt = None
        for h in (0, 1):
            mask = lane_half(q.shape, h)
            qh = jnp.where(mask, q, jnp.bfloat16(0))
            doh = jnp.where(mask, do, jnp.bfloat16(0))
            delta = jnp.sum(prod[64 * h:64 * h + 64], axis=0, keepdims=True)
            s = dot(k, qh, NT)
            p = jnp.exp2(s * LOG2E - lse_ref[0, h:h+1, rows])
            if causal:
                tail = p[keys - bq:, :]
                r = lax.broadcasted_iota(jnp.int32, tail.shape, 1)
                c = lax.broadcasted_iota(jnp.int32, tail.shape, 0)
                tail = jnp.where(c <= r, tail, 0.0)
                p = tail if keys == bq else jnp.concatenate([p[:keys - bq], tail], 0)
            dp = dot(v, doh, NT)
            ds = (p * (dp - delta)).astype(jnp.bfloat16)
            dv_acc[:keys, :] += dot(p.astype(jnp.bfloat16), doh, NN)
            dk_acc[:keys, :] += dot(ds, qh, NN)
            part = dot(kt[64 * h:64 * h + 64, :keys], ds, NN)
            dqt = part if h == 0 else jnp.concatenate([dqt, part], 0)
        dq_ref[0, rows, :] = (jnp.transpose(dqt) * 0.125).astype(jnp.bfloat16)
    dk_ref[0] = dk_acc[...].astype(jnp.bfloat16)
    dv_ref[0] = dv_acc[...].astype(jnp.bfloat16)

def attend_bwd(q, k, v, o, lse, do, causal, bq=256):
    pairs = q.shape[0]
    spec = pl.BlockSpec((1, LEN, LANES), lambda i: (i, 0, 0))
    return pl.pallas_call(
        functools.partial(bwd_kernel, causal, bq),
        grid=(pairs,),
        out_shape=[jax.ShapeDtypeStruct(q.shape, jnp.bfloat16)] * 3,
        in_specs=[spec] * 4 + [pl.BlockSpec((1, 8, LEN), lambda i: (i, 0, 0)), spec],
        out_specs=[spec] * 3,
        scratch_shapes=[pltpu.VMEM((LEN, LANES), jnp.float32)] * 2,
        compiler_params=pltpu.CompilerParams(vmem_limit_bytes=48 << 20),
        cost_estimate=pl.CostEstimate(flops=pairs * 5 * 2 * 2 * LEN * LEN * 64, bytes_accessed=pairs * LEN * LANES * 16, transcendentals=pairs * 2 * LEN * LEN),
    )(q, k, v, o, lse, do)


def cols_kernel(count, x_ref, w_ref, *outs):
    out = dot(x_ref[...], w_ref[0], NN)
    width = out.shape[1] // count
    for i, o_ref in enumerate(outs):
        o_ref[...] = out[:, i * width : (i + 1) * width].astype(o_ref.dtype)


def cols_product(x, weight, count, dtype=jnp.bfloat16):
    n, d = x.shape
    t, _, c = weight.shape
    width = c // count
    return pl.pallas_call(
        functools.partial(cols_kernel, count),
        grid=(t,),
        out_shape=[jax.ShapeDtypeStruct((n, t * width), dtype)] * count,
        in_specs=[
            pl.BlockSpec((n, d), lambda i: (0, 0)),
            pl.BlockSpec((1, d, c), lambda i: (i, 0, 0)),
        ],
        out_specs=[pl.BlockSpec((n, width), lambda i: (0, i))] * count,
        compiler_params=pltpu.CompilerParams(vmem_limit_bytes=48 << 20),
        cost_estimate=pl.CostEstimate(
            flops=2 * n * d * t * c, bytes_accessed=2 * (t * d * c + n * d + n * t * c), transcendentals=0
        ),
    )(x, weight)


def back_kernel(count, *refs):
    ys, w_ref, o_ref = refs[:count], refs[count], refs[count + 1]
    y = jnp.concatenate([y_ref[...] for y_ref in ys], 1) if count > 1 else ys[0][...]
    term = dot(y, w_ref[0], NT)

    @pl.when(pl.program_id(0) == 0)
    def _():
        o_ref[...] = term

    @pl.when(pl.program_id(0) != 0)
    def _():
        o_ref[...] += term


def back_product(ys, weight):
    count = len(ys)
    n = ys[0].shape[0]
    t, d, c = weight.shape
    width = c // count
    return pl.pallas_call(
        functools.partial(back_kernel, count),
        grid=(t,),
        out_shape=jax.ShapeDtypeStruct((n, d), jnp.float32),
        in_specs=[pl.BlockSpec((n, width), lambda i: (0, i))] * count
        + [pl.BlockSpec((1, d, c), lambda i: (i, 0, 0))],
        out_specs=pl.BlockSpec((n, d), lambda i: (0, 0)),
        compiler_params=pltpu.CompilerParams(vmem_limit_bytes=48 << 20),
        cost_estimate=pl.CostEstimate(
            flops=2 * n * d * t * c, bytes_accessed=2 * (t * d * c + 2 * n * d + n * t * c), transcendentals=0
        ),
    )(*ys, weight)


def by_side(grad, t):
    return jnp.swapaxes(grad.reshape(t // 2, 2, *grad.shape[1:]), 0, 1)


def cols_grad_kernel(count, x_ref, *refs):
    ys, o_ref, xt_ref = refs[:count], refs[count], refs[count + 1]

    @pl.when(pl.program_id(0) == 0)
    def _():
        xt_ref[...] = jnp.transpose(x_ref[...])

    y = jnp.concatenate([y_ref[...] for y_ref in ys], 1) if count > 1 else ys[0][...]
    out = dot(xt_ref[...], y, NN).astype(o_ref.dtype)
    d = out.shape[0]
    for j in range(out.shape[1] // LANES):
        o_ref[0, 0, j * d : j * d + d, :] = out[:, j * LANES : j * LANES + LANES]


def cols_grad(x, ys, t):
    count = len(ys)
    n, d = x.shape
    blocks = min(t, ys[0].shape[1] // LANES)
    width = ys[0].shape[1] // blocks
    c = width * count
    whole = blocks == t
    out = pl.pallas_call(
        functools.partial(cols_grad_kernel, count),
        grid=(blocks,),
        out_shape=jax.ShapeDtypeStruct(
            (2, t // 2, c // LANES * d, LANES) if whole else (blocks, 1, c // LANES * d, LANES), jnp.bfloat16
        ),
        in_specs=[pl.BlockSpec((n, d), lambda i: (0, 0))]
        + [pl.BlockSpec((n, width), lambda i: (0, i))] * count,
        out_specs=pl.BlockSpec(
            (1, 1, c // LANES * d, LANES), (lambda i: (i % 2, i // 2, 0, 0)) if whole else (lambda i: (i, 0, 0, 0))
        ),
        scratch_shapes=[pltpu.VMEM((d, n), jnp.bfloat16)],
        compiler_params=pltpu.CompilerParams(vmem_limit_bytes=48 << 20),
        cost_estimate=pl.CostEstimate(
            flops=2 * n * d * blocks * c, bytes_accessed=2 * (blocks * d * c + n * d + n * blocks * c), transcendentals=0
        ),
    )(x, *ys)
    if whole:
        return out
    m = t // blocks
    parts = out.reshape(blocks, count, d, m, LANES // m).transpose(0, 3, 1, 2, 4)
    return by_side(parts.reshape(t, count * d // m, LANES), t)


def cols_result(total, count, d, width):
    total = total.astype(jnp.float32)
    if width < LANES:
        return total.reshape(count, d, width).transpose(1, 0, 2).reshape(d, count * width)
    return total.reshape(-1, d, LANES).transpose(1, 0, 2).reshape(d, count * width)


def rows_grad_kernel(x_ref, y_ref, o_ref):
    out = dot(jnp.transpose(x_ref[...]), y_ref[...], NN).astype(o_ref.dtype)
    r = out.shape[0]
    for j in range(out.shape[1] // LANES):
        o_ref[0, 0, j * r : j * r + r, :] = out[:, j * LANES : j * LANES + LANES]


def rows_grad(x, y, t):
    n, d = y.shape
    blocks = min(t, x.shape[1] // LANES)
    r = x.shape[1] // blocks
    whole = blocks == t
    size = d // LANES * r
    out = pl.pallas_call(
        rows_grad_kernel,
        grid=(blocks,),
        out_shape=jax.ShapeDtypeStruct((2, t // 2, size, LANES) if whole else (blocks, 1, size, LANES), jnp.bfloat16),
        in_specs=[pl.BlockSpec((n, r), lambda i: (0, i)), pl.BlockSpec((n, d), lambda i: (0, 0))],
        out_specs=pl.BlockSpec(
            (1, 1, size, LANES), (lambda i: (i % 2, i // 2, 0, 0)) if whole else (lambda i: (i, 0, 0, 0))
        ),
        compiler_params=pltpu.CompilerParams(vmem_limit_bytes=48 << 20),
        cost_estimate=pl.CostEstimate(
            flops=2 * n * d * blocks * r, bytes_accessed=2 * (blocks * d * r + n * d + n * blocks * r), transcendentals=0
        ),
    )(x, y)
    if whole:
        return out
    m = t // blocks
    parts = out.reshape(blocks, d // LANES, m, r // m, LANES).transpose(0, 2, 1, 3, 4)
    return by_side(parts.reshape(t, size // m, LANES), t)


def rows_result(total, r, d):
    return total.astype(jnp.float32).reshape(d // LANES, r, LANES).transpose(1, 0, 2).reshape(r, d)


def gather_weight(weight):
    dp, t = lax.axis_size("dp"), lax.axis_size("tensor")
    rows = weight.shape[0] // dp
    share = lax.dynamic_slice_in_dim(weight, lax.axis_index("dp") * rows, rows, 0)
    whole = lax.all_gather(share, ("tensor", "dp"), axis=0, tiled=True)
    return whole.reshape(t, weight.shape[0], weight.shape[1])


def widen(weight, count):
    t, r, c = weight.shape
    width = c // count
    if width % LANES == 0:
        return weight
    m = LANES // width
    parts = weight.reshape(t // m, m, r, count, width).transpose(0, 2, 3, 1, 4)
    return parts.reshape(t // m, r, count * LANES)


def swap(value, axis, bit):
    size = lax.axis_size(axis)
    return lax.ppermute(value, axis, [(i, i ^ bit) for i in range(size)])


def settle(total):
    bit = 4
    while bit < lax.axis_size("dp"):
        total = total + swap(total, "dp", bit)
        bit *= 2
    return total


gather_ahead = 1
def x_rows(half):
    return min(max(int(half * 0.36 / 16 + 0.5), 0) * 16, half // 32 * 16)

def piece_list(shapes, size):
    pieces = []
    for w, (r, c) in enumerate(shapes):
        rows = r
        while rows % 64 == 0 and rows * c > size:
            rows //= 2
        pieces += [(w, at, rows) for at in range(0, r, rows)]
    return pieces

def gather_kernel(t_size, pieces, count, *refs):
    ins, outs = refs[:count], refs[count:2*count]
    z_send, y_send, x_send, d_send, plane_recv, x_recv, d_recv, own_sem = refs[2*count:]
    me_d, me = lax.axis_index("dp"), lax.axis_index("tensor")
    core, xpos = me_d % 2, (me_d // 2) % 2
    line, side = me // 2, me % 2
    depth = t_size // 2
    y_mate = 2 * line + 1 - side
    x_mate = me_d + 2 - 4 * xpos
    sibling = me_d + 1 - 2 * core
    barrier = pltpu.get_barrier_semaphore()
    def z_mate(i):
        return 2 * lax.rem(line + i, depth) + side
    for p in [z_mate(i) for i in range(1, depth)] + [y_mate]:
        pl.semaphore_signal(barrier, inc=1, device_id={"tensor": p}, device_id_type=MESH)
    for p in (x_mate, sibling):
        pl.semaphore_signal(barrier, inc=1, device_id={"dp": p}, device_id_type=MESH)
    pl.semaphore_wait(barrier, depth + 2)

    def rows_of(n, kind):
        _, at, rows = pieces[n]
        half = rows // 2
        a = x_rows(half)
        start = at + core * half
        if kind == "plane":
            return pl.ds(pl.multiple_of(start + xpos * a, 16), half - a)
        if kind == "x_out":
            return pl.ds(pl.multiple_of(start + xpos * (half - a), 16), a)
        return pl.ds(pl.multiple_of(start + (1 - xpos) * (half - a), 16), a)
    def has_x(n):
        return x_rows(pieces[n][2] // 2) > 0
    def remote(n, src, block, rows, ss, rs, device):
        return pltpu.make_async_remote_copy(src, outs[pieces[n][0]].at[block, rows, :], ss, rs, device_id=device, device_id_type=MESH)
    def z_copy(n, i):
        rows = rows_of(n, "plane")
        return remote(n, ins[pieces[n][0]].at[rows, :], me, rows, z_send.at[n, i], plane_recv.at[n, me], {"tensor": z_mate(i)})
    def y_own(n):
        rows = rows_of(n, "plane")
        return remote(n, ins[pieces[n][0]].at[rows, :], me, rows, y_send.at[n, me // 2], plane_recv.at[n, me], {"tensor": y_mate})
    def y_copy(n, block):
        rows = rows_of(n, "plane")
        return remote(n, outs[pieces[n][0]].at[block, rows, :], block, rows, y_send.at[n, block // 2], plane_recv.at[n, block], {"tensor": y_mate})
    def x_copy(n, block):
        rows = rows_of(n, "x_out")
        return remote(n, outs[pieces[n][0]].at[block, rows, :], block, rows, x_send.at[n, block], x_recv.at[n, block], {"dp": x_mate})
    def d_copy(n, block, k):
        rows = rows_of(n, ("plane", "x_in")[k])
        return remote(n, outs[pieces[n][0]].at[block, rows, :], block, rows, d_send.at[n, block, k], d_recv.at[n, block, k], {"dp": sibling})
    def landed(n, block, kind, sem):
        ref = outs[pieces[n][0]].at[block, rows_of(n, kind), :]
        pltpu.make_async_copy(ref, ref, sem).wait()
    def loop(lo, hi, body):
        def step(i, _):
            body(i)
            return 0
        lax.fori_loop(lo, hi, step, 0)
    def own_copy(w):
        return pltpu.make_async_copy(ins[w], outs[w].at[me], own_sem.at[w])

    total = len(pieces)
    def launch(n):
        if n < total:
            for i in range(1, depth):
                z_copy(n, i).start()
            y_own(n).start()
    for n in range(gather_ahead):
        launch(n)
    for w in range(count):
        own_copy(w).start()
    for step in range(total + 2):
        n = step
        launch(n + gather_ahead)
        if n < total:
            def z_stage(i):
                block = z_mate(depth - i)
                landed(n, block, "plane", plane_recv.at[n, block])
                y_copy(n, block).start()
                if has_x(n):
                    x_copy(n, block).start()
                d_copy(n, block, 0).start()
            loop(1, depth, z_stage)
        n1 = step - 1
        if 0 <= n1 < total:
            def y_stage(i):
                block = 2 * lax.rem(line + depth - i, depth) + 1 - side
                landed(n1, block, "plane", plane_recv.at[n1, block])
                if has_x(n1):
                    x_copy(n1, block).start()
                d_copy(n1, block, 0).start()
            loop(0, depth, y_stage)
        n2 = step - 2
        if 0 <= n2 < total and has_x(n2):
            def x_stage(i):
                block = lax.rem(me + i, t_size)
                landed(n2, block, "x_in", x_recv.at[n2, block])
                d_copy(n2, block, 1).start()
            loop(1, t_size, x_stage)
    for w in range(count):
        own_copy(w).wait()
    for n in range(total):
        loop(1, depth, lambda i: z_copy(n, i).wait_send())
        y_own(n).wait_send()
        loop(1, depth, lambda i: y_copy(n, z_mate(i)).wait_send())
        def finish(i):
            block = lax.rem(me + i, t_size)
            for k in range(2 if has_x(n) else 1):
                d_copy(n, block, k).wait_send()
            if has_x(n):
                x_copy(n, block).wait_send()
        loop(1, t_size, finish)
        def final(i):
            block = lax.rem(me + i, t_size)
            _, at, rows = pieces[n]
            half = rows // 2
            a = x_rows(half)
            start = at + (1 - core) * half
            got = pl.ds(pl.multiple_of(start + xpos * a, 16), half - a)
            ref = outs[pieces[n][0]].at[block, got, :]
            pltpu.make_async_copy(ref, ref, d_recv.at[n, block, 0]).wait()
            if has_x(n):
                got = pl.ds(pl.multiple_of(start + (1 - xpos) * (half - a), 16), a)
                ref = outs[pieces[n][0]].at[block, got, :]
                pltpu.make_async_copy(ref, ref, d_recv.at[n, block, 1]).wait()
        loop(1, t_size, final)

def gather_weights(weights, t, cid, size=1 << 17):
    count = len(weights)
    shapes = [w.shape for w in weights]
    pieces = piece_list(shapes, size)
    dma = pltpu.SemaphoreType.DMA
    depth = t // 2
    m = len(pieces)
    return pl.pallas_call(
        functools.partial(gather_kernel, t, pieces, count),
        out_shape=[jax.ShapeDtypeStruct((t,) + w.shape, w.dtype) for w in weights],
        in_specs=[pl.BlockSpec(memory_space=pl.ANY)] * count,
        out_specs=[pl.BlockSpec(memory_space=pl.ANY)] * count,
        scratch_shapes=[dma((m, depth)), dma((m, depth)), dma((m, t)), dma((m, t, 2)), dma((m, t)), dma((m, t)), dma((m, t, 2)), dma((count,))],
        compiler_params=pltpu.CompilerParams(collective_id=cid, has_side_effects=True),
    )(*weights)


def reduce_kernel(depth, pieces, count, size, *refs):
    ins, outs = refs[:count], refs[count:2*count]
    own, r1, r2y, r2x, r3y, r3x, s3y, r4y, r4x, fin, send, recv, local, store = refs[2*count:]
    H = size // 2
    Hy = H // 2
    Q = H // 4
    me_d, me = lax.axis_index("dp"), lax.axis_index("tensor")
    core, xpos = me_d % 2, (me_d // 2) % 2
    line, side = me // 2, me % 2
    y_mate = {"tensor": 2 * line + 1 - side}
    x_mate = {"dp": me_d + 2 - 4 * xpos}
    sibling = {"dp": me_d + 1 - 2 * core}
    z_lines = [None] + [lax.rem(line + i, depth) for i in range(1, depth)]
    barrier = pltpu.get_barrier_semaphore()
    for p in [{"tensor": 2 * z + side} for z in z_lines[1:]] + [y_mate, x_mate, sibling]:
        pl.semaphore_signal(barrier, inc=1, device_id=p, device_id_type=MESH)
    pl.semaphore_wait(barrier, depth + 2)

    def remote(src, dst, n, k, device):
        return pltpu.make_async_remote_copy(src, dst, send.at[n, k], recv.at[n, k], device_id=device, device_id_type=MESH)
    def at16(v):
        return pl.multiple_of(v, 16)
    def load(n):
        w, at = pieces[n]
        return pltpu.make_async_copy(ins[w].at[:, :, pl.ds(at16(at + core * H), H), :], own.at[n], local.at[n])
    def copy_core(n):
        w, at = pieces[n]
        return remote(ins[w].at[:, :, pl.ds(at16(at + (1 - core) * H), H), :], r1.at[n], n, 0, sibling)
    def copy_y(n):
        return remote(r1.at[n, 1 - side, :, pl.ds(0, Hy), :], r2y.at[n], n, 1, y_mate)
    def copy_x(n):
        return remote(r1.at[n, :, :, pl.ds(at16(Hy + (1 - xpos) * Q), Q), :], r2x.at[n], n, 2, x_mate)
    def copy_yz(n, i):
        return remote(r2y.at[n, z_lines[i]], r3y.at[n, i - 1], n, 2 + i, {"tensor": 2 * z_lines[i] + side})
    def copy_xy(n):
        return remote(r2x.at[n, 1 - side], r3x.at[n], n, 2 + depth, y_mate)
    def copy_yx(n):
        return remote(s3y.at[n], r4y.at[n], n, 3 + depth, x_mate)
    def copy_xz(n, i):
        return remote(r3x.at[n, z_lines[i]], r4x.at[n, i - 1], n, 3 + depth + i, {"tensor": 2 * z_lines[i] + side})
    def copy_xx(n):
        ref = fin.at[n, pl.ds(at16(core * H + Hy + xpos * Q), Q), :]
        return remote(ref, ref, n, 3 + 2 * depth, x_mate)
    def copy_back(n):
        ref = fin.at[n, pl.ds(at16(core * H), H), :]
        return remote(ref, ref, n, 4 + 2 * depth, sibling)
    def write(n):
        w, at = pieces[n]
        return pltpu.make_async_copy(fin.at[n], outs[w].at[pl.ds(at, size), :], store.at[n])
    def loop(hi, body):
        def step(i, _):
            body(i)
            return 0
        lax.fori_loop(0, hi, step, 0)

    total = len(pieces)
    for n in range(total):
        load(n).start()
        copy_core(n).start()

    def stage0(n):
        load(n).wait()
        copy_core(n).wait_recv()
        def add(i):
            a, b = i // depth, i % depth
            r1[n, a, b] = r1[n, a, b] + own[n, a, b]
        loop(2 * depth, add)
        copy_y(n).start()
        copy_x(n).start()
    def stage1(n):
        copy_y(n).wait_recv()
        def add(i):
            r2y[n, i] = r2y[n, i] + r1[n, side, i, 0:Hy, :]
        loop(depth, add)
        for i in range(1, depth):
            copy_yz(n, i).start()
        copy_x(n).wait_recv()
        def addx(i):
            a, b = i // depth, i % depth
            r2x[n, a, b] = r2x[n, a, b] + r1[n, a, b, pl.ds(at16(Hy + xpos * Q), Q), :]
        loop(2 * depth, addx)
        copy_xy(n).start()
    def stage2(n):
        copy_xy(n).wait_recv()
        def add(i):
            r3x[n, i] = r3x[n, i] + r2x[n, side, i]
        loop(depth, add)
        for i in range(1, depth):
            copy_xz(n, i).start()
        for i in range(1, depth):
            copy_yz(n, i).wait_recv()
        part = r2y[n, line].astype(jnp.float32)
        for i in range(1, depth):
            part = part + r3y[n, i - 1].astype(jnp.float32)
        s3y[n] = part.astype(jnp.bfloat16)
        copy_yx(n).start()
    def stage3(n):
        for i in range(1, depth):
            copy_xz(n, i).wait_recv()
        part = r3x[n, line].astype(jnp.float32)
        for i in range(1, depth):
            part = part + r4x[n, i - 1].astype(jnp.float32)
        fin[n, pl.ds(at16(core * H + Hy + xpos * Q), Q), :] = part.astype(jnp.bfloat16)
        copy_xx(n).start()
        copy_yx(n).wait_recv()
        fin[n, pl.ds(at16(core * H), Hy), :] = s3y[n] + r4y[n]
    def stage4(n):
        copy_xx(n).wait_recv()
        copy_back(n).start()
    def stage5(n):
        copy_back(n).wait_recv()
        write(n).start()
    stages = [stage0, stage1, stage2, stage3, stage4, stage5]
    for step in range(total + len(stages) - 1):
        for k in range(len(stages) - 1, -1, -1):
            if 0 <= step - k < total:
                stages[k](step - k)
    for n in range(total):
        copy_core(n).wait_send()
        copy_y(n).wait_send()
        copy_x(n).wait_send()
        copy_xy(n).wait_send()
        copy_yx(n).wait_send()
        copy_xx(n).wait_send()
        copy_back(n).wait_send()
        for i in range(1, depth):
            copy_yz(n, i).wait_send()
            copy_xz(n, i).wait_send()
        write(n).wait()

def reduce_grads(grads, t, cid, size=1024):
    count = len(grads)
    depth = t // 2
    pieces = [(w, at) for w, g in enumerate(grads) for at in range(0, g.shape[2], size)]
    m = len(pieces)
    H = size // 2
    Hy, Q = H // 2, H // 4
    dma = pltpu.SemaphoreType.DMA
    def buf(*shape):
        return pltpu.VMEM((m,) + shape + (LANES,), jnp.bfloat16)
    return pl.pallas_call(
        functools.partial(reduce_kernel, depth, pieces, count, size),
        out_shape=[jax.ShapeDtypeStruct(g.shape[2:], jnp.bfloat16) for g in grads],
        in_specs=[pl.BlockSpec(memory_space=pl.ANY)] * count,
        out_specs=[pl.BlockSpec(memory_space=pl.ANY)] * count,
        scratch_shapes=[buf(2, depth, H), buf(2, depth, H), buf(depth, Hy), buf(2, depth, Q), buf(depth - 1, Hy), buf(depth, Q), buf(Hy), buf(Hy), buf(depth - 1, Q), buf(size),
            dma((m, 5 + 2 * depth)), dma((m, 5 + 2 * depth)), dma((m,)), dma((m,))],
        compiler_params=pltpu.CompilerParams(collective_id=cid, has_side_effects=True, vmem_limit_bytes=56 << 20),
    )(*grads)


def normalize(rows_in, gain_row, shift_row):
    row_mean = jnp.mean(rows_in, axis=-1, keepdims=True)
    centered = rows_in - row_mean
    variance = jnp.mean(centered * centered, axis=-1, keepdims=True)
    return centered * lax.rsqrt(variance + norm_eps) * gain_row + shift_row


def gelu_tanh(values):
    return jax.nn.gelu(values, approximate=True)


def product(values, weight):
    return jnp.dot(values, weight, preferred_element_type=jnp.float32)


def per_device(
    tokens,
    memory,
    self_qkv,
    self_out,
    cross_q,
    cross_kv,
    cross_out,
    hidden_weight,
    hidden_bias,
    output_weight,
    output_bias,
    norm_gain,
    norm_shift,
    grad_output,
):
    low = jnp.bfloat16
    t = lax.axis_size("tensor")
    n, d = tokens.shape
    w_qkv, w_so, w_cq, w_kv, w_co = gather_weights(
        [self_qkv.reshape(d, -1), self_out, cross_q, cross_kv.reshape(d, -1), cross_out], t, 8
    )
    w_qkv, w_cq, w_kv = widen(w_qkv, 3), widen(w_cq, 1), widen(w_kv, 2)
    w_so, w_co = w_so.reshape(d, d), w_co.reshape(d, d)
    w_hid = gather_weight(hidden_weight)
    w_out = gather_weight(output_weight).reshape(-1, d)
    bias_all = lax.all_gather(hidden_bias, "tensor", axis=0, tiled=True)

    qkv = cols_product(tokens, w_qkv, 3)
    sq, sk, sv = to_heads(qkv, t, 0)
    so, s_lse = attend_fwd(sq, sk, sv, True, 512)
    (self_heads,) = to_tokens([so], n, d, t, 1)
    branch_one = product(self_heads, w_so)
    normed_one, pull_one = jax.vjp(
        normalize, residual_alpha * tokens.astype(jnp.float32) + branch_one, norm_gain[0], norm_shift[0]
    )
    normed_one_low = normed_one.astype(low)
    kv = cols_product(memory, w_kv, 2)
    cq = cols_product(normed_one_low, w_cq, 1)
    cq, ck, cv = to_heads([*cq, *kv], t, 2)
    co, c_lse = attend_fwd(cq, ck, cv, False, 512)
    (cross_heads,) = to_tokens([co], n, d, t, 3)
    branch_two = product(cross_heads, w_co)
    normed_two, pull_two = jax.vjp(
        normalize, residual_alpha * normed_one + branch_two, norm_gain[1], norm_shift[1]
    )
    normed_two_low = normed_two.astype(low)
    (hidden_low,) = cols_product(normed_two_low, w_hid, 1, jnp.float32)
    hidden_pre = hidden_low + bias_all
    activated, gelu_pull = jax.vjp(gelu_tanh, hidden_pre)
    activated_low = activated.astype(low)
    branch_three = product(activated_low, w_out)
    layer_out, pull_three = jax.vjp(
        normalize, residual_alpha * normed_two + branch_three + output_bias, norm_gain[2], norm_shift[2]
    )
    grad_three, gain_three, shift_three = pull_three(grad_output.astype(jnp.float32))
    bias_out_grad = jnp.sum(grad_three, axis=0)
    grad_three_low = grad_three.astype(low)
    out_weight_part = rows_grad(activated_low, grad_three_low, t)
    grad_act = lax.dot_general(grad_three_low, w_out, NT, preferred_element_type=jnp.float32)
    grad_hidden = gelu_pull(grad_act)[0].astype(low)
    hidden_bias_grad = jnp.sum(grad_hidden, axis=0, dtype=jnp.float32)
    hidden_weight_part = cols_grad(normed_two_low, [grad_hidden], t)
    size = LEN * 8 // t
    out_weight_grad, hidden_weight_grad = reduce_grads([out_weight_part, hidden_weight_part], t, 9, size)
    out_weight_grad = rows_result(settle(out_weight_grad), output_weight.shape[0], d)
    hidden_weight_grad = cols_result(settle(hidden_weight_grad), 1, d, hidden_weight.shape[1])
    grad_two, gain_two, shift_two = pull_two(
        residual_alpha * grad_three + back_product([grad_hidden], w_hid)
    )
    grad_two_low = grad_two.astype(low)
    cross_out_part = rows_grad(cross_heads, grad_two_low, t)
    grad_co = lax.dot_general(grad_two_low, w_co, NT, preferred_element_type=jnp.float32).astype(low)
    (grad_co,) = to_heads([grad_co], t, 4)
    cross_grads = attend_bwd(cq, ck, cv, co, c_lse, grad_co, False, 256)
    g_cq, g_ck, g_cv = to_tokens(cross_grads, n, d, t, 5)
    cross_q_part = cols_grad(normed_one_low, [g_cq], t)
    cross_kv_part = cols_grad(memory, [g_ck, g_cv], t)
    cross_out_grad, cross_q_grad, cross_kv_grad = reduce_grads(
        [cross_out_part, cross_q_part, cross_kv_part], t, 10, size
    )
    cross_out_grad = rows_result(settle(cross_out_grad), cross_out.shape[0], d)
    cross_q_grad = cols_result(settle(cross_q_grad), 1, d, cross_q.shape[1])
    cross_kv_grad = cols_result(settle(cross_kv_grad), 2, d, cross_kv.shape[2]).reshape(cross_kv.shape)
    grad_memory = back_product([g_ck, g_cv], w_kv)
    grad_one, gain_one, shift_one = pull_one(residual_alpha * grad_two + back_product([g_cq], w_cq))
    grad_one_low = grad_one.astype(low)
    self_out_part = rows_grad(self_heads, grad_one_low, t)
    grad_so = lax.dot_general(grad_one_low, w_so, NT, preferred_element_type=jnp.float32).astype(low)
    (grad_so,) = to_heads([grad_so], t, 6)
    self_grads = attend_bwd(sq, sk, sv, so, s_lse, grad_so, True, 256)
    g_qkv = to_tokens(self_grads, n, d, t, 7)
    self_qkv_part = cols_grad(tokens, g_qkv, t)
    self_out_grad, self_qkv_grad = reduce_grads([self_out_part, self_qkv_part], t, 11, size)
    self_out_grad = rows_result(settle(self_out_grad), self_out.shape[0], d)
    self_qkv_grad = cols_result(settle(self_qkv_grad), 3, d, self_qkv.shape[2]).reshape(self_qkv.shape)
    grad_tokens = residual_alpha * grad_one + back_product(g_qkv, w_qkv)
    gain_total, shift_total, bias_total, hidden_bias_total = lax.psum(
        (
            jnp.stack([gain_one, gain_two, gain_three]),
            jnp.stack([shift_one, shift_two, shift_three]),
            bias_out_grad,
            hidden_bias_grad,
        ),
        ("dp", "tensor"),
    )
    units = hidden_bias.shape[0]
    hidden_bias_total = lax.dynamic_slice_in_dim(hidden_bias_total, lax.axis_index("tensor") * units, units, 0)
    return (
        layer_out.astype(low),
        grad_tokens,
        grad_memory,
        self_qkv_grad,
        self_out_grad,
        cross_q_grad,
        cross_kv_grad,
        cross_out_grad,
        hidden_weight_grad,
        hidden_bias_total,
        out_weight_grad,
        bias_total,
        gain_total,
        shift_total,
    )


def solution(mesh):
    return jax.shard_map(
        per_device,
        mesh=mesh,
        in_specs=(
            P(("dp", "tensor"), None),
            P(("dp", "tensor"), None),
            P(None, None, "tensor"),
            P("tensor", None),
            P(None, "tensor"),
            P(None, None, "tensor"),
            P("tensor", None),
            P(None, "tensor"),
            P("tensor"),
            P("tensor", None),
            P(),
            P(),
            P(),
            P(("dp", "tensor"), None),
        ),
        out_specs=(
            P(("dp", "tensor"), None),
            P(("dp", "tensor"), None),
            P(("dp", "tensor"), None),
            P(None, None, "tensor"),
            P("tensor", None),
            P(None, "tensor"),
            P(None, None, "tensor"),
            P("tensor", None),
            P(None, "tensor"),
            P("tensor"),
            P("tensor", None),
            P(),
            P(),
            P(),
        ),
        check_vma=False,
    )
```

```python
import functools
import math

import jax
import jax.numpy as jnp
from jax import lax
from jax.experimental import pallas as pl
from jax.experimental.pallas import tpu as pltpu
from jax.sharding import PartitionSpec as P

MESH = pl.DeviceIdType.MESH
DH = 64
LANES = 128
LEN = 1024

residual_alpha = 300.0**0.25
norm_eps = 1e-05


def loop(lo, hi, body):
    def step(i, _):
        body(i)
        return 0

    lax.fori_loop(lo, hi, step, 0)


def weave(main, back):
    for steps in main:
        while steps != 0 and next(back, None) is not None:
            steps -= 1
    for _ in back:
        pass


class Place:
    def __init__(self, t):
        self.t, self.depth = t, t // 2
        self.d, self.me = lax.axis_index("dp"), lax.axis_index("tensor")
        self.core, self.xpos = self.d % 2, (self.d // 2) % 2
        self.line, self.side = self.me // 2, self.me % 2
        self.y_mate = {"tensor": 2 * self.line + 1 - self.side}
        self.x_mate = {"dp": self.d + 2 - 4 * self.xpos}
        self.sibling = {"dp": self.d + 1 - 2 * self.core}

    def line_at(self, i):
        return lax.rem(self.line + i, self.depth)

    def z_mate(self, i):
        return {"tensor": 2 * self.line_at(i) + self.side}

    def greet(self):
        barrier = pltpu.get_barrier_semaphore()
        peers = [{"tensor": lax.rem(self.me + i, self.t)} for i in range(1, self.t)]
        for p in peers + [self.x_mate, self.sibling]:
            pl.semaphore_signal(barrier, inc=1, device_id=p, device_id_type=MESH)
        pl.semaphore_wait(barrier, self.t + 1)


def remote(src, dst, send, recv, device):
    return pltpu.make_async_remote_copy(src, dst, send, recv, device_id=device, device_id_type=MESH)


def landed(ref, sem):
    pltpu.make_async_copy(ref, ref, sem).wait()


def at16(v):
    return pl.multiple_of(v, 16)


def rows_at(start, count):
    return pl.ds(pl.multiple_of(start, count), count)


class Slots:
    def __init__(self, t, n, d):
        self.block = math.gcd(n, LEN)
        self.blocks = n // self.block
        self.per_seq = LEN // self.block
        self.wide = d // LANES
        self.total = n * t // LEN * self.wide
        self.pairs = -(-self.total // t)
        self.units = self.blocks * self.wide
        self.lands = self.pairs * self.per_seq


class ToHeads:
    def __init__(self, place, slots, ins, outs, send, recv):
        self.place, self.slots, self.ins, self.outs, self.send, self.recv = place, slots, ins, outs, send, recv

    def unit(self, a, u):
        s = self.slots
        j, p = u // s.wide, u % s.wide
        g = self.place.me * s.blocks + j
        q = (g // s.per_seq) * s.wide + p
        dst, slot, k = q // s.pairs, q % s.pairs, g % s.per_seq
        src = self.ins[a].at[rows_at(j * s.block, s.block), rows_at(p * LANES, LANES)]
        to = self.outs[a].at[slot, rows_at(k * s.block, s.block), :]
        return dst, src, to, self.send.at[a, u], self.recv.at[a, slot * s.per_seq + k]

    def start(self):
        for a in range(len(self.ins)):

            def one(u):
                dst, src, to, ss, rs = self.unit(a, u)

                @pl.when(dst == self.place.me)
                def _():
                    pltpu.make_async_copy(src, to, rs).start()

                @pl.when(dst != self.place.me)
                def _():
                    remote(src, to, ss, rs, {"tensor": dst}).start()

            loop(0, self.slots.units, one)

    def wait_slot(self, slot):
        s = self.slots

        @pl.when(self.place.me * s.pairs + slot < s.total)
        def _():
            for a in range(len(self.ins)):
                loop(
                    0,
                    s.per_seq,
                    lambda k: landed(
                        self.outs[a].at[slot, rows_at(k * s.block, s.block), :], self.recv.at[a, slot * s.per_seq + k]
                    ),
                )

    def finish(self):
        for a in range(len(self.ins)):

            def one(u):
                dst, src, to, ss, rs = self.unit(a, u)

                @pl.when(dst != self.place.me)
                def _():
                    remote(src, to, ss, rs, {"tensor": dst}).wait_send()

            loop(0, self.slots.units, one)


class ToTokens:
    def __init__(self, place, slots, ins, outs, send, recv):
        self.place, self.slots, self.ins, self.outs, self.send, self.recv = place, slots, ins, outs, send, recv

    def unit(self, a, slot, k):
        s = self.slots
        q = self.place.me * s.pairs + slot
        g = (q // s.wide) * s.per_seq + k
        dst, j, p = g // s.blocks, g % s.blocks, q % s.wide
        src = self.ins[a].at[slot, rows_at(k * s.block, s.block), :]
        to = self.outs[a].at[rows_at(j * s.block, s.block), rows_at(p * LANES, LANES)]
        return q < s.total, dst, src, to, self.send.at[a, slot * s.per_seq + k], self.recv.at[a, j * s.wide + p]

    def start_slot(self, slot):
        for a in range(len(self.ins)):

            def one(k):
                real, dst, src, to, ss, rs = self.unit(a, slot, k)

                @pl.when(real & (dst == self.place.me))
                def _():
                    pltpu.make_async_copy(src, to, rs).start()

                @pl.when(real & (dst != self.place.me))
                def _():
                    remote(src, to, ss, rs, {"tensor": dst}).start()

            loop(0, self.slots.per_seq, one)

    def finish(self):
        s = self.slots
        for a in range(len(self.ins)):

            def sent(u):
                real, dst, src, to, ss, rs = self.unit(a, u // s.per_seq, u % s.per_seq)

                @pl.when(real & (dst != self.place.me))
                def _():
                    remote(src, to, ss, rs, {"tensor": dst}).wait_send()

            loop(0, s.lands, sent)

            def got(r):
                j, p = r // s.wide, r % s.wide
                landed(
                    self.outs[a].at[rows_at(j * s.block, s.block), rows_at(p * LANES, LANES)], self.recv.at[a, r]
                )

            loop(0, s.units, got)


def reshard_sems(slots, heads, tokens):
    dma = pltpu.SemaphoreType.DMA
    return [dma((heads, slots.units)), dma((heads, slots.lands)), dma((tokens, slots.lands)), dma((tokens, slots.units))]


NT = (((1,), (1,)), ((), ()))
NN = (((1,), (0,)), ((), ()))
LOG2E = math.log2(math.e)


def dot(a, b, dims):
    return lax.dot_general(a, b, dims, preferred_element_type=jnp.float32)


def lane_half(shape, h):
    return (lax.broadcasted_iota(jnp.int32, shape, len(shape) - 1) // DH) == h


def attend_block(i, bq, causal, q_ref, k_ref, v_ref, o_ref, lse_ref):
    keys = bq * (i + 1) if causal else LEN
    rows = pl.ds(i * bq, bq)
    q = q_ref[rows, :] * jnp.bfloat16(0.125)
    k = k_ref[:keys, :]
    v = v_ref[:keys, :]
    total = None
    for h in (0, 1):
        qh = jnp.where(lane_half(q.shape, h), q, jnp.bfloat16(0))
        s = dot(qh, k, NT)
        if causal:
            tail = s[:, keys - bq :]
            r = lax.broadcasted_iota(jnp.int32, tail.shape, 0)
            c = lax.broadcasted_iota(jnp.int32, tail.shape, 1)
            tail = jnp.where(c <= r, tail, -1e30)
            s = tail if keys == bq else jnp.concatenate([s[:, : keys - bq], tail], 1)
        m = jnp.max(s, axis=-1, keepdims=True)
        e = jnp.exp2((s - m) * LOG2E)
        total_e = jnp.sum(e, axis=-1, keepdims=True)
        o = dot(e.astype(jnp.bfloat16), v, NN) / total_e
        total = o if h == 0 else jnp.where(lane_half(o.shape, 0), total, o)
        lse = m * LOG2E + jnp.log2(total_e)
        lse_ref[h : h + 1, rows] = jnp.transpose(jnp.broadcast_to(lse, (bq, LANES)))[0:1]
    o_ref[rows, :] = total.astype(jnp.bfloat16)


def attend_back_block(i, bq, causal, q_ref, k_ref, v_ref, o_ref, lse_ref, do_ref, dq_ref, kt_ref, dk_ref, dv_ref):
    keys = bq * (i + 1) if causal else LEN
    rows = pl.ds(i * bq, bq)
    q = q_ref[rows, :] * jnp.bfloat16(0.125)
    do = do_ref[rows, :]
    prod = jnp.transpose(do.astype(jnp.float32) * o_ref[rows, :].astype(jnp.float32))
    k = k_ref[:keys, :]
    v = v_ref[:keys, :]
    dqt = []
    for h in (0, 1):
        mask = lane_half(q.shape, h)
        qh = jnp.where(mask, q, jnp.bfloat16(0))
        doh = jnp.where(mask, do, jnp.bfloat16(0))
        delta = jnp.sum(prod[DH * h : DH * h + DH], axis=0, keepdims=True)
        p = jnp.exp2(dot(k, qh, NT) * LOG2E - lse_ref[h : h + 1, rows])
        if causal:
            tail = p[keys - bq :, :]
            r = lax.broadcasted_iota(jnp.int32, tail.shape, 1)
            c = lax.broadcasted_iota(jnp.int32, tail.shape, 0)
            tail = jnp.where(c <= r, tail, 0.0)
            p = tail if keys == bq else jnp.concatenate([p[: keys - bq], tail], 0)
        ds = (p * (dot(v, doh, NT) - delta)).astype(jnp.bfloat16)
        dv_ref[:keys, :] += dot(p.astype(jnp.bfloat16), doh, NN)
        dk_ref[:keys, :] += dot(ds, qh, NN)
        dqt.append(dot(kt_ref[DH * h : DH * h + DH, :keys], ds, NN))
    dq_ref[rows, :] = (jnp.transpose(jnp.concatenate(dqt, 0)) * 0.125).astype(jnp.bfloat16)


def x_rows(half):
    return min(int(half * 0.36 / 16 + 0.5) * 16, half // 32 * 16)


class Gather:
    def __init__(self, weights, t, size=1 << 17):
        self.t, self.depth = t, t // 2
        self.shapes = [w.shape for w in weights]
        self.pieces = []
        for w, (r, c) in enumerate(self.shapes):
            rows = r
            while rows % 64 == 0 and rows * c > size:
                rows //= 2
            self.pieces += [(w, at, rows) for at in range(0, r, rows)]
        m, dma = len(self.pieces), pltpu.SemaphoreType.DMA
        self.out_shape = [jax.ShapeDtypeStruct((t,) + w.shape, w.dtype) for w in weights]
        self.scratch = [
            dma((m, self.depth)),
            dma((m, self.depth)),
            dma((m, t)),
            dma((m, t, 2)),
            dma((m, t)),
            dma((m, t)),
            dma((m, t, 2)),
            dma((len(weights),)),
        ]

    def rows_of(self, n, kind, core):
        _, at, rows = self.pieces[n]
        half = rows // 2
        a = x_rows(half)
        start, xpos = at + core * half, self.place.xpos
        if kind == "plane":
            return pl.ds(at16(start + xpos * a), half - a)
        if kind == "x_out":
            return pl.ds(at16(start + xpos * (half - a)), a)
        return pl.ds(at16(start + (1 - xpos) * (half - a)), a)

    def steps(self, place, ins, outs, scratch):
        z_send, y_send, x_send, d_send, plane_recv, x_recv, d_recv, own_sem = scratch
        self.place = place
        me, depth, t, pieces = place.me, self.depth, self.t, self.pieces

        def has_x(n):
            return x_rows(pieces[n][2] // 2) > 0

        def rows_of(n, kind, core=place.core):
            return self.rows_of(n, kind, core)

        def part(n, block, kind, core=place.core):
            return outs[pieces[n][0]].at[block, rows_of(n, kind, core), :]

        def column(i, side):
            return 2 * place.line_at(depth - i) + side

        def own(n):
            return ins[pieces[n][0]].at[rows_of(n, "plane"), :]

        def z_copy(n, i):
            return remote(own(n), part(n, me, "plane"), z_send.at[n, i], plane_recv.at[n, me], place.z_mate(i))

        def y_own(n):
            return remote(own(n), part(n, me, "plane"), y_send.at[n, place.line], plane_recv.at[n, me], place.y_mate)

        def y_copy(n, block):
            ref = part(n, block, "plane")
            return remote(ref, ref, y_send.at[n, block // 2], plane_recv.at[n, block], place.y_mate)

        def x_copy(n, block):
            ref = part(n, block, "x_out")
            return remote(ref, ref, x_send.at[n, block], x_recv.at[n, block], place.x_mate)

        def d_copy(n, block, k):
            ref = part(n, block, ("plane", "x_in")[k])
            return remote(ref, ref, d_send.at[n, block, k], d_recv.at[n, block, k], place.sibling)

        def own_copy(w):
            return pltpu.make_async_copy(ins[w], outs[w].at[me], own_sem.at[w])

        total = len(pieces)

        def launch(n):
            if n < total:
                for i in range(1, depth):
                    z_copy(n, i).start()
                y_own(n).start()

        launch(0)
        for w in range(len(ins)):
            own_copy(w).start()
        yield True
        for step in range(total + 2):
            launch(step + 1)
            n = step
            if n < total:

                def z_stage(i):
                    block = column(i, place.side)
                    landed(part(n, block, "plane"), plane_recv.at[n, block])
                    y_copy(n, block).start()
                    if has_x(n):
                        x_copy(n, block).start()
                    d_copy(n, block, 0).start()

                loop(1, depth, z_stage)
            n1 = step - 1
            if 0 <= n1 < total:

                def y_stage(i):
                    block = column(i, 1 - place.side)
                    landed(part(n1, block, "plane"), plane_recv.at[n1, block])
                    if has_x(n1):
                        x_copy(n1, block).start()
                    d_copy(n1, block, 0).start()

                loop(0, depth, y_stage)
            n2 = step - 2
            if 0 <= n2 < total and has_x(n2):

                def x_stage(i):
                    block = lax.rem(me + i, t)
                    landed(part(n2, block, "x_in"), x_recv.at[n2, block])
                    d_copy(n2, block, 1).start()

                loop(1, t, x_stage)
            yield True
        for w in range(len(ins)):
            own_copy(w).wait()
        for n in range(total):
            loop(1, depth, lambda i: z_copy(n, i).wait_send())
            y_own(n).wait_send()
            loop(1, depth, lambda i: y_copy(n, column(i, place.side)).wait_send())

            def finish(i):
                block = lax.rem(me + i, t)
                for k in range(2 if has_x(n) else 1):
                    d_copy(n, block, k).wait_send()
                    landed(part(n, block, ("plane", "x_in")[k], 1 - place.core), d_recv.at[n, block, k])
                if has_x(n):
                    x_copy(n, block).wait_send()

            loop(1, t, finish)
        yield True


class Reduce:
    def __init__(self, grads, t, size):
        self.t, self.depth, self.size = t, t // 2, size
        self.pieces = [(w, at) for w, g in enumerate(grads) for at in range(0, g.shape[2], size)]
        m, depth, dma = len(self.pieces), self.depth, pltpu.SemaphoreType.DMA
        H, Hy, Q = size // 2, size // 4, size // 8

        def buf(*shape):
            return pltpu.VMEM((m,) + shape + (LANES,), jnp.bfloat16)

        self.out_shape = [jax.ShapeDtypeStruct(g.shape[2:], jnp.bfloat16) for g in grads]
        self.scratch = [
            buf(2, depth, H),
            buf(2, depth, H),
            buf(depth, Hy),
            buf(2, depth, Q),
            buf(depth - 1, Hy),
            buf(depth, Q),
            buf(Hy),
            buf(Hy),
            buf(depth - 1, Q),
            buf(size),
            dma((m, 5 + 2 * depth)),
            dma((m, 5 + 2 * depth)),
            dma((m,)),
            dma((m,)),
        ]

    def steps(self, place, ins, outs, scratch):
        own, r1, r2y, r2x, r3y, r3x, s3y, r4y, r4x, fin, send, recv, local, store = scratch
        size, depth, pieces = self.size, self.depth, self.pieces
        H, Hy, Q = size // 2, size // 4, size // 8
        core, xpos, line, side = place.core, place.xpos, place.line, place.side

        def move(src, dst, n, k, device):
            return remote(src, dst, send.at[n, k], recv.at[n, k], device)

        def load(n):
            w, at = pieces[n]
            return pltpu.make_async_copy(ins[w].at[:, :, pl.ds(at16(at + core * H), H), :], own.at[n], local.at[n])

        def copy_core(n):
            w, at = pieces[n]
            return move(ins[w].at[:, :, pl.ds(at16(at + (1 - core) * H), H), :], r1.at[n], n, 0, place.sibling)

        def copy_y(n):
            return move(r1.at[n, 1 - side, :, pl.ds(0, Hy), :], r2y.at[n], n, 1, place.y_mate)

        def copy_x(n):
            return move(r1.at[n, :, :, pl.ds(at16(Hy + (1 - xpos) * Q), Q), :], r2x.at[n], n, 2, place.x_mate)

        def copy_yz(n, i):
            return move(r2y.at[n, place.line_at(i)], r3y.at[n, i - 1], n, 2 + i, place.z_mate(i))

        def copy_xy(n):
            return move(r2x.at[n, 1 - side], r3x.at[n], n, 2 + depth, place.y_mate)

        def copy_yx(n):
            return move(s3y.at[n], r4y.at[n], n, 3 + depth, place.x_mate)

        def copy_xz(n, i):
            return move(r3x.at[n, place.line_at(i)], r4x.at[n, i - 1], n, 3 + depth + i, place.z_mate(i))

        def copy_xx(n):
            ref = fin.at[n, pl.ds(at16(core * H + Hy + xpos * Q), Q), :]
            return move(ref, ref, n, 3 + 2 * depth, place.x_mate)

        def copy_back(n):
            ref = fin.at[n, pl.ds(at16(core * H), H), :]
            return move(ref, ref, n, 4 + 2 * depth, place.sibling)

        def write(n):
            w, at = pieces[n]
            return pltpu.make_async_copy(fin.at[n], outs[w].at[pl.ds(at, size), :], store.at[n])

        total = len(pieces)
        for n in range(total):
            load(n).start()
            copy_core(n).start()
        yield True

        def stage0(n):
            load(n).wait()
            copy_core(n).wait_recv()

            def add(i):
                a, b = i // depth, i % depth
                r1[n, a, b] = r1[n, a, b] + own[n, a, b]

            loop(0, 2 * depth, add)
            copy_y(n).start()
            copy_x(n).start()

        def stage1(n):
            copy_y(n).wait_recv()

            def add(i):
                r2y[n, i] = r2y[n, i] + r1[n, side, i, 0:Hy, :]

            loop(0, depth, add)
            for i in range(1, depth):
                copy_yz(n, i).start()
            copy_x(n).wait_recv()

            def addx(i):
                a, b = i // depth, i % depth
                r2x[n, a, b] = r2x[n, a, b] + r1[n, a, b, pl.ds(at16(Hy + xpos * Q), Q), :]

            loop(0, 2 * depth, addx)
            copy_xy(n).start()

        def stage2(n):
            copy_xy(n).wait_recv()

            def add(i):
                r3x[n, i] = r3x[n, i] + r2x[n, side, i]

            loop(0, depth, add)
            for i in range(1, depth):
                copy_xz(n, i).start()
            for i in range(1, depth):
                copy_yz(n, i).wait_recv()
            part = r2y[n, line].astype(jnp.float32)
            for i in range(1, depth):
                part = part + r3y[n, i - 1].astype(jnp.float32)
            s3y[n] = part.astype(jnp.bfloat16)
            copy_yx(n).start()

        def stage3(n):
            for i in range(1, depth):
                copy_xz(n, i).wait_recv()
            part = r3x[n, line].astype(jnp.float32)
            for i in range(1, depth):
                part = part + r4x[n, i - 1].astype(jnp.float32)
            fin[n, pl.ds(at16(core * H + Hy + xpos * Q), Q), :] = part.astype(jnp.bfloat16)
            copy_xx(n).start()
            copy_yx(n).wait_recv()
            fin[n, pl.ds(at16(core * H), Hy), :] = s3y[n] + r4y[n]

        def stage4(n):
            copy_xx(n).wait_recv()
            copy_back(n).start()

        def stage5(n):
            copy_back(n).wait_recv()
            write(n).start()

        stages = [stage0, stage1, stage2, stage3, stage4, stage5]
        for step in range(total + len(stages) - 1):
            for k in range(len(stages) - 1, -1, -1):
                if 0 <= step - k < total:
                    stages[k](step - k)
            yield True
        for n in range(total):
            copy_core(n).wait_send()
            copy_y(n).wait_send()
            copy_x(n).wait_send()
            copy_xy(n).wait_send()
            copy_yx(n).wait_send()
            copy_xx(n).wait_send()
            copy_back(n).wait_send()
            for i in range(1, depth):
                copy_yz(n, i).wait_send()
                copy_xz(n, i).wait_send()
            write(n).wait()
        yield True


class Total:
    def __init__(self, value, t):
        self.depth = t // 2
        rows, dma = value.shape[0], pltpu.SemaphoreType.DMA
        self.out_shape = [jax.ShapeDtypeStruct(value.shape, jnp.float32)]
        self.scratch = [
            pltpu.VMEM((self.depth, rows, LANES), jnp.float32),
            pltpu.VMEM((3, 2, rows, LANES), jnp.float32),
            dma((self.depth + 3,)),
            dma((self.depth + 3,)),
            dma((2,)),
        ]

    def steps(self, place, ins, outs, scratch):
        along, pair, send, recv, local = scratch
        depth = self.depth

        def z_copy(i):
            return remote(ins[0], along.at[place.line], send.at[i], recv.at[i], place.z_mate(i))

        def swap_copy(k):
            device = (place.y_mate, place.x_mate, place.sibling)[k]
            return remote(pair.at[k, 0], pair.at[k, 1], send.at[depth + k], recv.at[depth + k], device)

        own = pltpu.make_async_copy(ins[0], along.at[place.line], local.at[0])
        own.start()
        for i in range(1, depth):
            z_copy(i).start()
        yield True
        own.wait()
        for i in range(1, depth):
            landed(along.at[place.line_at(depth - i)], recv.at[i])
        total = along[0]
        for i in range(1, depth):
            total = total + along[i]
        for k in range(3):
            pair[k, 0] = total
            swap_copy(k).start()
            yield True
            swap_copy(k).wait_recv()
            total = pair[k, 0] + pair[k, 1]
        for i in range(1, depth):
            z_copy(i).wait_send()
        for k in range(3):
            swap_copy(k).wait_send()
        pair[0, 0] = total
        out = pltpu.make_async_copy(pair.at[0, 0], outs[0], local.at[1])
        out.start()
        out.wait()
        yield True


class Nothing:
    out_shape, scratch = [], []

    def steps(self, place, ins, outs, scratch):
        yield from ()


ANY = pl.BlockSpec(memory_space=pl.ANY)
VMEM = pl.BlockSpec(memory_space=pltpu.VMEM)


def communicate(body, out_shape, ins, in_specs, out_specs, scratch, cid):
    return pl.pallas_call(
        body,
        out_shape=out_shape,
        in_specs=in_specs,
        out_specs=out_specs,
        scratch_shapes=scratch,
        compiler_params=pltpu.CompilerParams(collective_id=cid, has_side_effects=True, vmem_limit_bytes=58 << 20),
    )(*ins)


def jobs_kernel(jobs, groups, t, cid):
    counts = [len(g) for g in groups]
    sizes = [len(j.scratch) for j in jobs]

    def body(*refs):
        place = Place(t)
        place.greet()
        refs = list(refs)
        ins = [[refs.pop(0) for _ in range(c)] for c in counts]
        outs = [[refs.pop(0) for _ in range(c)] for c in counts]
        scratch = [[refs.pop(0) for _ in range(c)] for c in sizes]
        running = [j.steps(place, i, o, s) for j, i, o, s in zip(jobs, ins, outs, scratch)]
        while running:
            running = [g for g in running if next(g, None) is not None]

    total = sum(counts)
    return communicate(
        body,
        [s for j in jobs for s in j.out_shape],
        [a for g in groups for a in g],
        [ANY] * total,
        [ANY] * total,
        [s for j in jobs for s in j.scratch],
        cid,
    )


def attend(tokens_qkv, t, causal, bq, job, job_ins, lead, each, cid):
    n, d = tokens_qkv[0].shape
    slots = Slots(t, n, d)
    pairs = slots.pairs
    held = jax.ShapeDtypeStruct((pairs, LEN, LANES), jnp.bfloat16)
    extra = len(job_ins)

    def body(*refs):
        qkv, refs = refs[:3], refs[3:]
        job_refs, refs = refs[:extra], refs[extra:]
        out, saved, lse, refs = refs[0], refs[1:5], refs[5], refs[6:]
        job_outs, refs = refs[:extra], refs[extra:]
        here, (hs, hr, ts, tr, keep), refs = refs[:4], refs[4:9], refs[9:]
        place = Place(t)
        place.greet()

        def main():
            move = ToHeads(place, slots, qkv, here[:3], hs, hr)
            back = ToTokens(place, slots, here[3:], [out], ts, tr)
            move.start()
            yield lead
            for slot in range(pairs):
                move.wait_slot(slot)
                for i in range(LEN // bq):
                    attend_block(i, bq, causal, *(r.at[slot] for r in here), lse.at[slot])
                    yield each
                back.start_slot(slot)
            copies = [pltpu.make_async_copy(h, s, keep.at[i]) for i, (h, s) in enumerate(zip(here, saved))]
            for c in copies:
                c.start()
            move.finish()
            yield -1
            back.finish()
            for c in copies:
                c.wait()

        weave(main(), job.steps(place, job_refs, job_outs, refs))

    out = communicate(
        body,
        [jax.ShapeDtypeStruct((n, d), jnp.bfloat16)]
        + [held] * 4
        + [jax.ShapeDtypeStruct((pairs, 8, LEN), jnp.float32)]
        + job.out_shape,
        [*tokens_qkv, *job_ins],
        [ANY] * (3 + extra),
        [ANY] * 5 + [VMEM] + [ANY] * extra,
        [pltpu.VMEM(held.shape, held.dtype)] * 4
        + reshard_sems(slots, 3, 1)
        + [pltpu.SemaphoreType.DMA((4,))]
        + job.scratch,
        cid,
    )
    return out[0], out[1:6], out[6:]


def attend_back(grad, saved, t, causal, bq, job, job_ins, lead, every, cid):
    n, d = grad.shape
    slots = Slots(t, n, d)
    pairs = slots.pairs
    held = pltpu.VMEM((pairs, LEN, LANES), jnp.bfloat16)
    extra = len(job_ins)

    def body(grad_ref, q, k, v, o, lse, *refs):
        job_refs, refs = refs[:extra], refs[extra:]
        outs, refs = refs[:3], refs[3:]
        job_outs, refs = refs[:extra], refs[extra:]
        (do, *made, kt, dk, dv, hs, hr, ts, tr), refs = refs[:11], refs[11:]
        place = Place(t)
        place.greet()

        def main():
            move = ToHeads(place, slots, [grad_ref], [do], hs, hr)
            back = ToTokens(place, slots, made, outs, ts, tr)
            move.start()
            yield lead
            count = 0
            for slot in range(pairs):
                move.wait_slot(slot)
                dk[...] = jnp.zeros_like(dk)
                dv[...] = jnp.zeros_like(dv)
                kt[...] = jnp.transpose(k[slot])
                for i in range(LEN // bq):
                    attend_back_block(
                        i,
                        bq,
                        causal,
                        *(r.at[slot] for r in (q, k, v, o, lse, do, made[0])),
                        kt,
                        dk,
                        dv,
                    )
                    count += 1
                    yield 1 if count % every == 0 else 0
                made[1][slot] = dk[...].astype(jnp.bfloat16)
                made[2][slot] = dv[...].astype(jnp.bfloat16)
                back.start_slot(slot)
            move.finish()
            yield -1
            back.finish()

        weave(main(), job.steps(place, job_refs, job_outs, refs))

    out = communicate(
        body,
        [jax.ShapeDtypeStruct((n, d), jnp.bfloat16)] * 3 + job.out_shape,
        [grad, *saved, *job_ins],
        [ANY] + [VMEM] * 5 + [ANY] * extra,
        [ANY] * (3 + extra),
        [held] * 4
        + [pltpu.VMEM((LANES, LEN), jnp.bfloat16)]
        + [pltpu.VMEM((LEN, LANES), jnp.float32)] * 2
        + reshard_sems(slots, 1, 3)
        + job.scratch,
        cid,
    )
    return out[:3], out[3:]


def cols_kernel(count, x_ref, w_ref, *outs):
    out = dot(x_ref[...], w_ref[0], NN)
    width = out.shape[1] // count
    for i, o_ref in enumerate(outs):
        o_ref[...] = out[:, i * width : (i + 1) * width].astype(o_ref.dtype)


def cols_product(x, weight, count, dtype=jnp.bfloat16):
    n, d = x.shape
    t, _, c = weight.shape
    width = c // count
    return pl.pallas_call(
        functools.partial(cols_kernel, count),
        grid=(t,),
        out_shape=[jax.ShapeDtypeStruct((n, t * width), dtype)] * count,
        in_specs=[
            pl.BlockSpec((n, d), lambda i: (0, 0)),
            pl.BlockSpec((1, d, c), lambda i: (i, 0, 0)),
        ],
        out_specs=[pl.BlockSpec((n, width), lambda i: (0, i))] * count,
        compiler_params=pltpu.CompilerParams(vmem_limit_bytes=48 << 20),
        cost_estimate=pl.CostEstimate(
            flops=2 * n * d * t * c, bytes_accessed=2 * (t * d * c + n * d + n * t * c), transcendentals=0
        ),
    )(x, weight)


def back_kernel(count, *refs):
    ys, w_ref, o_ref = refs[:count], refs[count], refs[count + 1]
    y = jnp.concatenate([y_ref[...] for y_ref in ys], 1) if count > 1 else ys[0][...]
    term = dot(y, w_ref[0], NT)

    @pl.when(pl.program_id(0) == 0)
    def _():
        o_ref[...] = term

    @pl.when(pl.program_id(0) != 0)
    def _():
        o_ref[...] += term


def back_product(ys, weight):
    count = len(ys)
    n = ys[0].shape[0]
    t, d, c = weight.shape
    width = c // count
    return pl.pallas_call(
        functools.partial(back_kernel, count),
        grid=(t,),
        out_shape=jax.ShapeDtypeStruct((n, d), jnp.float32),
        in_specs=[pl.BlockSpec((n, width), lambda i: (0, i))] * count
        + [pl.BlockSpec((1, d, c), lambda i: (i, 0, 0))],
        out_specs=pl.BlockSpec((n, d), lambda i: (0, 0)),
        compiler_params=pltpu.CompilerParams(vmem_limit_bytes=48 << 20),
        cost_estimate=pl.CostEstimate(
            flops=2 * n * d * t * c, bytes_accessed=2 * (t * d * c + 2 * n * d + n * t * c), transcendentals=0
        ),
    )(*ys, weight)


def by_side(grad, t):
    return jnp.swapaxes(grad.reshape(t // 2, 2, *grad.shape[1:]), 0, 1)


def cols_grad_kernel(count, x_ref, *refs):
    ys, o_ref, xt_ref = refs[:count], refs[count], refs[count + 1]

    @pl.when(pl.program_id(0) == 0)
    def _():
        xt_ref[...] = jnp.transpose(x_ref[...])

    y = jnp.concatenate([y_ref[...] for y_ref in ys], 1) if count > 1 else ys[0][...]
    out = dot(xt_ref[...], y, NN).astype(o_ref.dtype)
    d = out.shape[0]
    for j in range(out.shape[1] // LANES):
        o_ref[0, 0, j * d : j * d + d, :] = out[:, j * LANES : j * LANES + LANES]


def cols_grad(x, ys, t):
    count = len(ys)
    n, d = x.shape
    blocks = min(t, ys[0].shape[1] // LANES)
    width = ys[0].shape[1] // blocks
    c = width * count
    whole = blocks == t
    out = pl.pallas_call(
        functools.partial(cols_grad_kernel, count),
        grid=(blocks,),
        out_shape=jax.ShapeDtypeStruct(
            (2, t // 2, c // LANES * d, LANES) if whole else (blocks, 1, c // LANES * d, LANES), jnp.bfloat16
        ),
        in_specs=[pl.BlockSpec((n, d), lambda i: (0, 0))]
        + [pl.BlockSpec((n, width), lambda i: (0, i))] * count,
        out_specs=pl.BlockSpec(
            (1, 1, c // LANES * d, LANES), (lambda i: (i % 2, i // 2, 0, 0)) if whole else (lambda i: (i, 0, 0, 0))
        ),
        scratch_shapes=[pltpu.VMEM((d, n), jnp.bfloat16)],
        compiler_params=pltpu.CompilerParams(vmem_limit_bytes=48 << 20),
        cost_estimate=pl.CostEstimate(
            flops=2 * n * d * blocks * c, bytes_accessed=2 * (blocks * d * c + n * d + n * blocks * c), transcendentals=0
        ),
    )(x, *ys)
    if whole:
        return out
    m = t // blocks
    parts = out.reshape(blocks, count, d, m, LANES // m).transpose(0, 3, 1, 2, 4)
    return by_side(parts.reshape(t, count * d // m, LANES), t)


def cols_result(total, count, d, width):
    total = total.astype(jnp.float32)
    if width < LANES:
        return total.reshape(count, d, width).transpose(1, 0, 2).reshape(d, count * width)
    return total.reshape(-1, d, LANES).transpose(1, 0, 2).reshape(d, count * width)


def rows_grad_kernel(x_ref, y_ref, o_ref):
    out = dot(jnp.transpose(x_ref[...]), y_ref[...], NN).astype(o_ref.dtype)
    r = out.shape[0]
    for j in range(out.shape[1] // LANES):
        o_ref[0, 0, j * r : j * r + r, :] = out[:, j * LANES : j * LANES + LANES]


def rows_grad(x, y, t):
    n, d = y.shape
    blocks = min(t, x.shape[1] // LANES)
    r = x.shape[1] // blocks
    whole = blocks == t
    size = d // LANES * r
    out = pl.pallas_call(
        rows_grad_kernel,
        grid=(blocks,),
        out_shape=jax.ShapeDtypeStruct((2, t // 2, size, LANES) if whole else (blocks, 1, size, LANES), jnp.bfloat16),
        in_specs=[pl.BlockSpec((n, r), lambda i: (0, i)), pl.BlockSpec((n, d), lambda i: (0, 0))],
        out_specs=pl.BlockSpec(
            (1, 1, size, LANES), (lambda i: (i % 2, i // 2, 0, 0)) if whole else (lambda i: (i, 0, 0, 0))
        ),
        compiler_params=pltpu.CompilerParams(vmem_limit_bytes=48 << 20),
        cost_estimate=pl.CostEstimate(
            flops=2 * n * d * blocks * r, bytes_accessed=2 * (blocks * d * r + n * d + n * blocks * r), transcendentals=0
        ),
    )(x, y)
    if whole:
        return out
    m = t // blocks
    parts = out.reshape(blocks, d // LANES, m, r // m, LANES).transpose(0, 2, 1, 3, 4)
    return by_side(parts.reshape(t, size // m, LANES), t)


def rows_result(total, r, d):
    return total.astype(jnp.float32).reshape(d // LANES, r, LANES).transpose(1, 0, 2).reshape(r, d)


def gather_weight(weight):
    dp, t = lax.axis_size("dp"), lax.axis_size("tensor")
    rows = weight.shape[0] // dp
    share = lax.dynamic_slice_in_dim(weight, lax.axis_index("dp") * rows, rows, 0)
    whole = lax.all_gather(share, ("tensor", "dp"), axis=0, tiled=True)
    return whole.reshape(t, weight.shape[0], weight.shape[1])


def widen(weight, count):
    t, r, c = weight.shape
    width = c // count
    if width % LANES == 0:
        return weight
    m = LANES // width
    parts = weight.reshape(t // m, m, r, count, width).transpose(0, 2, 3, 1, 4)
    return parts.reshape(t // m, r, count * LANES)


def swap(value, axis, bit):
    size = lax.axis_size(axis)
    return lax.ppermute(value, axis, [(i, i ^ bit) for i in range(size)])


def settle(total):
    bit = 4
    while bit < lax.axis_size("dp"):
        total = total + swap(total, "dp", bit)
        bit *= 2
    return total


def normalize(rows_in, gain_row, shift_row):
    row_mean = jnp.mean(rows_in, axis=-1, keepdims=True)
    centered = rows_in - row_mean
    variance = jnp.mean(centered * centered, axis=-1, keepdims=True)
    return centered * lax.rsqrt(variance + norm_eps) * gain_row + shift_row


def gelu_tanh(values):
    return jax.nn.gelu(values, approximate=True)


def product(values, weight):
    return jnp.dot(values, weight, preferred_element_type=jnp.float32)


def per_device(
    tokens,
    memory,
    self_qkv,
    self_out,
    cross_q,
    cross_kv,
    cross_out,
    hidden_weight,
    hidden_bias,
    output_weight,
    output_bias,
    norm_gain,
    norm_shift,
    grad_output,
):
    low = jnp.bfloat16
    t = lax.axis_size("tensor")
    n, d = tokens.shape
    size = LEN * 8 // t
    w_hid = gather_weight(hidden_weight)
    w_out = gather_weight(output_weight).reshape(-1, d)
    units = hidden_bias.shape[0]
    bias_block = jnp.pad(hidden_bias, (0, 64 * LANES - units)).reshape(64, LANES)
    first = [self_qkv.reshape(d, -1), bias_block]
    w_qkv, bias_all = jobs_kernel([Gather(first, t)], [first], t, 0)
    w_qkv = widen(w_qkv, 3)
    bias_all = bias_all.reshape(t, -1)[:, :units].reshape(-1)

    qkv = cols_product(tokens, w_qkv, 3)
    second = [self_out, cross_q, cross_kv.reshape(d, -1), cross_out]
    self_heads, self_saved, (w_so, w_cq, w_kv, w_co) = attend(
        qkv, t, True, 512, Gather(second, t), second, 4, 1, 1
    )
    w_cq, w_kv = widen(w_cq, 1), widen(w_kv, 2)
    w_so, w_co = w_so.reshape(d, d), w_co.reshape(d, d)
    branch_one = product(self_heads, w_so)
    normed_one, pull_one = jax.vjp(
        normalize, residual_alpha * tokens.astype(jnp.float32) + branch_one, norm_gain[0], norm_shift[0]
    )
    normed_one_low = normed_one.astype(low)
    kv = cols_product(memory, w_kv, 2)
    cq = cols_product(normed_one_low, w_cq, 1)
    cross_heads, cross_saved, _ = attend([*cq, *kv], t, False, 512, Nothing(), [], 0, 0, 2)
    branch_two = product(cross_heads, w_co)
    normed_two, pull_two = jax.vjp(
        normalize, residual_alpha * normed_one + branch_two, norm_gain[1], norm_shift[1]
    )
    normed_two_low = normed_two.astype(low)
    (hidden_low,) = cols_product(normed_two_low, w_hid, 1, jnp.float32)
    hidden_pre = hidden_low + bias_all
    activated, gelu_pull = jax.vjp(gelu_tanh, hidden_pre)
    activated_low = activated.astype(low)
    branch_three = product(activated_low, w_out)
    layer_out, pull_three = jax.vjp(
        normalize, residual_alpha * normed_two + branch_three + output_bias, norm_gain[2], norm_shift[2]
    )
    grad_three, gain_three, shift_three = pull_three(grad_output.astype(jnp.float32))
    bias_out_grad = jnp.sum(grad_three, axis=0)
    grad_three_low = grad_three.astype(low)
    out_weight_part = rows_grad(activated_low, grad_three_low, t)
    grad_act = lax.dot_general(grad_three_low, w_out, NT, preferred_element_type=jnp.float32)
    grad_hidden = gelu_pull(grad_act)[0].astype(low)
    hidden_bias_grad = jnp.sum(grad_hidden, axis=0, dtype=jnp.float32)
    hidden_weight_part = cols_grad(normed_two_low, [grad_hidden], t)
    grad_two, gain_two, shift_two = pull_two(
        residual_alpha * grad_three + back_product([grad_hidden], w_hid)
    )
    grad_two_low = grad_two.astype(low)
    cross_out_part = rows_grad(cross_heads, grad_two_low, t)
    grad_co = lax.dot_general(grad_two_low, w_co, NT, preferred_element_type=jnp.float32).astype(low)
    ff_parts = [out_weight_part, hidden_weight_part]
    (g_cq, g_ck, g_cv), (out_weight_grad, hidden_weight_grad) = attend_back(
        grad_co, cross_saved, t, False, 256, Reduce(ff_parts, t, size), ff_parts, 2, 2, 3
    )
    cross_q_part = cols_grad(normed_one_low, [g_cq], t)
    cross_kv_part = cols_grad(memory, [g_ck, g_cv], t)
    grad_one, gain_one, shift_one = pull_one(residual_alpha * grad_two + back_product([g_cq], w_cq))
    grad_one_low = grad_one.astype(low)
    self_out_part = rows_grad(self_heads, grad_one_low, t)
    grad_so = lax.dot_general(grad_one_low, w_so, NT, preferred_element_type=jnp.float32).astype(low)
    parts = [cross_out_part, cross_q_part, cross_kv_part, self_out_part]
    g_qkv, (cross_out_grad, cross_q_grad, cross_kv_grad, self_out_grad) = attend_back(
        grad_so, self_saved, t, True, 256, Reduce(parts, t, size), parts, 2, 2, 4
    )
    self_qkv_part = cols_grad(tokens, g_qkv, t)
    small = jnp.concatenate(
        [gain_one, gain_two, gain_three, shift_one, shift_two, shift_three, bias_out_grad, hidden_bias_grad]
    ).reshape(-1, LANES)
    self_qkv_grad, small = jobs_kernel(
        [Reduce([self_qkv_part], t, size), Total(small, t)], [[self_qkv_part], [small]], t, 5
    )
    small = settle(small).reshape(-1)
    gain_total, shift_total = small[: 3 * d].reshape(3, d), small[3 * d : 6 * d].reshape(3, d)
    bias_total = small[6 * d : 7 * d]
    hidden_bias_total = lax.dynamic_slice_in_dim(small, 7 * d + lax.axis_index("tensor") * units, units, 0)
    out_weight_grad = rows_result(settle(out_weight_grad), output_weight.shape[0], d)
    hidden_weight_grad = cols_result(settle(hidden_weight_grad), 1, d, hidden_weight.shape[1])
    cross_out_grad = rows_result(settle(cross_out_grad), cross_out.shape[0], d)
    cross_q_grad = cols_result(settle(cross_q_grad), 1, d, cross_q.shape[1])
    cross_kv_grad = cols_result(settle(cross_kv_grad), 2, d, cross_kv.shape[2]).reshape(cross_kv.shape)
    self_out_grad = rows_result(settle(self_out_grad), self_out.shape[0], d)
    self_qkv_grad = cols_result(settle(self_qkv_grad), 3, d, self_qkv.shape[2]).reshape(self_qkv.shape)
    grad_memory = back_product([g_ck, g_cv], w_kv)
    grad_tokens = residual_alpha * grad_one + back_product(g_qkv, w_qkv)
    return (
        layer_out.astype(low),
        grad_tokens,
        grad_memory,
        self_qkv_grad,
        self_out_grad,
        cross_q_grad,
        cross_kv_grad,
        cross_out_grad,
        hidden_weight_grad,
        hidden_bias_total,
        out_weight_grad,
        bias_total,
        gain_total,
        shift_total,
    )


def solution(mesh):
    return jax.shard_map(
        per_device,
        mesh=mesh,
        in_specs=(
            P(("dp", "tensor"), None),
            P(("dp", "tensor"), None),
            P(None, None, "tensor"),
            P("tensor", None),
            P(None, "tensor"),
            P(None, None, "tensor"),
            P("tensor", None),
            P(None, "tensor"),
            P("tensor"),
            P("tensor", None),
            P(),
            P(),
            P(),
            P(("dp", "tensor"), None),
        ),
        out_specs=(
            P(("dp", "tensor"), None),
            P(("dp", "tensor"), None),
            P(("dp", "tensor"), None),
            P(None, None, "tensor"),
            P("tensor", None),
            P(None, "tensor"),
            P(None, None, "tensor"),
            P("tensor", None),
            P(None, "tensor"),
            P("tensor"),
            P("tensor", None),
            P(),
            P(),
            P(),
        ),
        check_vma=False,
    )
```

```python
import functools
import math

import jax
import jax.numpy as jnp
from jax import lax
from jax.experimental import pallas as pl
from jax.experimental.pallas import tpu as pltpu
from jax.sharding import PartitionSpec as P

MESH = pl.DeviceIdType.MESH
DH = 64
LANES = 128
LEN = 1024

residual_alpha = 300.0**0.25
norm_eps = 1e-05


def loop(lo, hi, body):
    def step(i, _):
        body(i)
        return 0

    lax.fori_loop(lo, hi, step, 0)


def weave(main, back):
    for steps in main:
        while steps != 0 and next(back, None) is not None:
            steps -= 1
    for _ in back:
        pass


class Place:
    def __init__(self, t):
        self.t, self.depth = t, t // 2
        self.d, self.me = lax.axis_index("dp"), lax.axis_index("tensor")
        self.core, self.xpos = self.d % 2, (self.d // 2) % 2
        self.line, self.side = self.me // 2, self.me % 2
        self.y_mate = {"tensor": 2 * self.line + 1 - self.side}
        self.x_mate = {"dp": self.d + 2 - 4 * self.xpos}
        self.sibling = {"dp": self.d + 1 - 2 * self.core}

    def line_at(self, i):
        return lax.rem(self.line + i, self.depth)

    def z_mate(self, i):
        return {"tensor": 2 * self.line_at(i) + self.side}

    def greet(self):
        barrier = pltpu.get_barrier_semaphore()
        peers = [{"tensor": lax.rem(self.me + i, self.t)} for i in range(1, self.t)]
        for p in peers + [self.x_mate, self.sibling]:
            pl.semaphore_signal(barrier, inc=1, device_id=p, device_id_type=MESH)
        pl.semaphore_wait(barrier, self.t + 1)


def remote(src, dst, send, recv, device):
    return pltpu.make_async_remote_copy(src, dst, send, recv, device_id=device, device_id_type=MESH)


def landed(ref, sem):
    pltpu.make_async_copy(ref, ref, sem).wait()


def at16(v):
    return pl.multiple_of(v, 16)


def rows_at(start, count):
    return pl.ds(pl.multiple_of(start, count), count)


class Slots:
    def __init__(self, t, n, d):
        self.block = math.gcd(n, LEN)
        self.blocks = n // self.block
        self.per_seq = LEN // self.block
        self.wide = d // LANES
        self.total = n * t // LEN * self.wide
        self.pairs = -(-self.total // t)
        self.units = self.blocks * self.wide
        self.lands = self.pairs * self.per_seq


class ToHeads:
    def __init__(self, place, slots, ins, outs, send, recv):
        self.place, self.slots, self.ins, self.outs, self.send, self.recv = place, slots, ins, outs, send, recv

    def unit(self, a, u):
        s = self.slots
        j, p = u // s.wide, u % s.wide
        g = self.place.me * s.blocks + j
        q = (g // s.per_seq) * s.wide + p
        dst, slot, k = q // s.pairs, q % s.pairs, g % s.per_seq
        src = self.ins[a].at[rows_at(j * s.block, s.block), rows_at(p * LANES, LANES)]
        to = self.outs[a].at[slot, rows_at(k * s.block, s.block), :]
        return dst, src, to, self.send.at[a, u], self.recv.at[a, slot * s.per_seq + k]

    def start(self):
        for a in range(len(self.ins)):

            def one(u):
                dst, src, to, ss, rs = self.unit(a, u)

                @pl.when(dst == self.place.me)
                def _():
                    pltpu.make_async_copy(src, to, rs).start()

                @pl.when(dst != self.place.me)
                def _():
                    remote(src, to, ss, rs, {"tensor": dst}).start()

            loop(0, self.slots.units, one)

    def wait_slot(self, slot):
        s = self.slots

        @pl.when(self.place.me * s.pairs + slot < s.total)
        def _():
            for a in range(len(self.ins)):
                loop(
                    0,
                    s.per_seq,
                    lambda k: landed(
                        self.outs[a].at[slot, rows_at(k * s.block, s.block), :], self.recv.at[a, slot * s.per_seq + k]
                    ),
                )

    def finish(self):
        for a in range(len(self.ins)):

            def one(u):
                dst, src, to, ss, rs = self.unit(a, u)

                @pl.when(dst != self.place.me)
                def _():
                    remote(src, to, ss, rs, {"tensor": dst}).wait_send()

            loop(0, self.slots.units, one)


class ToTokens:
    def __init__(self, place, slots, ins, outs, send, recv):
        self.place, self.slots, self.ins, self.outs, self.send, self.recv = place, slots, ins, outs, send, recv

    def unit(self, a, slot, k):
        s = self.slots
        q = self.place.me * s.pairs + slot
        g = (q // s.wide) * s.per_seq + k
        dst, j, p = g // s.blocks, g % s.blocks, q % s.wide
        src = self.ins[a].at[slot, rows_at(k * s.block, s.block), :]
        to = self.outs[a].at[rows_at(j * s.block, s.block), rows_at(p * LANES, LANES)]
        return q < s.total, dst, src, to, self.send.at[a, slot * s.per_seq + k], self.recv.at[a, j * s.wide + p]

    def start_slot(self, slot):
        for a in range(len(self.ins)):

            def one(k):
                real, dst, src, to, ss, rs = self.unit(a, slot, k)

                @pl.when(real & (dst == self.place.me))
                def _():
                    pltpu.make_async_copy(src, to, rs).start()

                @pl.when(real & (dst != self.place.me))
                def _():
                    remote(src, to, ss, rs, {"tensor": dst}).start()

            loop(0, self.slots.per_seq, one)

    def finish(self):
        s = self.slots
        for a in range(len(self.ins)):

            def sent(u):
                real, dst, src, to, ss, rs = self.unit(a, u // s.per_seq, u % s.per_seq)

                @pl.when(real & (dst != self.place.me))
                def _():
                    remote(src, to, ss, rs, {"tensor": dst}).wait_send()

            loop(0, s.lands, sent)

            def got(r):
                j, p = r // s.wide, r % s.wide
                landed(
                    self.outs[a].at[rows_at(j * s.block, s.block), rows_at(p * LANES, LANES)], self.recv.at[a, r]
                )

            loop(0, s.units, got)


def reshard_sems(slots, heads, tokens):
    dma = pltpu.SemaphoreType.DMA
    return [dma((heads, slots.units)), dma((heads, slots.lands)), dma((tokens, slots.lands)), dma((tokens, slots.units))]


NT = (((1,), (1,)), ((), ()))
NN = (((1,), (0,)), ((), ()))
LOG2E = math.log2(math.e)


def dot(a, b, dims):
    return lax.dot_general(a, b, dims, preferred_element_type=jnp.float32)


def lane_half(shape, h):
    return (lax.broadcasted_iota(jnp.int32, shape, len(shape) - 1) // DH) == h


def attend_block(i, bq, causal, q_ref, k_ref, v_ref, o_ref, lse_ref):
    keys = bq * (i + 1) if causal else LEN
    rows = pl.ds(i * bq, bq)
    q = q_ref[rows, :] * jnp.bfloat16(0.125)
    k = k_ref[:keys, :]
    v = v_ref[:keys, :]
    total = None
    for h in (0, 1):
        qh = jnp.where(lane_half(q.shape, h), q, jnp.bfloat16(0))
        s = dot(qh, k, NT)
        if causal:
            tail = s[:, keys - bq :]
            r = lax.broadcasted_iota(jnp.int32, tail.shape, 0)
            c = lax.broadcasted_iota(jnp.int32, tail.shape, 1)
            tail = jnp.where(c <= r, tail, -1e30)
            s = tail if keys == bq else jnp.concatenate([s[:, : keys - bq], tail], 1)
        m = jnp.max(s, axis=-1, keepdims=True)
        e = jnp.exp2((s - m) * LOG2E)
        total_e = jnp.sum(e, axis=-1, keepdims=True)
        o = dot(e.astype(jnp.bfloat16), v, NN) / total_e
        total = o if h == 0 else jnp.where(lane_half(o.shape, 0), total, o)
        lse = m * LOG2E + jnp.log2(total_e)
        lse_ref[h : h + 1, rows] = jnp.transpose(jnp.broadcast_to(lse, (bq, LANES)))[0:1]
    o_ref[rows, :] = total.astype(jnp.bfloat16)


def attend_back_block(i, bq, causal, q_ref, k_ref, v_ref, o_ref, lse_ref, do_ref, dq_ref, kt_ref, dk_ref, dv_ref):
    keys = bq * (i + 1) if causal else LEN
    rows = pl.ds(i * bq, bq)
    q = q_ref[rows, :] * jnp.bfloat16(0.125)
    do = do_ref[rows, :]
    prod = jnp.transpose(do.astype(jnp.float32) * o_ref[rows, :].astype(jnp.float32))
    k = k_ref[:keys, :]
    v = v_ref[:keys, :]
    dqt = []
    for h in (0, 1):
        mask = lane_half(q.shape, h)
        qh = jnp.where(mask, q, jnp.bfloat16(0))
        doh = jnp.where(mask, do, jnp.bfloat16(0))
        delta = jnp.sum(prod[DH * h : DH * h + DH], axis=0, keepdims=True)
        p = jnp.exp2(dot(k, qh, NT) * LOG2E - lse_ref[h : h + 1, rows])
        if causal:
            tail = p[keys - bq :, :]
            r = lax.broadcasted_iota(jnp.int32, tail.shape, 1)
            c = lax.broadcasted_iota(jnp.int32, tail.shape, 0)
            tail = jnp.where(c <= r, tail, 0.0)
            p = tail if keys == bq else jnp.concatenate([p[: keys - bq], tail], 0)
        ds = (p * (dot(v, doh, NT) - delta)).astype(jnp.bfloat16)
        dv_ref[:keys, :] += dot(p.astype(jnp.bfloat16), doh, NN)
        dk_ref[:keys, :] += dot(ds, qh, NN)
        dqt.append(dot(kt_ref[DH * h : DH * h + DH, :keys], ds, NN))
    dq_ref[rows, :] = (jnp.transpose(jnp.concatenate(dqt, 0)) * 0.125).astype(jnp.bfloat16)


class Gather:
    def __init__(self, weights, t, share, size=1 << 17):
        self.t, self.depth, self.share = t, t // 2, share
        self.ins, self.specs = list(weights), [ANY] * len(weights)
        self.shapes = [w.shape for w in weights]
        self.pieces = []
        for w, (r, c) in enumerate(self.shapes):
            rows = r
            while rows % 64 == 0 and rows * c > size:
                rows //= 2
            self.pieces += [(w, at, rows) for at in range(0, r, rows)]
        m, dma = len(self.pieces), pltpu.SemaphoreType.DMA
        self.out_shape = [jax.ShapeDtypeStruct((t,) + w.shape, w.dtype) for w in weights]
        self.scratch = [
            dma((m, self.depth)),
            dma((m, self.depth)),
            dma((m, t)),
            dma((m, t, 2)),
            dma((m, t)),
            dma((m, t)),
            dma((m, t, 2)),
            dma((len(weights),)),
        ]

    def x_rows(self, n):
        half = self.pieces[n][2] // 2
        return min(int(half * self.share / 16 + 0.5) * 16, half // 32 * 16)

    def rows_of(self, n, kind, core):
        _, at, rows = self.pieces[n]
        half = rows // 2
        a = self.x_rows(n)
        start, xpos = at + core * half, self.place.xpos
        if kind == "plane":
            return pl.ds(at16(start + xpos * a), half - a)
        if kind == "x_out":
            return pl.ds(at16(start + xpos * (half - a)), a)
        return pl.ds(at16(start + (1 - xpos) * (half - a)), a)

    def steps(self, place, ins, outs, scratch):
        z_send, y_send, x_send, d_send, plane_recv, x_recv, d_recv, own_sem = scratch
        self.place = place
        me, depth, t, pieces = place.me, self.depth, self.t, self.pieces

        def has_x(n):
            return self.x_rows(n) > 0

        def rows_of(n, kind, core=place.core):
            return self.rows_of(n, kind, core)

        def part(n, block, kind, core=place.core):
            return outs[pieces[n][0]].at[block, rows_of(n, kind, core), :]

        def column(i, side):
            return 2 * place.line_at(depth - i) + side

        def own(n):
            return ins[pieces[n][0]].at[rows_of(n, "plane"), :]

        def z_copy(n, i):
            return remote(own(n), part(n, me, "plane"), z_send.at[n, i], plane_recv.at[n, me], place.z_mate(i))

        def y_own(n):
            return remote(own(n), part(n, me, "plane"), y_send.at[n, place.line], plane_recv.at[n, me], place.y_mate)

        def y_copy(n, block):
            ref = part(n, block, "plane")
            return remote(ref, ref, y_send.at[n, block // 2], plane_recv.at[n, block], place.y_mate)

        def x_copy(n, block):
            ref = part(n, block, "x_out")
            return remote(ref, ref, x_send.at[n, block], x_recv.at[n, block], place.x_mate)

        def d_copy(n, block, k):
            ref = part(n, block, ("plane", "x_in")[k])
            return remote(ref, ref, d_send.at[n, block, k], d_recv.at[n, block, k], place.sibling)

        def own_copy(w):
            return pltpu.make_async_copy(ins[w], outs[w].at[me], own_sem.at[w])

        total = len(pieces)

        def launch(n):
            if n < total:
                for i in range(1, depth):
                    z_copy(n, i).start()
                y_own(n).start()

        launch(0)
        for w in range(len(ins)):
            own_copy(w).start()
        yield True
        for step in range(total + 2):
            launch(step + 1)
            n = step
            if n < total:

                def z_stage(i):
                    block = column(i, place.side)
                    landed(part(n, block, "plane"), plane_recv.at[n, block])
                    y_copy(n, block).start()
                    if has_x(n):
                        x_copy(n, block).start()
                    d_copy(n, block, 0).start()

                loop(1, depth, z_stage)
            n1 = step - 1
            if 0 <= n1 < total:

                def y_stage(i):
                    block = column(i, 1 - place.side)
                    landed(part(n1, block, "plane"), plane_recv.at[n1, block])
                    if has_x(n1):
                        x_copy(n1, block).start()
                    d_copy(n1, block, 0).start()

                loop(0, depth, y_stage)
            n2 = step - 2
            if 0 <= n2 < total and has_x(n2):

                def x_stage(i):
                    block = lax.rem(me + i, t)
                    landed(part(n2, block, "x_in"), x_recv.at[n2, block])
                    d_copy(n2, block, 1).start()

                loop(1, t, x_stage)
            yield True
        for w in range(len(ins)):
            own_copy(w).wait()
        for n in range(total):
            loop(1, depth, lambda i: z_copy(n, i).wait_send())
            y_own(n).wait_send()
            loop(1, depth, lambda i: y_copy(n, column(i, place.side)).wait_send())

            def finish(i):
                block = lax.rem(me + i, t)
                for k in range(2 if has_x(n) else 1):
                    d_copy(n, block, k).wait_send()
                    landed(part(n, block, ("plane", "x_in")[k], 1 - place.core), d_recv.at[n, block, k])
                if has_x(n):
                    x_copy(n, block).wait_send()

            loop(1, t, finish)
        yield True


class Weight:
    def __init__(self, x, ys, by_cols, t):
        self.arrays, self.by_cols = [x, *ys], by_cols
        n, m = x.shape
        wide = ys[0].shape[1]
        if by_cols:
            self.height, self.width = m, wide // t
            self.rows = len(ys) * m * self.width // LANES
        else:
            self.height, self.width = m // t, wide
            self.rows = m // t * wide // LANES

    def term(self, xt, ys, at, half, t, which):
        high = self.height
        if self.by_cols and self.width < LANES:
            panel, row = at // (high // 2), at % (high // 2) + which * half
            y = ys[panel][:, rows_at(t // 2 * LANES, LANES)]
            first, second = (dot(xt[rows_at(r, half), :], y, NN) for r in (row, row + high // 2))
            odd = t % 2 == 1
            first = jnp.where(odd, pltpu.roll(first, DH, 1), first)
            second = jnp.where(odd, second, pltpu.roll(second, DH, 1))
            return [jnp.where(lane_half(first.shape, 0), first, second)]
        if self.by_cols:
            panel, row = at // high, at % high
            per = self.width // LANES
            y, col = ys[panel // per], t * self.width + panel % per * LANES
            return [dot(xt[rows_at(row + which * half, half), :], y[:, rows_at(col, LANES)], NN)]
        panels = half // high
        cols = rows_at((at // high + which * panels) * LANES, panels * LANES)
        out = dot(xt[rows_at(t * high, high), :], ys[0][:, cols], NN)
        return [out[:, i * LANES : i * LANES + LANES] for i in range(panels)]


class Reduce:
    def __init__(self, weights, t, size, y_first):
        self.t, self.depth, self.size, self.weights = t, t // 2, size, weights
        self.y_rows = int(size // 2 * y_first) // 32 * 32
        self.ins = [a for w in weights for a in w.arrays]
        self.specs = [VMEM] * len(self.ins)
        self.pieces = [(w, at) for w, g in enumerate(weights) for at in range(0, g.rows, size)]
        m, depth, dma = len(self.pieces), self.depth, pltpu.SemaphoreType.DMA
        H, Hy, Q = size // 2, self.y_rows, (size // 2 - self.y_rows) // 2

        def buf(*shape):
            return pltpu.VMEM(shape + (LANES,), jnp.bfloat16)

        self.out_shape = [jax.ShapeDtypeStruct((g.rows, LANES), jnp.bfloat16) for g in weights]
        self.scratch = [
            buf(2, 2, depth, H),
            buf(2, 2, depth, H),
            buf(m, 2, depth, H),
            buf(m, depth, Hy),
            buf(m, 2, depth, Q),
            buf(m, depth - 1, Hy),
            buf(m, depth, Q),
            buf(m, Hy),
            buf(m, Hy),
            buf(m, depth - 1, Q),
            buf(m, size),
            dma((m, 5 + 2 * depth)),
            dma((m, 5 + 2 * depth)),
            dma((m,)),
        ] + [pltpu.VMEM(w.arrays[0].shape[::-1], jnp.bfloat16) for w in weights]

    def steps(self, place, ins, outs, scratch):
        away, own, r1, r2y, r2x, r3y, r3x, s3y, r4y, r4x, fin, send, recv, store = scratch[:14]
        size, depth, pieces, t = self.size, self.depth, self.pieces, self.t
        H, Hy, Q = size // 2, self.y_rows, (size // 2 - self.y_rows) // 2
        core, xpos, line, side = place.core, place.xpos, place.line, place.side
        turned, ins, arrays = scratch[14:], list(ins), []
        for w in self.weights:
            arrays.append([ins.pop(0) for _ in w.arrays])

        def move(src, dst, n, k, device):
            return remote(src, dst, send.at[n, k], recv.at[n, k], device)

        def copy_core(n):
            return move(away.at[n % 2], r1.at[n], n, 0, place.sibling)

        def copy_y(n):
            return move(r1.at[n, 1 - side, :, pl.ds(0, Hy), :], r2y.at[n], n, 1, place.y_mate)

        def copy_x(n):
            return move(r1.at[n, :, :, pl.ds(at16(Hy + (1 - xpos) * Q), Q), :], r2x.at[n], n, 2, place.x_mate)

        def copy_yz(n, i):
            return move(r2y.at[n, place.line_at(i)], r3y.at[n, i - 1], n, 2 + i, place.z_mate(i))

        def copy_xy(n):
            return move(r2x.at[n, 1 - side], r3x.at[n], n, 2 + depth, place.y_mate)

        def copy_yx(n):
            return move(s3y.at[n], r4y.at[n], n, 3 + depth, place.x_mate)

        def copy_xz(n, i):
            return move(r3x.at[n, place.line_at(i)], r4x.at[n, i - 1], n, 3 + depth + i, place.z_mate(i))

        def copy_xx(n):
            ref = fin.at[n, pl.ds(at16(core * H + Hy + xpos * Q), Q), :]
            return move(ref, ref, n, 3 + 2 * depth, place.x_mate)

        def copy_back(n):
            ref = fin.at[n, pl.ds(at16(core * H), H), :]
            return move(ref, ref, n, 4 + 2 * depth, place.sibling)

        def write(n):
            w, at = pieces[n]
            return pltpu.make_async_copy(fin.at[n], outs[w].at[pl.ds(at, size), :], store.at[n])

        def make(n):
            w, at = pieces[n]
            weight, (x, *ys) = self.weights[w], arrays[w]
            if n == 0 or pieces[n - 1][0] != w:
                turned[w][...] = jnp.transpose(x[...])
            if n >= 2:
                copy_core(n - 2).wait_send()
            for which, into in ((1 - core, away), (core, own)):

                def block(i):
                    parts = weight.term(turned[w], ys, at, H, i, which)
                    high = parts[0].shape[0]
                    for j, part in enumerate(parts):
                        into[n % 2, i % 2, i // 2, j * high : j * high + high, :] = part.astype(jnp.bfloat16)

                loop(0, t, block)
                if into is away:
                    copy_core(n).start()

        def stage0(n):
            copy_core(n).wait_recv()

            def add(i):
                a, b = i // depth, i % depth
                r1[n, a, b] = r1[n, a, b] + own[n % 2, a, b]

            loop(0, 2 * depth, add)
            if Hy:
                copy_y(n).start()
            copy_x(n).start()

        def stage1(n):
            if Hy:
                copy_y(n).wait_recv()

                def add(i):
                    r2y[n, i] = r2y[n, i] + r1[n, side, i, 0:Hy, :]

                loop(0, depth, add)
                for i in range(1, depth):
                    copy_yz(n, i).start()
            copy_x(n).wait_recv()

            def addx(i):
                a, b = i // depth, i % depth
                r2x[n, a, b] = r2x[n, a, b] + r1[n, a, b, pl.ds(at16(Hy + xpos * Q), Q), :]

            loop(0, 2 * depth, addx)
            copy_xy(n).start()

        def stage2(n):
            copy_xy(n).wait_recv()

            def add(i):
                r3x[n, i] = r3x[n, i] + r2x[n, side, i]

            loop(0, depth, add)
            for i in range(1, depth):
                copy_xz(n, i).start()
            if Hy:
                for i in range(1, depth):
                    copy_yz(n, i).wait_recv()
                part = r2y[n, line].astype(jnp.float32)
                for i in range(1, depth):
                    part = part + r3y[n, i - 1].astype(jnp.float32)
                s3y[n] = part.astype(jnp.bfloat16)
                copy_yx(n).start()

        def stage3(n):
            for i in range(1, depth):
                copy_xz(n, i).wait_recv()
            part = r3x[n, line].astype(jnp.float32)
            for i in range(1, depth):
                part = part + r4x[n, i - 1].astype(jnp.float32)
            fin[n, pl.ds(at16(core * H + Hy + xpos * Q), Q), :] = part.astype(jnp.bfloat16)
            copy_xx(n).start()
            if Hy:
                copy_yx(n).wait_recv()
                fin[n, pl.ds(at16(core * H), Hy), :] = s3y[n] + r4y[n]

        def stage4(n):
            copy_xx(n).wait_recv()
            copy_back(n).start()

        def stage5(n):
            copy_back(n).wait_recv()
            write(n).start()

        total = len(pieces)
        make(0)
        yield True
        stages = [stage0, stage1, stage2, stage3, stage4, stage5]
        for step in range(total + len(stages) - 1):
            for k in range(len(stages) - 1, -1, -1):
                if 0 <= step - k < total:
                    stages[k](step - k)
            if step + 1 < total:
                make(step + 1)
            yield True
        for n in range(total):
            if n >= total - 2:
                copy_core(n).wait_send()
            copy_x(n).wait_send()
            copy_xy(n).wait_send()
            copy_xx(n).wait_send()
            copy_back(n).wait_send()
            for i in range(1, depth):
                copy_xz(n, i).wait_send()
            if Hy:
                copy_y(n).wait_send()
                copy_yx(n).wait_send()
                for i in range(1, depth):
                    copy_yz(n, i).wait_send()
            write(n).wait()
        yield True


class Back:
    def __init__(self, ys, weight, rest=None, factor=1.0):
        self.count, self.has_rest, self.factor = len(ys), rest is not None, factor
        self.ins = [*ys, weight] + ([rest] if self.has_rest else [])
        self.specs = [VMEM] * self.count + [ANY] + [VMEM] * self.has_rest
        n, (t, d, c) = ys[0].shape[0], weight.shape
        self.blocks = t
        self.out_shape = [jax.ShapeDtypeStruct((n, d), jnp.float32)]
        self.scratch = [
            pltpu.VMEM((2, d, c), jnp.bfloat16),
            pltpu.VMEM((n, d), jnp.float32),
            pltpu.SemaphoreType.DMA((3,)),
        ]

    def steps(self, place, ins, outs, scratch):
        held, total, sem = scratch
        ys, weight = ins[: self.count], ins[self.count]
        width = held.shape[2] // self.count

        def load(i):
            return pltpu.make_async_copy(weight.at[i], held.at[i % 2], sem.at[i % 2])

        load(0).start()
        for i in range(self.blocks):
            load(i).wait()
            if i + 1 < self.blocks:
                load(i + 1).start()
            y = [y_ref[:, i * width : i * width + width] for y_ref in ys]
            term = dot(jnp.concatenate(y, 1) if len(y) > 1 else y[0], held[i % 2], NT)
            if i:
                total[...] += term
            else:
                total[...] = term + self.factor * ins[-1][...] if self.has_rest else term
            yield True
        out = pltpu.make_async_copy(total, outs[0], sem.at[2])
        out.start()
        out.wait()
        yield True


class Total:
    def __init__(self, value, t):
        self.depth = t // 2
        rows, dma = value.shape[0], pltpu.SemaphoreType.DMA
        self.ins, self.specs = [value], [ANY]
        self.out_shape = [jax.ShapeDtypeStruct(value.shape, jnp.float32)]
        self.scratch = [
            pltpu.VMEM((self.depth, rows, LANES), jnp.float32),
            pltpu.VMEM((3, 2, rows, LANES), jnp.float32),
            dma((self.depth + 3,)),
            dma((self.depth + 3,)),
            dma((2,)),
        ]

    def steps(self, place, ins, outs, scratch):
        along, pair, send, recv, local = scratch
        depth = self.depth

        def z_copy(i):
            return remote(ins[0], along.at[place.line], send.at[i], recv.at[i], place.z_mate(i))

        def swap_copy(k):
            device = (place.y_mate, place.x_mate, place.sibling)[k]
            return remote(pair.at[k, 0], pair.at[k, 1], send.at[depth + k], recv.at[depth + k], device)

        own = pltpu.make_async_copy(ins[0], along.at[place.line], local.at[0])
        own.start()
        for i in range(1, depth):
            z_copy(i).start()
        yield True
        own.wait()
        for i in range(1, depth):
            landed(along.at[place.line_at(depth - i)], recv.at[i])
        total = along[0]
        for i in range(1, depth):
            total = total + along[i]
        for k in range(3):
            pair[k, 0] = total
            swap_copy(k).start()
            yield True
            swap_copy(k).wait_recv()
            total = pair[k, 0] + pair[k, 1]
        for i in range(1, depth):
            z_copy(i).wait_send()
        for k in range(3):
            swap_copy(k).wait_send()
        pair[0, 0] = total
        out = pltpu.make_async_copy(pair.at[0, 0], outs[0], local.at[1])
        out.start()
        out.wait()
        yield True


class Nothing:
    ins, specs, out_shape, scratch = [], [], [], []

    def steps(self, place, ins, outs, scratch):
        yield from ()


ANY = pl.BlockSpec(memory_space=pl.ANY)
VMEM = pl.BlockSpec(memory_space=pltpu.VMEM)


def communicate(body, out_shape, ins, in_specs, out_specs, scratch, cid):
    return pl.pallas_call(
        body,
        out_shape=out_shape,
        in_specs=in_specs,
        out_specs=out_specs,
        scratch_shapes=scratch,
        compiler_params=pltpu.CompilerParams(collective_id=cid, has_side_effects=True, vmem_limit_bytes=58 << 20),
    )(*ins)


def jobs_kernel(jobs, t, cid):
    counts = [len(j.ins) for j in jobs]
    gives = [len(j.out_shape) for j in jobs]
    sizes = [len(j.scratch) for j in jobs]

    def body(*refs):
        place = Place(t)
        place.greet()
        refs = list(refs)
        ins = [[refs.pop(0) for _ in range(c)] for c in counts]
        outs = [[refs.pop(0) for _ in range(c)] for c in gives]
        scratch = [[refs.pop(0) for _ in range(c)] for c in sizes]
        running = [j.steps(place, i, o, s) for j, i, o, s in zip(jobs, ins, outs, scratch)]
        while running:
            running = [g for g in running if next(g, None) is not None]

    return communicate(
        body,
        [s for j in jobs for s in j.out_shape],
        [a for j in jobs for a in j.ins],
        [a for j in jobs for a in j.specs],
        [ANY] * sum(gives),
        [s for j in jobs for s in j.scratch],
        cid,
    )


def attend(tokens_qkv, t, causal, bq, job, lead, each, cid):
    n, d = tokens_qkv[0].shape
    slots = Slots(t, n, d)
    pairs = slots.pairs
    held = jax.ShapeDtypeStruct((pairs, LEN, LANES), jnp.bfloat16)
    extra, gives = len(job.ins), len(job.out_shape)

    def body(*refs):
        qkv, refs = refs[:3], refs[3:]
        job_refs, refs = refs[:extra], refs[extra:]
        out, saved, lse, refs = refs[0], refs[1:5], refs[5], refs[6:]
        job_outs, refs = refs[:gives], refs[gives:]
        here, (hs, hr, ts, tr, keep), refs = refs[:4], refs[4:9], refs[9:]
        place = Place(t)
        place.greet()

        def main():
            move = ToHeads(place, slots, qkv, here[:3], hs, hr)
            back = ToTokens(place, slots, here[3:], [out], ts, tr)
            move.start()
            yield lead
            for slot in range(pairs):
                move.wait_slot(slot)
                for i in range(LEN // bq):
                    attend_block(i, bq, causal, *(r.at[slot] for r in here), lse.at[slot])
                    yield each
                back.start_slot(slot)
            copies = [pltpu.make_async_copy(h, s, keep.at[i]) for i, (h, s) in enumerate(zip(here, saved))]
            for c in copies:
                c.start()
            move.finish()
            yield -1
            back.finish()
            for c in copies:
                c.wait()

        weave(main(), job.steps(place, job_refs, job_outs, refs))

    out = communicate(
        body,
        [jax.ShapeDtypeStruct((n, d), jnp.bfloat16)]
        + [held] * 4
        + [jax.ShapeDtypeStruct((pairs, 8, LEN), jnp.float32)]
        + job.out_shape,
        [*tokens_qkv, *job.ins],
        [ANY] * 3 + job.specs,
        [ANY] * 5 + [VMEM] + [ANY] * gives,
        [pltpu.VMEM(held.shape, held.dtype)] * 4
        + reshard_sems(slots, 3, 1)
        + [pltpu.SemaphoreType.DMA((4,))]
        + job.scratch,
        cid,
    )
    return out[0], out[1:6], out[6:]


def attend_back(grad, saved, t, causal, bq, job, lead, every, cid):
    n, d = grad.shape
    slots = Slots(t, n, d)
    pairs = slots.pairs
    held = pltpu.VMEM((pairs, LEN, LANES), jnp.bfloat16)
    extra, gives = len(job.ins), len(job.out_shape)

    def body(grad_ref, q, k, v, o, lse, *refs):
        job_refs, refs = refs[:extra], refs[extra:]
        outs, refs = refs[:3], refs[3:]
        job_outs, refs = refs[:gives], refs[gives:]
        (do, *made, kt, dk, dv, hs, hr, ts, tr), refs = refs[:11], refs[11:]
        place = Place(t)
        place.greet()

        def main():
            move = ToHeads(place, slots, [grad_ref], [do], hs, hr)
            back = ToTokens(place, slots, made, outs, ts, tr)
            move.start()
            yield lead
            count = 0
            for slot in range(pairs):
                move.wait_slot(slot)
                dk[...] = jnp.zeros_like(dk)
                dv[...] = jnp.zeros_like(dv)
                kt[...] = jnp.transpose(k[slot])
                for i in range(LEN // bq):
                    attend_back_block(
                        i,
                        bq,
                        causal,
                        *(r.at[slot] for r in (q, k, v, o, lse, do, made[0])),
                        kt,
                        dk,
                        dv,
                    )
                    count += 1
                    yield 1 if count % every == 0 else 0
                made[1][slot] = dk[...].astype(jnp.bfloat16)
                made[2][slot] = dv[...].astype(jnp.bfloat16)
                back.start_slot(slot)
            move.finish()
            yield -1
            back.finish()

        weave(main(), job.steps(place, job_refs, job_outs, refs))

    out = communicate(
        body,
        [jax.ShapeDtypeStruct((n, d), jnp.bfloat16)] * 3 + job.out_shape,
        [grad, *saved, *job.ins],
        [ANY] + [VMEM] * 5 + job.specs,
        [ANY] * (3 + gives),
        [held] * 4
        + [pltpu.VMEM((LANES, LEN), jnp.bfloat16)]
        + [pltpu.VMEM((LEN, LANES), jnp.float32)] * 2
        + reshard_sems(slots, 1, 3)
        + job.scratch,
        cid,
    )
    return out[:3], out[3:]


def cols_kernel(count, x_ref, w_ref, *outs):
    out = dot(x_ref[...], w_ref[0], NN)
    width = out.shape[1] // count
    for i, o_ref in enumerate(outs):
        o_ref[...] = out[:, i * width : (i + 1) * width].astype(o_ref.dtype)


def cols_product(x, weight, count, dtype=jnp.bfloat16):
    n, d = x.shape
    t, _, c = weight.shape
    width = c // count
    return pl.pallas_call(
        functools.partial(cols_kernel, count),
        grid=(t,),
        out_shape=[jax.ShapeDtypeStruct((n, t * width), dtype)] * count,
        in_specs=[
            pl.BlockSpec((n, d), lambda i: (0, 0)),
            pl.BlockSpec((1, d, c), lambda i: (i, 0, 0)),
        ],
        out_specs=[pl.BlockSpec((n, width), lambda i: (0, i))] * count,
        compiler_params=pltpu.CompilerParams(vmem_limit_bytes=48 << 20),
        cost_estimate=pl.CostEstimate(
            flops=2 * n * d * t * c, bytes_accessed=2 * (t * d * c + n * d + n * t * c), transcendentals=0
        ),
    )(x, weight)


def back_kernel(count, *refs):
    ys, w_ref, o_ref = refs[:count], refs[count], refs[count + 1]
    y = jnp.concatenate([y_ref[...] for y_ref in ys], 1) if count > 1 else ys[0][...]
    term = dot(y, w_ref[0], NT)

    @pl.when(pl.program_id(0) == 0)
    def _():
        o_ref[...] = term

    @pl.when(pl.program_id(0) != 0)
    def _():
        o_ref[...] += term


def back_product(ys, weight):
    count = len(ys)
    n = ys[0].shape[0]
    t, d, c = weight.shape
    width = c // count
    return pl.pallas_call(
        functools.partial(back_kernel, count),
        grid=(t,),
        out_shape=jax.ShapeDtypeStruct((n, d), jnp.float32),
        in_specs=[pl.BlockSpec((n, width), lambda i: (0, i))] * count
        + [pl.BlockSpec((1, d, c), lambda i: (i, 0, 0))],
        out_specs=pl.BlockSpec((n, d), lambda i: (0, 0)),
        compiler_params=pltpu.CompilerParams(vmem_limit_bytes=48 << 20),
        cost_estimate=pl.CostEstimate(
            flops=2 * n * d * t * c, bytes_accessed=2 * (t * d * c + 2 * n * d + n * t * c), transcendentals=0
        ),
    )(*ys, weight)


def forward_kernel(x_ref, w_ref, b_ref, v_ref, act_ref, slope_ref, o_ref):
    v = dot(x_ref[...], w_ref[0], NN) + b_ref[...].astype(jnp.float32)
    square = v * v
    th = jnp.tanh(math.sqrt(2 / math.pi) * v * (1 + 0.044715 * square))
    half = 0.5 * (1 + th)
    act = (v * half).astype(jnp.bfloat16)
    act_ref[...] = act
    inner = math.sqrt(2 / math.pi) * (1 + 3 * 0.044715 * square)
    slope_ref[...] = (half + 0.5 * v * (1 - th * th) * inner).astype(jnp.bfloat16)
    term = dot(act, v_ref[0], NN)

    @pl.when(pl.program_id(0) == 0)
    def _():
        o_ref[...] = term

    @pl.when(pl.program_id(0) != 0)
    def _():
        o_ref[...] += term


def forward_hidden(x, w_hid, bias, w_out):
    n, d = x.shape
    t, _, c = w_hid.shape
    low = jax.ShapeDtypeStruct((n, t * c), jnp.bfloat16)
    part = pl.BlockSpec((n, c), lambda i: (0, i))
    whole = pl.BlockSpec((n, d), lambda i: (0, 0))
    return pl.pallas_call(
        forward_kernel,
        grid=(t,),
        out_shape=[low, low, jax.ShapeDtypeStruct((n, d), jnp.float32)],
        in_specs=[
            whole,
            pl.BlockSpec((1, d, c), lambda i: (i, 0, 0)),
            pl.BlockSpec((1, c), lambda i: (0, i)),
            pl.BlockSpec((1, c, d), lambda i: (i, 0, 0)),
        ],
        out_specs=[part, part, whole],
        compiler_params=pltpu.CompilerParams(vmem_limit_bytes=48 << 20),
        cost_estimate=pl.CostEstimate(
            flops=4 * n * d * t * c, bytes_accessed=4 * t * d * c + 4 * n * t * c, transcendentals=n * t * c
        ),
    )(x, w_hid, bias, w_out)


def backward_kernel(g_ref, v_ref, slope_ref, w_ref, gh_ref, sum_ref, o_ref):
    grad = dot(g_ref[...], v_ref[0], NT) * slope_ref[...].astype(jnp.float32)
    grad = grad.astype(jnp.bfloat16)
    gh_ref[...] = grad
    sum_ref[...] = jnp.sum(grad.astype(jnp.float32), axis=0, keepdims=True)
    term = dot(grad, w_ref[0], NT)

    @pl.when(pl.program_id(0) == 0)
    def _():
        o_ref[...] = term

    @pl.when(pl.program_id(0) != 0)
    def _():
        o_ref[...] += term


def backward_hidden(grad, w_out, slopes, w_hid):
    n, d = grad.shape
    t, _, c = w_hid.shape
    part = pl.BlockSpec((n, c), lambda i: (0, i))
    whole = pl.BlockSpec((n, d), lambda i: (0, 0))
    return pl.pallas_call(
        backward_kernel,
        grid=(t,),
        out_shape=[
            jax.ShapeDtypeStruct((n, t * c), jnp.bfloat16),
            jax.ShapeDtypeStruct((1, t * c), jnp.float32),
            jax.ShapeDtypeStruct((n, d), jnp.float32),
        ],
        in_specs=[
            whole,
            pl.BlockSpec((1, c, d), lambda i: (i, 0, 0)),
            part,
            pl.BlockSpec((1, d, c), lambda i: (i, 0, 0)),
        ],
        out_specs=[part, pl.BlockSpec((1, c), lambda i: (0, i)), whole],
        compiler_params=pltpu.CompilerParams(vmem_limit_bytes=48 << 20),
        cost_estimate=pl.CostEstimate(
            flops=4 * n * d * t * c, bytes_accessed=4 * t * d * c + 4 * n * t * c, transcendentals=0
        ),
    )(grad, w_out, slopes, w_hid)


def cols_weight(x, ys, t):
    return Weight(x, ys, True, t)


def rows_weight(x, y, t):
    return Weight(x, [y], False, t)


def cols_result(total, count, d, width):
    total = total.astype(jnp.float32)
    if width < LANES:
        parts = total.reshape(count, d // 2, 2, width).transpose(2, 1, 0, 3)
        return parts.reshape(d, count * width)
    return total.reshape(-1, d, LANES).transpose(1, 0, 2).reshape(d, count * width)


def rows_grad_kernel(x_ref, y_ref, o_ref):
    out = dot(jnp.transpose(x_ref[...]), y_ref[...], NN).astype(o_ref.dtype)
    r = out.shape[0]
    for j in range(out.shape[1] // LANES):
        o_ref[0, 0, j * r : j * r + r, :] = out[:, j * LANES : j * LANES + LANES]


def rows_grad(x, y, t):
    n, d = y.shape
    blocks = min(t, x.shape[1] // LANES)
    r = x.shape[1] // blocks
    whole = blocks == t
    size = d // LANES * r
    out = pl.pallas_call(
        rows_grad_kernel,
        grid=(blocks,),
        out_shape=jax.ShapeDtypeStruct((2, t // 2, size, LANES) if whole else (blocks, 1, size, LANES), jnp.bfloat16),
        in_specs=[pl.BlockSpec((n, r), lambda i: (0, i)), pl.BlockSpec((n, d), lambda i: (0, 0))],
        out_specs=pl.BlockSpec(
            (1, 1, size, LANES), (lambda i: (i % 2, i // 2, 0, 0)) if whole else (lambda i: (i, 0, 0, 0))
        ),
        compiler_params=pltpu.CompilerParams(vmem_limit_bytes=48 << 20),
        cost_estimate=pl.CostEstimate(
            flops=2 * n * d * blocks * r, bytes_accessed=2 * (blocks * d * r + n * d + n * blocks * r), transcendentals=0
        ),
    )(x, y)
    if whole:
        return out
    m = t // blocks
    parts = out.reshape(blocks, d // LANES, m, r // m, LANES).transpose(0, 2, 1, 3, 4)
    return by_side(parts.reshape(t, size // m, LANES), t)


def rows_result(total, r, d):
    return total.astype(jnp.float32).reshape(d // LANES, r, LANES).transpose(1, 0, 2).reshape(r, d)


def gather_weight(weight):
    dp, t = lax.axis_size("dp"), lax.axis_size("tensor")
    rows = weight.shape[0] // dp
    share = lax.dynamic_slice_in_dim(weight, lax.axis_index("dp") * rows, rows, 0)
    whole = lax.all_gather(share, ("tensor", "dp"), axis=0, tiled=True)
    return whole.reshape(t, weight.shape[0], weight.shape[1])


def widen(weight, count):
    t, r, c = weight.shape
    width = c // count
    if width % LANES == 0:
        return weight
    m = LANES // width
    parts = weight.reshape(t // m, m, r, count, width).transpose(0, 2, 3, 1, 4)
    return parts.reshape(t // m, r, count * LANES)


def swap(value, axis, bit):
    size = lax.axis_size(axis)
    return lax.ppermute(value, axis, [(i, i ^ bit) for i in range(size)])


def settle(total):
    bit = 4
    while bit < lax.axis_size("dp"):
        total = total + swap(total, "dp", bit)
        bit *= 2
    return total


def normalize(rows_in, gain_row, shift_row):
    row_mean = jnp.mean(rows_in, axis=-1, keepdims=True)
    centered = rows_in - row_mean
    variance = jnp.mean(centered * centered, axis=-1, keepdims=True)
    return centered * lax.rsqrt(variance + norm_eps) * gain_row + shift_row


def gelu_tanh(values):
    return jax.nn.gelu(values, approximate=True)


def product(values, weight):
    return jnp.dot(values, weight, preferred_element_type=jnp.float32)


def per_device(
    tokens,
    memory,
    self_qkv,
    self_out,
    cross_q,
    cross_kv,
    cross_out,
    hidden_weight,
    hidden_bias,
    output_weight,
    output_bias,
    norm_gain,
    norm_shift,
    grad_output,
):
    low = jnp.bfloat16
    t = lax.axis_size("tensor")
    n, d = tokens.shape
    size = LEN * 8 // t
    units = hidden_bias.shape[0]
    bias_block = jnp.pad(hidden_bias, (0, 64 * LANES - units)).reshape(64, LANES)
    first = [self_qkv.reshape(d, -1), bias_block]
    w_qkv, bias_all = jobs_kernel([Gather(first, t, 0.36)], t, 0)
    w_qkv = widen(w_qkv, 3)
    bias_all = bias_all.reshape(t, -1)[:, :units].reshape(1, -1)

    qkv = cols_product(tokens, w_qkv, 3)
    second = [self_out, cross_q, cross_kv.reshape(d, -1), cross_out]
    self_heads, self_saved, (w_so, w_cq, w_kv, w_co) = attend(
        qkv, t, True, 512, Gather(second, t, 0.36), 4, 1, 1
    )
    w_cq, w_kv = widen(w_cq, 1), widen(w_kv, 2)
    w_so, w_co = w_so.reshape(d, d), w_co.reshape(d, d)
    branch_one = product(self_heads, w_so)
    normed_one, pull_one = jax.vjp(
        normalize, residual_alpha * tokens.astype(jnp.float32) + branch_one, norm_gain[0], norm_shift[0]
    )
    normed_one_low = normed_one.astype(low)
    kv = cols_product(memory, w_kv, 2)
    cq = cols_product(normed_one_low, w_cq, 1)
    third = [hidden_weight, output_weight]
    cross_heads, cross_saved, (w_hid, w_out) = attend([*cq, *kv], t, False, 512, Gather(third, t, 0.36), 4, 1, 2)
    branch_two = product(cross_heads, w_co)
    normed_two, pull_two = jax.vjp(
        normalize, residual_alpha * normed_one + branch_two, norm_gain[1], norm_shift[1]
    )
    normed_two_low = normed_two.astype(low)
    activated, slopes, branch_three = forward_hidden(normed_two_low, w_hid, bias_all, w_out)
    layer_out, pull_three = jax.vjp(
        normalize, residual_alpha * normed_two + branch_three + output_bias, norm_gain[2], norm_shift[2]
    )
    grad_three, gain_three, shift_three = pull_three(grad_output.astype(jnp.float32))
    bias_out_grad = jnp.sum(grad_three, axis=0)
    grad_three_low = grad_three.astype(low)
    grad_hidden, hidden_bias_grad, grad_normed = backward_hidden(grad_three_low, w_out, slopes, w_hid)
    grad_two, gain_two, shift_two = pull_two(
        residual_alpha * grad_three + grad_normed
    )
    grad_two_low = grad_two.astype(low)
    grad_co = lax.dot_general(grad_two_low, w_co, NT, preferred_element_type=jnp.float32).astype(low)
    reduce_ff = Reduce(
        [rows_weight(activated, grad_three_low, t), cols_weight(normed_two_low, [grad_hidden], t)], t, size, 0.25
    )
    (g_cq, g_ck, g_cv), (out_weight_grad, hidden_weight_grad) = attend_back(
        grad_co, cross_saved, t, False, 256, reduce_ff, 2, 2, 3
    )
    grad_one, gain_one, shift_one = pull_one(residual_alpha * grad_two + back_product([g_cq], w_cq))
    grad_one_low = grad_one.astype(low)
    grad_so = lax.dot_general(grad_one_low, w_so, NT, preferred_element_type=jnp.float32).astype(low)
    reduce_cross = Reduce(
        [
            rows_weight(cross_heads, grad_two_low, t),
            cols_weight(normed_one_low, [g_cq], t),
            cols_weight(memory, [g_ck, g_cv], t),
            rows_weight(self_heads, grad_one_low, t),
        ],
        t,
        size,
        0.25,
    )
    g_qkv, (cross_out_grad, cross_q_grad, cross_kv_grad, self_out_grad) = attend_back(
        grad_so, self_saved, t, True, 256, reduce_cross, 2, 2, 4
    )
    small = jnp.concatenate(
        [gain_one, gain_two, gain_three, shift_one, shift_two, shift_three, bias_out_grad, hidden_bias_grad[0]]
    ).reshape(-1, LANES)
    self_qkv_grad, small, grad_tokens, grad_memory = jobs_kernel(
        [
            Reduce([cols_weight(tokens, g_qkv, t)], t, size, 0.5),
            Total(small, t),
            Back(g_qkv, w_qkv, grad_one, residual_alpha),
            Back([g_ck, g_cv], w_kv),
        ],
        t,
        5,
    )
    small = settle(small).reshape(-1)
    gain_total, shift_total = small[: 3 * d].reshape(3, d), small[3 * d : 6 * d].reshape(3, d)
    bias_total = small[6 * d : 7 * d]
    hidden_bias_total = lax.dynamic_slice_in_dim(small, 7 * d + lax.axis_index("tensor") * units, units, 0)
    out_weight_grad = rows_result(settle(out_weight_grad), output_weight.shape[0], d)
    hidden_weight_grad = cols_result(settle(hidden_weight_grad), 1, d, hidden_weight.shape[1])
    cross_out_grad = rows_result(settle(cross_out_grad), cross_out.shape[0], d)
    cross_q_grad = cols_result(settle(cross_q_grad), 1, d, cross_q.shape[1])
    cross_kv_grad = cols_result(settle(cross_kv_grad), 2, d, cross_kv.shape[2]).reshape(cross_kv.shape)
    self_out_grad = rows_result(settle(self_out_grad), self_out.shape[0], d)
    self_qkv_grad = cols_result(settle(self_qkv_grad), 3, d, self_qkv.shape[2]).reshape(self_qkv.shape)
    return (
        layer_out.astype(low),
        grad_tokens,
        grad_memory,
        self_qkv_grad,
        self_out_grad,
        cross_q_grad,
        cross_kv_grad,
        cross_out_grad,
        hidden_weight_grad,
        hidden_bias_total,
        out_weight_grad,
        bias_total,
        gain_total,
        shift_total,
    )


def solution(mesh):
    return jax.shard_map(
        per_device,
        mesh=mesh,
        in_specs=(
            P(("dp", "tensor"), None),
            P(("dp", "tensor"), None),
            P(None, None, "tensor"),
            P("tensor", None),
            P(None, "tensor"),
            P(None, None, "tensor"),
            P("tensor", None),
            P(None, "tensor"),
            P("tensor"),
            P("tensor", None),
            P(),
            P(),
            P(),
            P(("dp", "tensor"), None),
        ),
        out_specs=(
            P(("dp", "tensor"), None),
            P(("dp", "tensor"), None),
            P(("dp", "tensor"), None),
            P(None, None, "tensor"),
            P("tensor", None),
            P(None, "tensor"),
            P(None, None, "tensor"),
            P("tensor", None),
            P(None, "tensor"),
            P("tensor"),
            P("tensor", None),
            P(),
            P(),
            P(),
        ),
        check_vma=False,
    )
```

```python
import functools
import math

import jax
import jax.numpy as jnp
from jax import lax
from jax.experimental import pallas as pl
from jax.experimental.pallas import tpu as pltpu
from jax.sharding import PartitionSpec as P

MESH = pl.DeviceIdType.MESH
DH = 64
LANES = 128
LEN = 1024

residual_alpha = 300.0**0.25
norm_eps = 1e-05


def loop(lo, hi, body):
    def step(i, _):
        body(i)
        return 0

    lax.fori_loop(lo, hi, step, 0)


def weave(main, back):
    for steps in main:
        while steps != 0 and next(back, None) is not None:
            steps -= 1
    for _ in back:
        pass


class Place:
    def __init__(self, t):
        self.t, self.depth = t, t // 2
        self.d, self.me = lax.axis_index("dp"), lax.axis_index("tensor")
        self.core, self.xpos = self.d % 2, (self.d // 2) % 2
        self.line, self.side = self.me // 2, self.me % 2
        self.y_mate = {"tensor": 2 * self.line + 1 - self.side}
        self.x_mate = {"dp": self.d + 2 - 4 * self.xpos}
        self.sibling = {"dp": self.d + 1 - 2 * self.core}

    def line_at(self, i):
        return lax.rem(self.line + i, self.depth)

    def z_mate(self, i):
        return {"tensor": 2 * self.line_at(i) + self.side}

    def greet(self):
        barrier = pltpu.get_barrier_semaphore()
        peers = [{"tensor": lax.rem(self.me + i, self.t)} for i in range(1, self.t)]
        for p in peers + [self.x_mate, self.sibling]:
            pl.semaphore_signal(barrier, inc=1, device_id=p, device_id_type=MESH)
        pl.semaphore_wait(barrier, self.t + 1)


def remote(src, dst, send, recv, device):
    return pltpu.make_async_remote_copy(src, dst, send, recv, device_id=device, device_id_type=MESH)


def landed(ref, sem):
    pltpu.make_async_copy(ref, ref, sem).wait()


def at16(v):
    return pl.multiple_of(v, 16)


def rows_at(start, count):
    return pl.ds(pl.multiple_of(start, count), count)


class Slots:
    def __init__(self, t, n, d):
        self.block = math.gcd(n, LEN)
        self.blocks = n // self.block
        self.per_seq = LEN // self.block
        self.wide = d // LANES
        self.total = n * t // LEN * self.wide
        self.pairs = -(-self.total // t)
        self.units = self.blocks * self.wide
        self.lands = self.pairs * self.per_seq


class ToHeads:
    def __init__(self, place, slots, ins, outs, send, recv):
        self.place, self.slots, self.ins, self.outs, self.send, self.recv = place, slots, ins, outs, send, recv

    def unit(self, a, u):
        s = self.slots
        j, p = u // s.wide, u % s.wide
        g = self.place.me * s.blocks + j
        q = (g // s.per_seq) * s.wide + p
        dst, slot, k = q // s.pairs, q % s.pairs, g % s.per_seq
        src = self.ins[a].at[rows_at(j * s.block, s.block), rows_at(p * LANES, LANES)]
        to = self.outs[a].at[slot, rows_at(k * s.block, s.block), :]
        return dst, src, to, self.send.at[a, u], self.recv.at[a, slot * s.per_seq + k]

    def start(self):
        for a in range(len(self.ins)):

            def one(u):
                dst, src, to, ss, rs = self.unit(a, u)

                @pl.when(dst == self.place.me)
                def _():
                    pltpu.make_async_copy(src, to, rs).start()

                @pl.when(dst != self.place.me)
                def _():
                    remote(src, to, ss, rs, {"tensor": dst}).start()

            loop(0, self.slots.units, one)

    def wait_slot(self, slot):
        s = self.slots

        @pl.when(self.place.me * s.pairs + slot < s.total)
        def _():
            for a in range(len(self.ins)):
                loop(
                    0,
                    s.per_seq,
                    lambda k: landed(
                        self.outs[a].at[slot, rows_at(k * s.block, s.block), :], self.recv.at[a, slot * s.per_seq + k]
                    ),
                )

    def finish(self):
        for a in range(len(self.ins)):

            def one(u):
                dst, src, to, ss, rs = self.unit(a, u)

                @pl.when(dst != self.place.me)
                def _():
                    remote(src, to, ss, rs, {"tensor": dst}).wait_send()

            loop(0, self.slots.units, one)


class ToTokens:
    def __init__(self, place, slots, ins, outs, send, recv):
        self.place, self.slots, self.ins, self.outs, self.send, self.recv = place, slots, ins, outs, send, recv

    def unit(self, a, slot, k):
        s = self.slots
        q = self.place.me * s.pairs + slot
        g = (q // s.wide) * s.per_seq + k
        dst, j, p = g // s.blocks, g % s.blocks, q % s.wide
        src = self.ins[a].at[slot, rows_at(k * s.block, s.block), :]
        to = self.outs[a].at[rows_at(j * s.block, s.block), rows_at(p * LANES, LANES)]
        return q < s.total, dst, src, to, self.send.at[a, slot * s.per_seq + k], self.recv.at[a, j * s.wide + p]

    def start_slot(self, slot):
        for a in range(len(self.ins)):

            def one(k):
                real, dst, src, to, ss, rs = self.unit(a, slot, k)

                @pl.when(real & (dst == self.place.me))
                def _():
                    pltpu.make_async_copy(src, to, rs).start()

                @pl.when(real & (dst != self.place.me))
                def _():
                    remote(src, to, ss, rs, {"tensor": dst}).start()

            loop(0, self.slots.per_seq, one)

    def finish(self):
        s = self.slots
        for a in range(len(self.ins)):

            def sent(u):
                real, dst, src, to, ss, rs = self.unit(a, u // s.per_seq, u % s.per_seq)

                @pl.when(real & (dst != self.place.me))
                def _():
                    remote(src, to, ss, rs, {"tensor": dst}).wait_send()

            loop(0, s.lands, sent)

            def got(r):
                j, p = r // s.wide, r % s.wide
                landed(
                    self.outs[a].at[rows_at(j * s.block, s.block), rows_at(p * LANES, LANES)], self.recv.at[a, r]
                )

            loop(0, s.units, got)


def reshard_sems(slots, heads, tokens):
    dma = pltpu.SemaphoreType.DMA
    return [dma((heads, slots.units)), dma((heads, slots.lands)), dma((tokens, slots.lands)), dma((tokens, slots.units))]


NT = (((1,), (1,)), ((), ()))
NN = (((1,), (0,)), ((), ()))
LOG2E = math.log2(math.e)


def dot(a, b, dims):
    return lax.dot_general(a, b, dims, preferred_element_type=jnp.float32)


def lane_half(shape, h):
    return (lax.broadcasted_iota(jnp.int32, shape, len(shape) - 1) // DH) == h


def attend_block(i, bq, causal, q_ref, k_ref, v_ref, o_ref, lse_ref):
    keys = bq * (i + 1) if causal else LEN
    rows = pl.ds(i * bq, bq)
    q = q_ref[rows, :] * jnp.bfloat16(0.125)
    k = k_ref[:keys, :]
    v = v_ref[:keys, :]
    total = None
    for h in (0, 1):
        qh = jnp.where(lane_half(q.shape, h), q, jnp.bfloat16(0))
        s = dot(qh, k, NT)
        if causal:
            tail = s[:, keys - bq :]
            r = lax.broadcasted_iota(jnp.int32, tail.shape, 0)
            c = lax.broadcasted_iota(jnp.int32, tail.shape, 1)
            tail = jnp.where(c <= r, tail, -1e30)
            s = tail if keys == bq else jnp.concatenate([s[:, : keys - bq], tail], 1)
        m = jnp.max(s, axis=-1, keepdims=True)
        e = jnp.exp2((s - m) * LOG2E)
        total_e = jnp.sum(e, axis=-1, keepdims=True)
        o = dot(e.astype(jnp.bfloat16), v, NN) / total_e
        total = o if h == 0 else jnp.where(lane_half(o.shape, 0), total, o)
        lse = m * LOG2E + jnp.log2(total_e)
        lse_ref[h : h + 1, rows] = jnp.transpose(jnp.broadcast_to(lse, (bq, LANES)))[0:1]
    o_ref[rows, :] = total.astype(jnp.bfloat16)


def attend_back_block(i, bq, causal, q_ref, k_ref, v_ref, o_ref, lse_ref, do_ref, dq_ref, kt_ref, dk_ref, dv_ref):
    keys = bq * (i + 1) if causal else LEN
    rows = pl.ds(i * bq, bq)
    q = q_ref[rows, :] * jnp.bfloat16(0.125)
    do = do_ref[rows, :]
    prod = jnp.transpose(do.astype(jnp.float32) * o_ref[rows, :].astype(jnp.float32))
    k = k_ref[:keys, :]
    v = v_ref[:keys, :]
    dqt = []
    for h in (0, 1):
        mask = lane_half(q.shape, h)
        qh = jnp.where(mask, q, jnp.bfloat16(0))
        doh = jnp.where(mask, do, jnp.bfloat16(0))
        delta = jnp.sum(prod[DH * h : DH * h + DH], axis=0, keepdims=True)
        p = jnp.exp2(dot(k, qh, NT) * LOG2E - lse_ref[h : h + 1, rows])
        if causal:
            tail = p[keys - bq :, :]
            r = lax.broadcasted_iota(jnp.int32, tail.shape, 1)
            c = lax.broadcasted_iota(jnp.int32, tail.shape, 0)
            tail = jnp.where(c <= r, tail, 0.0)
            p = tail if keys == bq else jnp.concatenate([p[: keys - bq], tail], 0)
        ds = (p * (dot(v, doh, NT) - delta)).astype(jnp.bfloat16)
        dv_ref[:keys, :] += dot(p.astype(jnp.bfloat16), doh, NN)
        dk_ref[:keys, :] += dot(ds, qh, NN)
        dqt.append(dot(kt_ref[DH * h : DH * h + DH, :keys], ds, NN))
    dq_ref[rows, :] = (jnp.transpose(jnp.concatenate(dqt, 0)) * 0.125).astype(jnp.bfloat16)


class Gather:
    def __init__(self, weights, t, share, size=1 << 17):
        self.t, self.depth, self.share = t, t // 2, share
        self.ins, self.specs = list(weights), [ANY] * len(weights)
        self.shapes = [w.shape for w in weights]
        self.pieces = []
        for w, (r, c) in enumerate(self.shapes):
            rows = r
            while rows % 64 == 0 and rows * c > size:
                rows //= 2
            self.pieces += [(w, at, rows) for at in range(0, r, rows)]
        m, dma = len(self.pieces), pltpu.SemaphoreType.DMA
        self.out_shape = [jax.ShapeDtypeStruct((t,) + w.shape, w.dtype) for w in weights]
        self.scratch = [
            dma((m, self.depth)),
            dma((m, 2)),
            dma((m, self.depth)),
            dma((m, t)),
            dma((m, t, 2)),
            dma((m, t)),
            dma((m, t)),
            dma((m, t, 2)),
            dma((len(weights),)),
        ]

    def x_rows(self, n):
        half = self.pieces[n][2] // 2
        return min(int(half * self.share / 16 + 0.5) * 16, half // 32 * 16)

    def rows_of(self, n, kind, core):
        _, at, rows = self.pieces[n]
        half = rows // 2
        a = self.x_rows(n)
        start, xpos = at + core * half, self.place.xpos
        if kind == "plane":
            return pl.ds(at16(start + xpos * a), half - a)
        if kind == "x_out":
            return pl.ds(at16(start + xpos * (half - a)), a)
        return pl.ds(at16(start + (1 - xpos) * (half - a)), a)

    def steps(self, place, ins, outs, scratch):
        z_send, own_send, y_send, x_send, d_send, plane_recv, x_recv, d_recv, own_sem = scratch
        self.place = place
        me, depth, t, pieces = place.me, self.depth, self.t, self.pieces

        def has_x(n):
            return self.x_rows(n) > 0

        def rows_of(n, kind, core=place.core):
            return self.rows_of(n, kind, core)

        def part(n, block, kind, core=place.core):
            return outs[pieces[n][0]].at[block, rows_of(n, kind, core), :]

        def own(n):
            return ins[pieces[n][0]].at[rows_of(n, "plane"), :]

        line, side = place.line, place.side

        def along(n, block, sign):
            src = part(n, block, "plane")
            device = {"tensor": 2 * (line + sign) + side}
            return remote(src, src, z_send.at[n, block // 2], plane_recv.at[n, block], device)

        def z_own(n, sign):
            device = {"tensor": 2 * (line + sign) + side}
            return remote(own(n), part(n, me, "plane"), own_send.at[n, (1 - sign) // 2], plane_recv.at[n, me], device)

        def y_own(n):
            return remote(own(n), part(n, me, "plane"), y_send.at[n, line], plane_recv.at[n, me], place.y_mate)

        def y_copy(n, block):
            ref = part(n, block, "plane")
            return remote(ref, ref, y_send.at[n, block // 2], plane_recv.at[n, block], place.y_mate)

        def x_copy(n, block):
            ref = part(n, block, "x_out")
            return remote(ref, ref, x_send.at[n, block], x_recv.at[n, block], place.x_mate)

        def d_copy(n, block, k):
            ref = part(n, block, ("plane", "x_in")[k])
            return remote(ref, ref, d_send.at[n, block, k], d_recv.at[n, block, k], place.sibling)

        def own_copy(w):
            return pltpu.make_async_copy(ins[w], outs[w].at[me], own_sem.at[w])

        def ends(distance):
            yield line >= distance, line - distance, line < depth - 1, 1
            yield line < depth - distance, line + distance, line > 0, -1

        total = len(pieces)

        def launch(n):
            if n < total:
                for sign, there in ((1, line < depth - 1), (-1, line > 0)):

                    @pl.when(there)
                    def _():
                        z_own(n, sign).start()

                y_own(n).start()

        def z_stage(n, distance):
            for there, at, more, sign in ends(distance):

                @pl.when(there)
                def _():
                    block = 2 * at + side
                    landed(part(n, block, "plane"), plane_recv.at[n, block])

                    @pl.when(more)
                    def _():
                        along(n, block, sign).start()

                    y_copy(n, block).start()
                    if has_x(n):
                        x_copy(n, block).start()
                    d_copy(n, block, 0).start()

        def y_stage(n, distance):
            for there, at, _, sign in ends(distance):
                if distance == 0 and sign < 0:
                    continue

                @pl.when(there)
                def _():
                    block = 2 * at + 1 - side
                    landed(part(n, block, "plane"), plane_recv.at[n, block])
                    if has_x(n):
                        x_copy(n, block).start()
                    d_copy(n, block, 0).start()

        def x_stage(n, distance, same):
            if not has_x(n):
                return
            for there, at, _, sign in ends(distance):
                if distance == 0 and sign < 0:
                    continue

                @pl.when(there)
                def _():
                    block = 2 * at + (side if same else 1 - side)
                    landed(part(n, block, "x_in"), x_recv.at[n, block])
                    d_copy(n, block, 1).start()

        launch(0)
        for w in range(len(ins)):
            own_copy(w).start()
        yield True
        for step in range(total + depth):
            launch(step + 1)
            for late in range(depth, -1, -1):
                n = step - late
                if not 0 <= n < total:
                    continue
                if late < depth - 1:
                    z_stage(n, late + 1)
                if late < depth:
                    y_stage(n, late)
                if 0 < late < depth:
                    x_stage(n, late, True)
                if late > 0:
                    x_stage(n, late - 1, False)
            yield True
        for w in range(len(ins)):
            own_copy(w).wait()
        for n in range(total):
            y_own(n).wait_send()
            for sign, there in ((1, line < depth - 1), (-1, line > 0)):

                @pl.when(there)
                def _():
                    z_own(n, sign).wait_send()

            for distance in range(1, depth):
                for there, at, more, sign in ends(distance):

                    @pl.when(there)
                    def _():
                        y_copy(n, 2 * at + side).wait_send()

                    @pl.when(there & more)
                    def _():
                        along(n, 2 * at + side, sign).wait_send()

            def finish(i):
                block = lax.rem(me + i, t)
                for k in range(2 if has_x(n) else 1):
                    d_copy(n, block, k).wait_send()
                    landed(part(n, block, ("plane", "x_in")[k], 1 - place.core), d_recv.at[n, block, k])
                if has_x(n):
                    x_copy(n, block).wait_send()

            loop(1, t, finish)
        yield True


class Weight:
    def __init__(self, x, ys, by_cols, t):
        self.arrays, self.by_cols = [x, *ys], by_cols
        n, m = x.shape
        wide = ys[0].shape[1]
        if by_cols:
            self.height, self.width = m, wide // t
            self.rows = len(ys) * m * self.width // LANES
        else:
            self.height, self.width = m // t, wide
            self.rows = m // t * wide // LANES

    def term(self, xt, ys, at, half, t, which):
        high = self.height
        if self.by_cols and self.width < LANES:
            panel, row = at // (high // 2), at % (high // 2) + which * half
            y = ys[panel][:, rows_at(t // 2 * LANES, LANES)]
            first, second = (dot(xt[rows_at(r, half), :], y, NN) for r in (row, row + high // 2))
            odd = t % 2 == 1
            first = jnp.where(odd, pltpu.roll(first, DH, 1), first)
            second = jnp.where(odd, second, pltpu.roll(second, DH, 1))
            return [jnp.where(lane_half(first.shape, 0), first, second)]
        if self.by_cols:
            panel, row = at // high, at % high
            per = self.width // LANES
            y, col = ys[panel // per], t * self.width + panel % per * LANES
            return [dot(xt[rows_at(row + which * half, half), :], y[:, rows_at(col, LANES)], NN)]
        panels = half // high
        cols = rows_at((at // high + which * panels) * LANES, panels * LANES)
        out = dot(xt[rows_at(t * high, high), :], ys[0][:, cols], NN)
        return [out[:, i * LANES : i * LANES + LANES] for i in range(panels)]


class Reduce:
    def __init__(self, weights, t, size, y_first):
        self.t, self.depth, self.size, self.weights = t, t // 2, size, weights
        self.y_rows = int(size // 2 * y_first) // 32 * 32
        self.ins = [a for w in weights for a in w.arrays]
        self.specs = [VMEM] * len(self.ins)
        self.pieces = [(w, at) for w, g in enumerate(weights) for at in range(0, g.rows, size)]
        m, depth, dma = len(self.pieces), self.depth, pltpu.SemaphoreType.DMA
        H, Hy, Q = size // 2, self.y_rows, (size // 2 - self.y_rows) // 2

        def buf(*shape):
            return pltpu.VMEM(shape + (LANES,), jnp.bfloat16)

        self.out_shape = [jax.ShapeDtypeStruct((g.rows, LANES), jnp.bfloat16) for g in weights]
        self.scratch = [
            buf(2, 2, depth, H),
            buf(2, 2, depth, H),
            buf(m, 2, depth, H),
            buf(m, depth, Hy),
            buf(m, 2, depth, Q),
            buf(m, depth - 1, Hy),
            buf(m, depth, Q),
            buf(m, Hy),
            buf(m, Hy),
            buf(m, depth - 1, Q),
            buf(m, size),
            dma((m, 5 + 2 * depth)),
            dma((m, 5 + 2 * depth)),
            dma((m,)),
        ] + [pltpu.VMEM(w.arrays[0].shape[::-1], jnp.bfloat16) for w in weights]

    def steps(self, place, ins, outs, scratch):
        away, own, r1, r2y, r2x, r3y, r3x, s3y, r4y, r4x, fin, send, recv, store = scratch[:14]
        size, depth, pieces, t = self.size, self.depth, self.pieces, self.t
        H, Hy, Q = size // 2, self.y_rows, (size // 2 - self.y_rows) // 2
        core, xpos, line, side = place.core, place.xpos, place.line, place.side
        turned, ins, arrays = scratch[14:], list(ins), []
        for w in self.weights:
            arrays.append([ins.pop(0) for _ in w.arrays])

        def move(src, dst, n, k, device):
            return remote(src, dst, send.at[n, k], recv.at[n, k], device)

        def copy_core(n):
            return move(away.at[n % 2], r1.at[n], n, 0, place.sibling)

        def copy_y(n):
            return move(r1.at[n, 1 - side, :, pl.ds(0, Hy), :], r2y.at[n], n, 1, place.y_mate)

        def copy_x(n):
            return move(r1.at[n, :, :, pl.ds(at16(Hy + (1 - xpos) * Q), Q), :], r2x.at[n], n, 2, place.x_mate)

        def copy_yz(n, i):
            return move(r2y.at[n, place.line_at(i)], r3y.at[n, i - 1], n, 2 + i, place.z_mate(i))

        def copy_xy(n):
            return move(r2x.at[n, 1 - side], r3x.at[n], n, 2 + depth, place.y_mate)

        def copy_yx(n):
            return move(s3y.at[n], r4y.at[n], n, 3 + depth, place.x_mate)

        def copy_xz(n, i):
            return move(r3x.at[n, place.line_at(i)], r4x.at[n, i - 1], n, 3 + depth + i, place.z_mate(i))

        def copy_xx(n):
            ref = fin.at[n, pl.ds(at16(core * H + Hy + xpos * Q), Q), :]
            return move(ref, ref, n, 3 + 2 * depth, place.x_mate)

        def copy_back(n):
            ref = fin.at[n, pl.ds(at16(core * H), H), :]
            return move(ref, ref, n, 4 + 2 * depth, place.sibling)

        def write(n):
            w, at = pieces[n]
            return pltpu.make_async_copy(fin.at[n], outs[w].at[pl.ds(at, size), :], store.at[n])

        def make(n):
            w, at = pieces[n]
            weight, (x, *ys) = self.weights[w], arrays[w]
            if n == 0 or pieces[n - 1][0] != w:
                turned[w][...] = jnp.transpose(x[...])
            if n >= 2:
                copy_core(n - 2).wait_send()
            for which, into in ((1 - core, away), (core, own)):

                def block(i):
                    parts = weight.term(turned[w], ys, at, H, i, which)
                    high = parts[0].shape[0]
                    for j, part in enumerate(parts):
                        into[n % 2, i % 2, i // 2, j * high : j * high + high, :] = part.astype(jnp.bfloat16)

                loop(0, t, block)
                if into is away:
                    copy_core(n).start()

        def stage0(n):
            copy_core(n).wait_recv()

            def add(i):
                a, b = i // depth, i % depth
                r1[n, a, b] = r1[n, a, b] + own[n % 2, a, b]

            loop(0, 2 * depth, add)
            if Hy:
                copy_y(n).start()
            copy_x(n).start()

        def stage1(n):
            if Hy:
                copy_y(n).wait_recv()

                def add(i):
                    r2y[n, i] = r2y[n, i] + r1[n, side, i, 0:Hy, :]

                loop(0, depth, add)
                for i in range(1, depth):
                    copy_yz(n, i).start()
            copy_x(n).wait_recv()

            def addx(i):
                a, b = i // depth, i % depth
                r2x[n, a, b] = r2x[n, a, b] + r1[n, a, b, pl.ds(at16(Hy + xpos * Q), Q), :]

            loop(0, 2 * depth, addx)
            copy_xy(n).start()

        def stage2(n):
            copy_xy(n).wait_recv()

            def add(i):
                r3x[n, i] = r3x[n, i] + r2x[n, side, i]

            loop(0, depth, add)
            for i in range(1, depth):
                copy_xz(n, i).start()
            if Hy:
                for i in range(1, depth):
                    copy_yz(n, i).wait_recv()
                part = r2y[n, line].astype(jnp.float32)
                for i in range(1, depth):
                    part = part + r3y[n, i - 1].astype(jnp.float32)
                s3y[n] = part.astype(jnp.bfloat16)
                copy_yx(n).start()

        def stage3(n):
            for i in range(1, depth):
                copy_xz(n, i).wait_recv()
            part = r3x[n, line].astype(jnp.float32)
            for i in range(1, depth):
                part = part + r4x[n, i - 1].astype(jnp.float32)
            fin[n, pl.ds(at16(core * H + Hy + xpos * Q), Q), :] = part.astype(jnp.bfloat16)
            copy_xx(n).start()
            if Hy:
                copy_yx(n).wait_recv()
                fin[n, pl.ds(at16(core * H), Hy), :] = s3y[n] + r4y[n]

        def stage4(n):
            copy_xx(n).wait_recv()
            copy_back(n).start()

        def stage5(n):
            copy_back(n).wait_recv()
            write(n).start()

        total = len(pieces)
        make(0)
        yield True
        stages = [stage0, stage1, stage2, stage3, stage4, stage5]
        for step in range(total + len(stages) - 1):
            for k in range(len(stages) - 1, -1, -1):
                if 0 <= step - k < total:
                    stages[k](step - k)
            if step + 1 < total:
                make(step + 1)
            yield True
        for n in range(total):
            if n >= total - 2:
                copy_core(n).wait_send()
            copy_x(n).wait_send()
            copy_xy(n).wait_send()
            copy_xx(n).wait_send()
            copy_back(n).wait_send()
            for i in range(1, depth):
                copy_xz(n, i).wait_send()
            if Hy:
                copy_y(n).wait_send()
                copy_yx(n).wait_send()
                for i in range(1, depth):
                    copy_yz(n, i).wait_send()
            write(n).wait()
        yield True


class Back:
    def __init__(self, ys, weight, rest=None, factor=1.0):
        self.count, self.has_rest, self.factor = len(ys), rest is not None, factor
        self.ins = [*ys, weight] + ([rest] if self.has_rest else [])
        self.specs = [VMEM] * self.count + [ANY] + [VMEM] * self.has_rest
        n, (t, d, c) = ys[0].shape[0], weight.shape
        self.blocks = t
        self.out_shape = [jax.ShapeDtypeStruct((n, d), jnp.float32)]
        self.scratch = [
            pltpu.VMEM((2, d, c), jnp.bfloat16),
            pltpu.VMEM((n, d), jnp.float32),
            pltpu.SemaphoreType.DMA((3,)),
        ]

    def steps(self, place, ins, outs, scratch):
        held, total, sem = scratch
        ys, weight = ins[: self.count], ins[self.count]
        width = held.shape[2] // self.count

        def load(i):
            return pltpu.make_async_copy(weight.at[i], held.at[i % 2], sem.at[i % 2])

        load(0).start()
        for i in range(self.blocks):
            load(i).wait()
            if i + 1 < self.blocks:
                load(i + 1).start()
            y = [y_ref[:, i * width : i * width + width] for y_ref in ys]
            term = dot(jnp.concatenate(y, 1) if len(y) > 1 else y[0], held[i % 2], NT)
            if i:
                total[...] += term
            else:
                total[...] = term + self.factor * ins[-1][...] if self.has_rest else term
            yield True
        out = pltpu.make_async_copy(total, outs[0], sem.at[2])
        out.start()
        out.wait()
        yield True


class Total:
    def __init__(self, value, t):
        self.depth = t // 2
        rows, dma = value.shape[0], pltpu.SemaphoreType.DMA
        self.ins, self.specs = [value], [ANY]
        self.out_shape = [jax.ShapeDtypeStruct(value.shape, jnp.float32)]
        self.scratch = [
            pltpu.VMEM((self.depth, rows, LANES), jnp.float32),
            pltpu.VMEM((3, 2, rows, LANES), jnp.float32),
            dma((self.depth + 3,)),
            dma((self.depth + 3,)),
            dma((2,)),
        ]

    def steps(self, place, ins, outs, scratch):
        along, pair, send, recv, local = scratch
        depth = self.depth

        def z_copy(i):
            return remote(ins[0], along.at[place.line], send.at[i], recv.at[i], place.z_mate(i))

        def swap_copy(k):
            device = (place.y_mate, place.x_mate, place.sibling)[k]
            return remote(pair.at[k, 0], pair.at[k, 1], send.at[depth + k], recv.at[depth + k], device)

        own = pltpu.make_async_copy(ins[0], along.at[place.line], local.at[0])
        own.start()
        for i in range(1, depth):
            z_copy(i).start()
        yield True
        own.wait()
        for i in range(1, depth):
            landed(along.at[place.line_at(depth - i)], recv.at[i])
        total = along[0]
        for i in range(1, depth):
            total = total + along[i]
        for k in range(3):
            pair[k, 0] = total
            swap_copy(k).start()
            yield True
            swap_copy(k).wait_recv()
            total = pair[k, 0] + pair[k, 1]
        for i in range(1, depth):
            z_copy(i).wait_send()
        for k in range(3):
            swap_copy(k).wait_send()
        pair[0, 0] = total
        out = pltpu.make_async_copy(pair.at[0, 0], outs[0], local.at[1])
        out.start()
        out.wait()
        yield True


class Nothing:
    ins, specs, out_shape, scratch = [], [], [], []

    def steps(self, place, ins, outs, scratch):
        yield from ()


ANY = pl.BlockSpec(memory_space=pl.ANY)
VMEM = pl.BlockSpec(memory_space=pltpu.VMEM)


def communicate(body, out_shape, ins, in_specs, out_specs, scratch, cid):
    return pl.pallas_call(
        body,
        out_shape=out_shape,
        in_specs=in_specs,
        out_specs=out_specs,
        scratch_shapes=scratch,
        compiler_params=pltpu.CompilerParams(collective_id=cid, has_side_effects=True, vmem_limit_bytes=58 << 20),
    )(*ins)


def jobs_kernel(jobs, t, cid):
    counts = [len(j.ins) for j in jobs]
    gives = [len(j.out_shape) for j in jobs]
    sizes = [len(j.scratch) for j in jobs]

    def body(*refs):
        place = Place(t)
        place.greet()
        refs = list(refs)
        ins = [[refs.pop(0) for _ in range(c)] for c in counts]
        outs = [[refs.pop(0) for _ in range(c)] for c in gives]
        scratch = [[refs.pop(0) for _ in range(c)] for c in sizes]
        running = [j.steps(place, i, o, s) for j, i, o, s in zip(jobs, ins, outs, scratch)]
        while running:
            running = [g for g in running if next(g, None) is not None]

    return communicate(
        body,
        [s for j in jobs for s in j.out_shape],
        [a for j in jobs for a in j.ins],
        [a for j in jobs for a in j.specs],
        [ANY] * sum(gives),
        [s for j in jobs for s in j.scratch],
        cid,
    )


def attend(tokens_qkv, t, causal, bq, job, lead, each, cid):
    n, d = tokens_qkv[0].shape
    slots = Slots(t, n, d)
    pairs = slots.pairs
    held = jax.ShapeDtypeStruct((pairs, LEN, LANES), jnp.bfloat16)
    extra, gives = len(job.ins), len(job.out_shape)

    def body(*refs):
        qkv, refs = refs[:3], refs[3:]
        job_refs, refs = refs[:extra], refs[extra:]
        out, saved, lse, refs = refs[0], refs[1:5], refs[5], refs[6:]
        job_outs, refs = refs[:gives], refs[gives:]
        here, (hs, hr, ts, tr, keep), refs = refs[:4], refs[4:9], refs[9:]
        place = Place(t)
        place.greet()

        def main():
            move = ToHeads(place, slots, qkv, here[:3], hs, hr)
            back = ToTokens(place, slots, here[3:], [out], ts, tr)
            move.start()
            yield lead
            for slot in range(pairs):
                move.wait_slot(slot)
                for i in range(LEN // bq):
                    attend_block(i, bq, causal, *(r.at[slot] for r in here), lse.at[slot])
                    yield each
                back.start_slot(slot)
            copies = [pltpu.make_async_copy(h, s, keep.at[i]) for i, (h, s) in enumerate(zip(here, saved))]
            for c in copies:
                c.start()
            move.finish()
            yield -1
            back.finish()
            for c in copies:
                c.wait()

        weave(main(), job.steps(place, job_refs, job_outs, refs))

    out = communicate(
        body,
        [jax.ShapeDtypeStruct((n, d), jnp.bfloat16)]
        + [held] * 4
        + [jax.ShapeDtypeStruct((pairs, 8, LEN), jnp.float32)]
        + job.out_shape,
        [*tokens_qkv, *job.ins],
        [ANY] * 3 + job.specs,
        [ANY] * 5 + [VMEM] + [ANY] * gives,
        [pltpu.VMEM(held.shape, held.dtype)] * 4
        + reshard_sems(slots, 3, 1)
        + [pltpu.SemaphoreType.DMA((4,))]
        + job.scratch,
        cid,
    )
    return out[0], out[1:6], out[6:]


def attend_back(grad, saved, t, causal, bq, job, lead, every, cid):
    n, d = grad.shape
    slots = Slots(t, n, d)
    pairs = slots.pairs
    held = pltpu.VMEM((pairs, LEN, LANES), jnp.bfloat16)
    extra, gives = len(job.ins), len(job.out_shape)

    def body(grad_ref, q, k, v, o, lse, *refs):
        job_refs, refs = refs[:extra], refs[extra:]
        outs, refs = refs[:3], refs[3:]
        job_outs, refs = refs[:gives], refs[gives:]
        (do, *made, kt, dk, dv, hs, hr, ts, tr), refs = refs[:11], refs[11:]
        place = Place(t)
        place.greet()

        def main():
            move = ToHeads(place, slots, [grad_ref], [do], hs, hr)
            back = ToTokens(place, slots, made, outs, ts, tr)
            move.start()
            yield lead
            count = 0
            for slot in range(pairs):
                move.wait_slot(slot)
                dk[...] = jnp.zeros_like(dk)
                dv[...] = jnp.zeros_like(dv)
                kt[...] = jnp.transpose(k[slot])
                for i in range(LEN // bq):
                    attend_back_block(
                        i,
                        bq,
                        causal,
                        *(r.at[slot] for r in (q, k, v, o, lse, do, made[0])),
                        kt,
                        dk,
                        dv,
                    )
                    count += 1
                    yield 1 if count % every == 0 else 0
                made[1][slot] = dk[...].astype(jnp.bfloat16)
                made[2][slot] = dv[...].astype(jnp.bfloat16)
                back.start_slot(slot)
            move.finish()
            yield -1
            back.finish()

        weave(main(), job.steps(place, job_refs, job_outs, refs))

    out = communicate(
        body,
        [jax.ShapeDtypeStruct((n, d), jnp.bfloat16)] * 3 + job.out_shape,
        [grad, *saved, *job.ins],
        [ANY] + [VMEM] * 5 + job.specs,
        [ANY] * (3 + gives),
        [held] * 4
        + [pltpu.VMEM((LANES, LEN), jnp.bfloat16)]
        + [pltpu.VMEM((LEN, LANES), jnp.float32)] * 2
        + reshard_sems(slots, 1, 3)
        + job.scratch,
        cid,
    )
    return out[:3], out[3:]


def cols_kernel(count, x_ref, w_ref, *outs):
    out = dot(x_ref[...], w_ref[0], NN)
    width = out.shape[1] // count
    for i, o_ref in enumerate(outs):
        o_ref[...] = out[:, i * width : (i + 1) * width].astype(o_ref.dtype)


def cols_product(x, weight, count, dtype=jnp.bfloat16):
    n, d = x.shape
    t, _, c = weight.shape
    width = c // count
    return pl.pallas_call(
        functools.partial(cols_kernel, count),
        grid=(t,),
        out_shape=[jax.ShapeDtypeStruct((n, t * width), dtype)] * count,
        in_specs=[
            pl.BlockSpec((n, d), lambda i: (0, 0)),
            pl.BlockSpec((1, d, c), lambda i: (i, 0, 0)),
        ],
        out_specs=[pl.BlockSpec((n, width), lambda i: (0, i))] * count,
        compiler_params=pltpu.CompilerParams(vmem_limit_bytes=48 << 20),
        cost_estimate=pl.CostEstimate(
            flops=2 * n * d * t * c, bytes_accessed=2 * (t * d * c + n * d + n * t * c), transcendentals=0
        ),
    )(x, weight)


def back_kernel(count, *refs):
    ys, w_ref, o_ref = refs[:count], refs[count], refs[count + 1]
    y = jnp.concatenate([y_ref[...] for y_ref in ys], 1) if count > 1 else ys[0][...]
    term = dot(y, w_ref[0], NT)

    @pl.when(pl.program_id(0) == 0)
    def _():
        o_ref[...] = term

    @pl.when(pl.program_id(0) != 0)
    def _():
        o_ref[...] += term


def back_product(ys, weight):
    count = len(ys)
    n = ys[0].shape[0]
    t, d, c = weight.shape
    width = c // count
    return pl.pallas_call(
        functools.partial(back_kernel, count),
        grid=(t,),
        out_shape=jax.ShapeDtypeStruct((n, d), jnp.float32),
        in_specs=[pl.BlockSpec((n, width), lambda i: (0, i))] * count
        + [pl.BlockSpec((1, d, c), lambda i: (i, 0, 0))],
        out_specs=pl.BlockSpec((n, d), lambda i: (0, 0)),
        compiler_params=pltpu.CompilerParams(vmem_limit_bytes=48 << 20),
        cost_estimate=pl.CostEstimate(
            flops=2 * n * d * t * c, bytes_accessed=2 * (t * d * c + 2 * n * d + n * t * c), transcendentals=0
        ),
    )(*ys, weight)


def forward_kernel(x_ref, w_ref, b_ref, v_ref, act_ref, slope_ref, o_ref):
    v = dot(x_ref[...], w_ref[0], NN) + b_ref[...].astype(jnp.float32)
    square = v * v
    th = jnp.tanh(math.sqrt(2 / math.pi) * v * (1 + 0.044715 * square))
    half = 0.5 * (1 + th)
    act = (v * half).astype(jnp.bfloat16)
    act_ref[...] = act
    inner = math.sqrt(2 / math.pi) * (1 + 3 * 0.044715 * square)
    slope_ref[...] = (half + 0.5 * v * (1 - th * th) * inner).astype(jnp.bfloat16)
    term = dot(act, v_ref[0], NN)

    @pl.when(pl.program_id(0) == 0)
    def _():
        o_ref[...] = term

    @pl.when(pl.program_id(0) != 0)
    def _():
        o_ref[...] += term


def forward_hidden(x, w_hid, bias, w_out):
    n, d = x.shape
    t, _, c = w_hid.shape
    low = jax.ShapeDtypeStruct((n, t * c), jnp.bfloat16)
    part = pl.BlockSpec((n, c), lambda i: (0, i))
    whole = pl.BlockSpec((n, d), lambda i: (0, 0))
    return pl.pallas_call(
        forward_kernel,
        grid=(t,),
        out_shape=[low, low, jax.ShapeDtypeStruct((n, d), jnp.float32)],
        in_specs=[
            whole,
            pl.BlockSpec((1, d, c), lambda i: (i, 0, 0)),
            pl.BlockSpec((1, c), lambda i: (0, i)),
            pl.BlockSpec((1, c, d), lambda i: (i, 0, 0)),
        ],
        out_specs=[part, part, whole],
        compiler_params=pltpu.CompilerParams(vmem_limit_bytes=48 << 20),
        cost_estimate=pl.CostEstimate(
            flops=4 * n * d * t * c, bytes_accessed=4 * t * d * c + 4 * n * t * c, transcendentals=n * t * c
        ),
    )(x, w_hid, bias, w_out)


def backward_kernel(g_ref, v_ref, slope_ref, w_ref, gh_ref, sum_ref, o_ref):
    grad = dot(g_ref[...], v_ref[0], NT) * slope_ref[...].astype(jnp.float32)
    grad = grad.astype(jnp.bfloat16)
    gh_ref[...] = grad
    sum_ref[...] = jnp.sum(grad.astype(jnp.float32), axis=0, keepdims=True)
    term = dot(grad, w_ref[0], NT)

    @pl.when(pl.program_id(0) == 0)
    def _():
        o_ref[...] = term

    @pl.when(pl.program_id(0) != 0)
    def _():
        o_ref[...] += term


def backward_hidden(grad, w_out, slopes, w_hid):
    n, d = grad.shape
    t, _, c = w_hid.shape
    part = pl.BlockSpec((n, c), lambda i: (0, i))
    whole = pl.BlockSpec((n, d), lambda i: (0, 0))
    return pl.pallas_call(
        backward_kernel,
        grid=(t,),
        out_shape=[
            jax.ShapeDtypeStruct((n, t * c), jnp.bfloat16),
            jax.ShapeDtypeStruct((1, t * c), jnp.float32),
            jax.ShapeDtypeStruct((n, d), jnp.float32),
        ],
        in_specs=[
            whole,
            pl.BlockSpec((1, c, d), lambda i: (i, 0, 0)),
            part,
            pl.BlockSpec((1, d, c), lambda i: (i, 0, 0)),
        ],
        out_specs=[part, pl.BlockSpec((1, c), lambda i: (0, i)), whole],
        compiler_params=pltpu.CompilerParams(vmem_limit_bytes=48 << 20),
        cost_estimate=pl.CostEstimate(
            flops=4 * n * d * t * c, bytes_accessed=4 * t * d * c + 4 * n * t * c, transcendentals=0
        ),
    )(grad, w_out, slopes, w_hid)


def cols_weight(x, ys, t):
    return Weight(x, ys, True, t)


def rows_weight(x, y, t):
    return Weight(x, [y], False, t)


def cols_result(total, count, d, width):
    total = total.astype(jnp.float32)
    if width < LANES:
        parts = total.reshape(count, d // 2, 2, width).transpose(2, 1, 0, 3)
        return parts.reshape(d, count * width)
    return total.reshape(-1, d, LANES).transpose(1, 0, 2).reshape(d, count * width)


def rows_grad_kernel(x_ref, y_ref, o_ref):
    out = dot(jnp.transpose(x_ref[...]), y_ref[...], NN).astype(o_ref.dtype)
    r = out.shape[0]
    for j in range(out.shape[1] // LANES):
        o_ref[0, 0, j * r : j * r + r, :] = out[:, j * LANES : j * LANES + LANES]


def rows_grad(x, y, t):
    n, d = y.shape
    blocks = min(t, x.shape[1] // LANES)
    r = x.shape[1] // blocks
    whole = blocks == t
    size = d // LANES * r
    out = pl.pallas_call(
        rows_grad_kernel,
        grid=(blocks,),
        out_shape=jax.ShapeDtypeStruct((2, t // 2, size, LANES) if whole else (blocks, 1, size, LANES), jnp.bfloat16),
        in_specs=[pl.BlockSpec((n, r), lambda i: (0, i)), pl.BlockSpec((n, d), lambda i: (0, 0))],
        out_specs=pl.BlockSpec(
            (1, 1, size, LANES), (lambda i: (i % 2, i // 2, 0, 0)) if whole else (lambda i: (i, 0, 0, 0))
        ),
        compiler_params=pltpu.CompilerParams(vmem_limit_bytes=48 << 20),
        cost_estimate=pl.CostEstimate(
            flops=2 * n * d * blocks * r, bytes_accessed=2 * (blocks * d * r + n * d + n * blocks * r), transcendentals=0
        ),
    )(x, y)
    if whole:
        return out
    m = t // blocks
    parts = out.reshape(blocks, d // LANES, m, r // m, LANES).transpose(0, 2, 1, 3, 4)
    return by_side(parts.reshape(t, size // m, LANES), t)


def rows_result(total, r, d):
    return total.astype(jnp.float32).reshape(d // LANES, r, LANES).transpose(1, 0, 2).reshape(r, d)


def gather_weight(weight):
    dp, t = lax.axis_size("dp"), lax.axis_size("tensor")
    rows = weight.shape[0] // dp
    share = lax.dynamic_slice_in_dim(weight, lax.axis_index("dp") * rows, rows, 0)
    whole = lax.all_gather(share, ("tensor", "dp"), axis=0, tiled=True)
    return whole.reshape(t, weight.shape[0], weight.shape[1])


def widen(weight, count):
    t, r, c = weight.shape
    width = c // count
    if width % LANES == 0:
        return weight
    m = LANES // width
    parts = weight.reshape(t // m, m, r, count, width).transpose(0, 2, 3, 1, 4)
    return parts.reshape(t // m, r, count * LANES)


def swap(value, axis, bit):
    size = lax.axis_size(axis)
    return lax.ppermute(value, axis, [(i, i ^ bit) for i in range(size)])


def settle(total):
    bit = 4
    while bit < lax.axis_size("dp"):
        total = total + swap(total, "dp", bit)
        bit *= 2
    return total


def normalize(rows_in, gain_row, shift_row):
    row_mean = jnp.mean(rows_in, axis=-1, keepdims=True)
    centered = rows_in - row_mean
    variance = jnp.mean(centered * centered, axis=-1, keepdims=True)
    return centered * lax.rsqrt(variance + norm_eps) * gain_row + shift_row


def gelu_tanh(values):
    return jax.nn.gelu(values, approximate=True)


def product(values, weight):
    return jnp.dot(values, weight, preferred_element_type=jnp.float32)


def per_device(
    tokens,
    memory,
    self_qkv,
    self_out,
    cross_q,
    cross_kv,
    cross_out,
    hidden_weight,
    hidden_bias,
    output_weight,
    output_bias,
    norm_gain,
    norm_shift,
    grad_output,
):
    low = jnp.bfloat16
    t = lax.axis_size("tensor")
    n, d = tokens.shape
    size = LEN * 8 // t
    units = hidden_bias.shape[0]
    bias_block = jnp.pad(hidden_bias, (0, 64 * LANES - units)).reshape(64, LANES)
    first = [self_qkv.reshape(d, -1), bias_block]
    w_qkv, bias_all = jobs_kernel([Gather(first, t, 0.36)], t, 0)
    w_qkv = widen(w_qkv, 3)
    bias_all = bias_all.reshape(t, -1)[:, :units].reshape(1, -1)

    qkv = cols_product(tokens, w_qkv, 3)
    second = [self_out, cross_q, cross_kv.reshape(d, -1), cross_out]
    self_heads, self_saved, (w_so, w_cq, w_kv, w_co) = attend(
        qkv, t, True, 512, Gather(second, t, 0.36), 4, 1, 1
    )
    w_cq, w_kv = widen(w_cq, 1), widen(w_kv, 2)
    w_so, w_co = w_so.reshape(d, d), w_co.reshape(d, d)
    branch_one = product(self_heads, w_so)
    normed_one, pull_one = jax.vjp(
        normalize, residual_alpha * tokens.astype(jnp.float32) + branch_one, norm_gain[0], norm_shift[0]
    )
    normed_one_low = normed_one.astype(low)
    kv = cols_product(memory, w_kv, 2)
    cq = cols_product(normed_one_low, w_cq, 1)
    third = [hidden_weight, output_weight]
    cross_heads, cross_saved, (w_hid, w_out) = attend([*cq, *kv], t, False, 512, Gather(third, t, 0.36), 4, 1, 2)
    branch_two = product(cross_heads, w_co)
    normed_two, pull_two = jax.vjp(
        normalize, residual_alpha * normed_one + branch_two, norm_gain[1], norm_shift[1]
    )
    normed_two_low = normed_two.astype(low)
    activated, slopes, branch_three = forward_hidden(normed_two_low, w_hid, bias_all, w_out)
    layer_out, pull_three = jax.vjp(
        normalize, residual_alpha * normed_two + branch_three + output_bias, norm_gain[2], norm_shift[2]
    )
    grad_three, gain_three, shift_three = pull_three(grad_output.astype(jnp.float32))
    bias_out_grad = jnp.sum(grad_three, axis=0)
    grad_three_low = grad_three.astype(low)
    grad_hidden, hidden_bias_grad, grad_normed = backward_hidden(grad_three_low, w_out, slopes, w_hid)
    grad_two, gain_two, shift_two = pull_two(
        residual_alpha * grad_three + grad_normed
    )
    grad_two_low = grad_two.astype(low)
    grad_co = lax.dot_general(grad_two_low, w_co, NT, preferred_element_type=jnp.float32).astype(low)
    reduce_ff = Reduce(
        [rows_weight(activated, grad_three_low, t), cols_weight(normed_two_low, [grad_hidden], t)], t, size, 0.25
    )
    (g_cq, g_ck, g_cv), (out_weight_grad, hidden_weight_grad) = attend_back(
        grad_co, cross_saved, t, False, 256, reduce_ff, 2, 2, 3
    )
    grad_one, gain_one, shift_one = pull_one(residual_alpha * grad_two + back_product([g_cq], w_cq))
    grad_one_low = grad_one.astype(low)
    grad_so = lax.dot_general(grad_one_low, w_so, NT, preferred_element_type=jnp.float32).astype(low)
    reduce_cross = Reduce(
        [
            rows_weight(cross_heads, grad_two_low, t),
            cols_weight(normed_one_low, [g_cq], t),
            cols_weight(memory, [g_ck, g_cv], t),
            rows_weight(self_heads, grad_one_low, t),
        ],
        t,
        size,
        0.25,
    )
    g_qkv, (cross_out_grad, cross_q_grad, cross_kv_grad, self_out_grad) = attend_back(
        grad_so, self_saved, t, True, 256, reduce_cross, 2, 2, 4
    )
    small = jnp.concatenate(
        [gain_one, gain_two, gain_three, shift_one, shift_two, shift_three, bias_out_grad, hidden_bias_grad[0]]
    ).reshape(-1, LANES)
    self_qkv_grad, small, grad_tokens, grad_memory = jobs_kernel(
        [
            Reduce([cols_weight(tokens, g_qkv, t)], t, size, 0.5),
            Total(small, t),
            Back(g_qkv, w_qkv, grad_one, residual_alpha),
            Back([g_ck, g_cv], w_kv),
        ],
        t,
        5,
    )
    small = settle(small).reshape(-1)
    gain_total, shift_total = small[: 3 * d].reshape(3, d), small[3 * d : 6 * d].reshape(3, d)
    bias_total = small[6 * d : 7 * d]
    hidden_bias_total = lax.dynamic_slice_in_dim(small, 7 * d + lax.axis_index("tensor") * units, units, 0)
    out_weight_grad = rows_result(settle(out_weight_grad), output_weight.shape[0], d)
    hidden_weight_grad = cols_result(settle(hidden_weight_grad), 1, d, hidden_weight.shape[1])
    cross_out_grad = rows_result(settle(cross_out_grad), cross_out.shape[0], d)
    cross_q_grad = cols_result(settle(cross_q_grad), 1, d, cross_q.shape[1])
    cross_kv_grad = cols_result(settle(cross_kv_grad), 2, d, cross_kv.shape[2]).reshape(cross_kv.shape)
    self_out_grad = rows_result(settle(self_out_grad), self_out.shape[0], d)
    self_qkv_grad = cols_result(settle(self_qkv_grad), 3, d, self_qkv.shape[2]).reshape(self_qkv.shape)
    return (
        layer_out.astype(low),
        grad_tokens,
        grad_memory,
        self_qkv_grad,
        self_out_grad,
        cross_q_grad,
        cross_kv_grad,
        cross_out_grad,
        hidden_weight_grad,
        hidden_bias_total,
        out_weight_grad,
        bias_total,
        gain_total,
        shift_total,
    )


def solution(mesh):
    return jax.shard_map(
        per_device,
        mesh=mesh,
        in_specs=(
            P(("dp", "tensor"), None),
            P(("dp", "tensor"), None),
            P(None, None, "tensor"),
            P("tensor", None),
            P(None, "tensor"),
            P(None, None, "tensor"),
            P("tensor", None),
            P(None, "tensor"),
            P("tensor"),
            P("tensor", None),
            P(),
            P(),
            P(),
            P(("dp", "tensor"), None),
        ),
        out_specs=(
            P(("dp", "tensor"), None),
            P(("dp", "tensor"), None),
            P(("dp", "tensor"), None),
            P(None, None, "tensor"),
            P("tensor", None),
            P(None, "tensor"),
            P(None, None, "tensor"),
            P("tensor", None),
            P(None, "tensor"),
            P("tensor"),
            P("tensor", None),
            P(),
            P(),
            P(),
        ),
        check_vma=False,
    )
```

```python
import functools
import math

import jax
import jax.numpy as jnp
from jax import lax
from jax.experimental import pallas as pl
from jax.experimental.pallas import tpu as pltpu
from jax.sharding import PartitionSpec as P

MESH = pl.DeviceIdType.MESH
DH = 64
LANES = 128
LEN = 1024

residual_alpha = 300.0**0.25
norm_eps = 1e-05


def loop(lo, hi, body):
    def step(i, _):
        body(i)
        return 0

    lax.fori_loop(lo, hi, step, 0)


def weave(main, back):
    for steps in main:
        while steps != 0 and next(back, None) is not None:
            steps -= 1
    for _ in back:
        pass


class Place:
    def __init__(self, t):
        self.t, self.depth = t, t // 2
        self.d, self.me = lax.axis_index("dp"), lax.axis_index("tensor")
        self.core, self.xpos = self.d % 2, (self.d // 2) % 2
        self.line, self.side = self.me // 2, self.me % 2
        self.y_mate = {"tensor": 2 * self.line + 1 - self.side}
        self.x_mate = {"dp": self.d + 2 - 4 * self.xpos}
        self.sibling = {"dp": self.d + 1 - 2 * self.core}

    def line_at(self, i):
        return lax.rem(self.line + i, self.depth)

    def z_mate(self, i):
        return {"tensor": 2 * self.line_at(i) + self.side}

    def greet(self):
        barrier = pltpu.get_barrier_semaphore()
        peers = [{"tensor": lax.rem(self.me + i, self.t)} for i in range(1, self.t)]
        for p in peers + [self.x_mate, self.sibling]:
            pl.semaphore_signal(barrier, inc=1, device_id=p, device_id_type=MESH)
        pl.semaphore_wait(barrier, self.t + 1)


def remote(src, dst, send, recv, device):
    return pltpu.make_async_remote_copy(src, dst, send, recv, device_id=device, device_id_type=MESH)


def landed(ref, sem):
    pltpu.make_async_copy(ref, ref, sem).wait()


def at16(v):
    return pl.multiple_of(v, 16)


def rows_at(start, count):
    return pl.ds(pl.multiple_of(start, count), count)


class Slots:
    def __init__(self, t, n, d):
        self.block = math.gcd(n, LEN)
        self.blocks = n // self.block
        self.per_seq = LEN // self.block
        self.wide = d // LANES
        self.total = n * t // LEN * self.wide
        self.pairs = -(-self.total // t)
        self.units = self.blocks * self.wide
        self.lands = self.pairs * self.per_seq


class ToHeads:
    def __init__(self, place, slots, ins, outs, send, recv):
        self.place, self.slots, self.ins, self.outs, self.send, self.recv = place, slots, ins, outs, send, recv

    def unit(self, a, u):
        s = self.slots
        j, p = u // s.wide, u % s.wide
        g = self.place.me * s.blocks + j
        q = (g // s.per_seq) * s.wide + p
        dst, slot, k = q // s.pairs, q % s.pairs, g % s.per_seq
        src = self.ins[a].at[rows_at(j * s.block, s.block), rows_at(p * LANES, LANES)]
        to = self.outs[a].at[slot, rows_at(k * s.block, s.block), :]
        return dst, src, to, self.send.at[a, u], self.recv.at[a, slot * s.per_seq + k]

    def start(self):
        for a in range(len(self.ins)):

            def one(u):
                dst, src, to, ss, rs = self.unit(a, u)

                @pl.when(dst == self.place.me)
                def _():
                    pltpu.make_async_copy(src, to, rs).start()

                @pl.when(dst != self.place.me)
                def _():
                    remote(src, to, ss, rs, {"tensor": dst}).start()

            loop(0, self.slots.units, one)

    def wait_slot(self, slot):
        s = self.slots

        @pl.when(self.place.me * s.pairs + slot < s.total)
        def _():
            for a in range(len(self.ins)):
                loop(
                    0,
                    s.per_seq,
                    lambda k: landed(
                        self.outs[a].at[slot, rows_at(k * s.block, s.block), :], self.recv.at[a, slot * s.per_seq + k]
                    ),
                )

    def finish(self):
        for a in range(len(self.ins)):

            def one(u):
                dst, src, to, ss, rs = self.unit(a, u)

                @pl.when(dst != self.place.me)
                def _():
                    remote(src, to, ss, rs, {"tensor": dst}).wait_send()

            loop(0, self.slots.units, one)


class ToTokens:
    def __init__(self, place, slots, ins, outs, send, recv):
        self.place, self.slots, self.ins, self.outs, self.send, self.recv = place, slots, ins, outs, send, recv

    def unit(self, a, slot, k):
        s = self.slots
        q = self.place.me * s.pairs + slot
        g = (q // s.wide) * s.per_seq + k
        dst, j, p = g // s.blocks, g % s.blocks, q % s.wide
        src = self.ins[a].at[slot, rows_at(k * s.block, s.block), :]
        to = self.outs[a].at[rows_at(j * s.block, s.block), rows_at(p * LANES, LANES)]
        return q < s.total, dst, src, to, self.send.at[a, slot * s.per_seq + k], self.recv.at[a, j * s.wide + p]

    def start_slot(self, slot):
        for a in range(len(self.ins)):

            def one(k):
                real, dst, src, to, ss, rs = self.unit(a, slot, k)

                @pl.when(real & (dst == self.place.me))
                def _():
                    pltpu.make_async_copy(src, to, rs).start()

                @pl.when(real & (dst != self.place.me))
                def _():
                    remote(src, to, ss, rs, {"tensor": dst}).start()

            loop(0, self.slots.per_seq, one)

    def finish(self):
        s = self.slots
        for a in range(len(self.ins)):

            def sent(u):
                real, dst, src, to, ss, rs = self.unit(a, u // s.per_seq, u % s.per_seq)

                @pl.when(real & (dst != self.place.me))
                def _():
                    remote(src, to, ss, rs, {"tensor": dst}).wait_send()

            loop(0, s.lands, sent)

            def got(r):
                j, p = r // s.wide, r % s.wide
                landed(
                    self.outs[a].at[rows_at(j * s.block, s.block), rows_at(p * LANES, LANES)], self.recv.at[a, r]
                )

            loop(0, s.units, got)


def reshard_sems(slots, heads, tokens):
    dma = pltpu.SemaphoreType.DMA
    return [dma((heads, slots.units)), dma((heads, slots.lands)), dma((tokens, slots.lands)), dma((tokens, slots.units))]


NT = (((1,), (1,)), ((), ()))
NN = (((1,), (0,)), ((), ()))
LOG2E = math.log2(math.e)


def dot(a, b, dims):
    return lax.dot_general(a, b, dims, preferred_element_type=jnp.float32)


def lane_half(shape, h):
    return (lax.broadcasted_iota(jnp.int32, shape, len(shape) - 1) // DH) == h


def attend_block(i, bq, causal, q_ref, k_ref, v_ref, o_ref, lse_ref):
    keys = bq * (i + 1) if causal else LEN
    rows = pl.ds(i * bq, bq)
    q = q_ref[rows, :] * jnp.bfloat16(0.125)
    k = k_ref[:keys, :]
    v = v_ref[:keys, :]
    total = None
    for h in (0, 1):
        qh = jnp.where(lane_half(q.shape, h), q, jnp.bfloat16(0))
        s = dot(qh, k, NT)
        if causal:
            tail = s[:, keys - bq :]
            r = lax.broadcasted_iota(jnp.int32, tail.shape, 0)
            c = lax.broadcasted_iota(jnp.int32, tail.shape, 1)
            tail = jnp.where(c <= r, tail, -1e30)
            s = tail if keys == bq else jnp.concatenate([s[:, : keys - bq], tail], 1)
        m = jnp.max(s, axis=-1, keepdims=True)
        e = jnp.exp2((s - m) * LOG2E)
        total_e = jnp.sum(e, axis=-1, keepdims=True)
        o = dot(e.astype(jnp.bfloat16), v, NN) / total_e
        total = o if h == 0 else jnp.where(lane_half(o.shape, 0), total, o)
        lse = m * LOG2E + jnp.log2(total_e)
        lse_ref[h : h + 1, rows] = jnp.transpose(jnp.broadcast_to(lse, (bq, LANES)))[0:1]
    o_ref[rows, :] = total.astype(jnp.bfloat16)


def attend_back_block(i, bq, causal, q_ref, k_ref, v_ref, o_ref, lse_ref, do_ref, dq_ref, kt_ref, dk_ref, dv_ref):
    keys = bq * (i + 1) if causal else LEN
    rows = pl.ds(i * bq, bq)
    q = q_ref[rows, :] * jnp.bfloat16(0.125)
    do = do_ref[rows, :]
    prod = jnp.transpose(do.astype(jnp.float32) * o_ref[rows, :].astype(jnp.float32))
    k = k_ref[:keys, :]
    v = v_ref[:keys, :]
    dqt = []
    for h in (0, 1):
        mask = lane_half(q.shape, h)
        qh = jnp.where(mask, q, jnp.bfloat16(0))
        doh = jnp.where(mask, do, jnp.bfloat16(0))
        delta = jnp.sum(prod[DH * h : DH * h + DH], axis=0, keepdims=True)
        p = jnp.exp2(dot(k, qh, NT) * LOG2E - lse_ref[h : h + 1, rows])
        if causal:
            tail = p[keys - bq :, :]
            r = lax.broadcasted_iota(jnp.int32, tail.shape, 1)
            c = lax.broadcasted_iota(jnp.int32, tail.shape, 0)
            tail = jnp.where(c <= r, tail, 0.0)
            p = tail if keys == bq else jnp.concatenate([p[: keys - bq], tail], 0)
        ds = (p * (dot(v, doh, NT) - delta)).astype(jnp.bfloat16)
        dv_ref[:keys, :] += dot(p.astype(jnp.bfloat16), doh, NN)
        dk_ref[:keys, :] += dot(ds, qh, NN)
        dqt.append(dot(kt_ref[DH * h : DH * h + DH, :keys], ds, NN))
    dq_ref[rows, :] = (jnp.transpose(jnp.concatenate(dqt, 0)) * 0.125).astype(jnp.bfloat16)


class Gather:
    def __init__(self, weights, t, share, size=1 << 17):
        self.t, self.depth, self.share = t, t // 2, share
        self.ins, self.specs = list(weights), [ANY] * len(weights)
        self.shapes = [w.shape for w in weights]
        self.pieces = []
        for w, (r, c) in enumerate(self.shapes):
            rows = r
            while rows % 64 == 0 and rows * c > size:
                rows //= 2
            self.pieces += [(w, at, rows) for at in range(0, r, rows)]
        m, dma = len(self.pieces), pltpu.SemaphoreType.DMA
        self.out_shape = [jax.ShapeDtypeStruct((t,) + w.shape, w.dtype) for w in weights]
        self.scratch = [
            dma((m, self.depth)),
            dma((m, 2)),
            dma((m, self.depth)),
            dma((m, t)),
            dma((m, t, 2)),
            dma((m, t)),
            dma((m, t)),
            dma((m, t, 2)),
            dma((len(weights),)),
        ]

    def x_rows(self, n):
        half = self.pieces[n][2] // 2
        return min(int(half * self.share / 16 + 0.5) * 16, half // 32 * 16)

    def rows_of(self, n, kind, core):
        _, at, rows = self.pieces[n]
        half = rows // 2
        a = self.x_rows(n)
        start, xpos = at + core * half, self.place.xpos
        if kind == "plane":
            return pl.ds(at16(start + xpos * a), half - a)
        if kind == "x_out":
            return pl.ds(at16(start + xpos * (half - a)), a)
        return pl.ds(at16(start + (1 - xpos) * (half - a)), a)

    def steps(self, place, ins, outs, scratch):
        z_send, own_send, y_send, x_send, d_send, plane_recv, x_recv, d_recv, own_sem = scratch
        self.place = place
        me, depth, t, pieces = place.me, self.depth, self.t, self.pieces

        def has_x(n):
            return self.x_rows(n) > 0

        def rows_of(n, kind, core=place.core):
            return self.rows_of(n, kind, core)

        def part(n, block, kind, core=place.core):
            return outs[pieces[n][0]].at[block, rows_of(n, kind, core), :]

        def own(n):
            return ins[pieces[n][0]].at[rows_of(n, "plane"), :]

        line, side = place.line, place.side

        def along(n, block, sign):
            src = part(n, block, "plane")
            device = {"tensor": 2 * (line + sign) + side}
            return remote(src, src, z_send.at[n, block // 2], plane_recv.at[n, block], device)

        def z_own(n, sign):
            device = {"tensor": 2 * (line + sign) + side}
            return remote(own(n), part(n, me, "plane"), own_send.at[n, (1 - sign) // 2], plane_recv.at[n, me], device)

        def y_own(n):
            return remote(own(n), part(n, me, "plane"), y_send.at[n, line], plane_recv.at[n, me], place.y_mate)

        def y_copy(n, block):
            ref = part(n, block, "plane")
            return remote(ref, ref, y_send.at[n, block // 2], plane_recv.at[n, block], place.y_mate)

        def x_copy(n, block):
            ref = part(n, block, "x_out")
            return remote(ref, ref, x_send.at[n, block], x_recv.at[n, block], place.x_mate)

        def d_copy(n, block, k):
            ref = part(n, block, ("plane", "x_in")[k])
            return remote(ref, ref, d_send.at[n, block, k], d_recv.at[n, block, k], place.sibling)

        def own_copy(w):
            return pltpu.make_async_copy(ins[w], outs[w].at[me], own_sem.at[w])

        def ends(distance):
            yield line >= distance, line - distance, line < depth - 1, 1
            yield line < depth - distance, line + distance, line > 0, -1

        total = len(pieces)

        def launch(n):
            if n < total:
                for sign, there in ((1, line < depth - 1), (-1, line > 0)):

                    @pl.when(there)
                    def _():
                        z_own(n, sign).start()

                y_own(n).start()

        def z_stage(n, distance):
            for there, at, more, sign in ends(distance):

                @pl.when(there)
                def _():
                    block = 2 * at + side
                    landed(part(n, block, "plane"), plane_recv.at[n, block])

                    @pl.when(more)
                    def _():
                        along(n, block, sign).start()

                    y_copy(n, block).start()
                    if has_x(n):
                        x_copy(n, block).start()
                    d_copy(n, block, 0).start()

        def y_stage(n, distance):
            for there, at, _, sign in ends(distance):
                if distance == 0 and sign < 0:
                    continue

                @pl.when(there)
                def _():
                    block = 2 * at + 1 - side
                    landed(part(n, block, "plane"), plane_recv.at[n, block])
                    if has_x(n):
                        x_copy(n, block).start()
                    d_copy(n, block, 0).start()

        def x_stage(n, distance, same):
            if not has_x(n):
                return
            for there, at, _, sign in ends(distance):
                if distance == 0 and sign < 0:
                    continue

                @pl.when(there)
                def _():
                    block = 2 * at + (side if same else 1 - side)
                    landed(part(n, block, "x_in"), x_recv.at[n, block])
                    d_copy(n, block, 1).start()

        launch(0)
        for w in range(len(ins)):
            own_copy(w).start()
        yield True
        for step in range(total + depth):
            launch(step + 1)
            for late in range(depth, -1, -1):
                n = step - late
                if not 0 <= n < total:
                    continue
                if late < depth - 1:
                    z_stage(n, late + 1)
                if late < depth:
                    y_stage(n, late)
                if 0 < late < depth:
                    x_stage(n, late, True)
                if late > 0:
                    x_stage(n, late - 1, False)
            yield True
        for w in range(len(ins)):
            own_copy(w).wait()
        for n in range(total):
            y_own(n).wait_send()
            for sign, there in ((1, line < depth - 1), (-1, line > 0)):

                @pl.when(there)
                def _():
                    z_own(n, sign).wait_send()

            for distance in range(1, depth):
                for there, at, more, sign in ends(distance):

                    @pl.when(there)
                    def _():
                        y_copy(n, 2 * at + side).wait_send()

                    @pl.when(there & more)
                    def _():
                        along(n, 2 * at + side, sign).wait_send()

            def finish(i):
                block = lax.rem(me + i, t)
                for k in range(2 if has_x(n) else 1):
                    d_copy(n, block, k).wait_send()
                    landed(part(n, block, ("plane", "x_in")[k], 1 - place.core), d_recv.at[n, block, k])
                if has_x(n):
                    x_copy(n, block).wait_send()

            loop(1, t, finish)
        yield True


class Weight:
    def __init__(self, x, ys, by_cols, t):
        self.arrays, self.by_cols = [x, *ys], by_cols
        n, m = x.shape
        wide = ys[0].shape[1]
        if by_cols:
            self.height, self.width = m, wide // t
            self.rows = len(ys) * m * self.width // LANES
        else:
            self.height, self.width = m // t, wide
            self.rows = m // t * wide // LANES

    def term(self, xt, ys, at, half, t, which):
        high = self.height
        if self.by_cols and self.width < LANES:
            panel, row = at // (high // 2), at % (high // 2) + which * half
            y = ys[panel][:, rows_at(t // 2 * LANES, LANES)]
            first, second = (dot(xt[rows_at(r, half), :], y, NN) for r in (row, row + high // 2))
            odd = t % 2 == 1
            first = jnp.where(odd, pltpu.roll(first, DH, 1), first)
            second = jnp.where(odd, second, pltpu.roll(second, DH, 1))
            return [jnp.where(lane_half(first.shape, 0), first, second)]
        if self.by_cols:
            panel, row = at // high, at % high
            per = self.width // LANES
            y, col = ys[panel // per], t * self.width + panel % per * LANES
            return [dot(xt[rows_at(row + which * half, half), :], y[:, rows_at(col, LANES)], NN)]
        panels = half // high
        cols = rows_at((at // high + which * panels) * LANES, panels * LANES)
        out = dot(xt[rows_at(t * high, high), :], ys[0][:, cols], NN)
        return [out[:, i * LANES : i * LANES + LANES] for i in range(panels)]


class Reduce:
    def __init__(self, weights, t, size, y_first):
        self.t, self.depth, self.size, self.weights = t, t // 2, size, weights
        self.y_rows = int(size // 2 * y_first) // 32 * 32
        self.ins = [a for w in weights for a in w.arrays]
        self.specs = [VMEM] * len(self.ins)
        self.pieces = [(w, at) for w, g in enumerate(weights) for at in range(0, g.rows, size)]
        m, depth, dma = len(self.pieces), self.depth, pltpu.SemaphoreType.DMA
        H, Hy, Q = size // 2, self.y_rows, (size // 2 - self.y_rows) // 2

        def buf(*shape):
            return pltpu.VMEM(shape + (LANES,), jnp.bfloat16)

        self.out_shape = [jax.ShapeDtypeStruct((g.rows, LANES), jnp.bfloat16) for g in weights]
        self.scratch = [
            buf(2, 2, depth, H),
            buf(2, 2, depth, H),
            buf(m, 2, depth, H),
            buf(m, depth, Hy),
            buf(m, 2, depth, Q),
            buf(m, depth - 1, Hy),
            buf(m, depth, Q),
            buf(m, Hy),
            buf(m, Hy),
            buf(m, depth - 1, Q),
            buf(m, size),
            dma((m, 5 + 2 * depth)),
            dma((m, 5 + 2 * depth)),
            dma((m,)),
        ] + [pltpu.VMEM(w.arrays[0].shape[::-1], jnp.bfloat16) for w in weights]

    def steps(self, place, ins, outs, scratch):
        away, own, r1, r2y, r2x, r3y, r3x, s3y, r4y, r4x, fin, send, recv, store = scratch[:14]
        size, depth, pieces, t = self.size, self.depth, self.pieces, self.t
        H, Hy, Q = size // 2, self.y_rows, (size // 2 - self.y_rows) // 2
        core, xpos, line, side = place.core, place.xpos, place.line, place.side
        turned, ins, arrays = scratch[14:], list(ins), []
        for w in self.weights:
            arrays.append([ins.pop(0) for _ in w.arrays])

        def move(src, dst, n, k, device):
            return remote(src, dst, send.at[n, k], recv.at[n, k], device)

        def copy_core(n):
            return move(away.at[n % 2], r1.at[n], n, 0, place.sibling)

        def copy_y(n):
            return move(r1.at[n, 1 - side, :, pl.ds(0, Hy), :], r2y.at[n], n, 1, place.y_mate)

        def copy_x(n):
            return move(r1.at[n, :, :, pl.ds(at16(Hy + (1 - xpos) * Q), Q), :], r2x.at[n], n, 2, place.x_mate)

        def copy_yz(n, i):
            return move(r2y.at[n, place.line_at(i)], r3y.at[n, i - 1], n, 2 + i, place.z_mate(i))

        def copy_xy(n):
            return move(r2x.at[n, 1 - side], r3x.at[n], n, 2 + depth, place.y_mate)

        def copy_yx(n):
            return move(s3y.at[n], r4y.at[n], n, 3 + depth, place.x_mate)

        def copy_xz(n, i):
            return move(r3x.at[n, place.line_at(i)], r4x.at[n, i - 1], n, 3 + depth + i, place.z_mate(i))

        def copy_xx(n):
            ref = fin.at[n, pl.ds(at16(core * H + Hy + xpos * Q), Q), :]
            return move(ref, ref, n, 3 + 2 * depth, place.x_mate)

        def copy_back(n):
            ref = fin.at[n, pl.ds(at16(core * H), H), :]
            return move(ref, ref, n, 4 + 2 * depth, place.sibling)

        def write(n):
            w, at = pieces[n]
            return pltpu.make_async_copy(fin.at[n], outs[w].at[pl.ds(at, size), :], store.at[n])

        def make(n):
            w, at = pieces[n]
            weight, (x, *ys) = self.weights[w], arrays[w]
            if n == 0 or pieces[n - 1][0] != w:
                turned[w][...] = jnp.transpose(x[...])
            if n >= 2:
                copy_core(n - 2).wait_send()
            for which, into in ((1 - core, away), (core, own)):

                def block(i):
                    parts = weight.term(turned[w], ys, at, H, i, which)
                    high = parts[0].shape[0]
                    for j, part in enumerate(parts):
                        into[n % 2, i % 2, i // 2, j * high : j * high + high, :] = part.astype(jnp.bfloat16)

                loop(0, t, block)
                if into is away:
                    copy_core(n).start()

        def stage0(n):
            copy_core(n).wait_recv()

            def add(i):
                a, b = i // depth, i % depth
                r1[n, a, b] = r1[n, a, b] + own[n % 2, a, b]

            loop(0, 2 * depth, add)
            if Hy:
                copy_y(n).start()
            copy_x(n).start()

        def stage1(n):
            if Hy:
                copy_y(n).wait_recv()

                def add(i):
                    r2y[n, i] = r2y[n, i] + r1[n, side, i, 0:Hy, :]

                loop(0, depth, add)
                for i in range(1, depth):
                    copy_yz(n, i).start()
            copy_x(n).wait_recv()

            def addx(i):
                a, b = i // depth, i % depth
                r2x[n, a, b] = r2x[n, a, b] + r1[n, a, b, pl.ds(at16(Hy + xpos * Q), Q), :]

            loop(0, 2 * depth, addx)
            copy_xy(n).start()

        def stage2(n):
            copy_xy(n).wait_recv()

            def add(i):
                r3x[n, i] = r3x[n, i] + r2x[n, side, i]

            loop(0, depth, add)
            for i in range(1, depth):
                copy_xz(n, i).start()
            if Hy:
                for i in range(1, depth):
                    copy_yz(n, i).wait_recv()
                part = r2y[n, line].astype(jnp.float32)
                for i in range(1, depth):
                    part = part + r3y[n, i - 1].astype(jnp.float32)
                s3y[n] = part.astype(jnp.bfloat16)
                copy_yx(n).start()

        def stage3(n):
            for i in range(1, depth):
                copy_xz(n, i).wait_recv()
            part = r3x[n, line].astype(jnp.float32)
            for i in range(1, depth):
                part = part + r4x[n, i - 1].astype(jnp.float32)
            fin[n, pl.ds(at16(core * H + Hy + xpos * Q), Q), :] = part.astype(jnp.bfloat16)
            copy_xx(n).start()
            if Hy:
                copy_yx(n).wait_recv()
                fin[n, pl.ds(at16(core * H), Hy), :] = s3y[n] + r4y[n]

        def stage4(n):
            copy_xx(n).wait_recv()
            copy_back(n).start()

        def stage5(n):
            copy_back(n).wait_recv()
            write(n).start()

        total = len(pieces)
        make(0)
        yield True
        stages = [stage0, stage1, stage2, stage3, stage4, stage5]
        for step in range(total + len(stages) - 1):
            for k in range(len(stages) - 1, -1, -1):
                if 0 <= step - k < total:
                    stages[k](step - k)
            if step + 1 < total:
                make(step + 1)
            yield True
        for n in range(total):
            if n >= total - 2:
                copy_core(n).wait_send()
            copy_x(n).wait_send()
            copy_xy(n).wait_send()
            copy_xx(n).wait_send()
            copy_back(n).wait_send()
            for i in range(1, depth):
                copy_xz(n, i).wait_send()
            if Hy:
                copy_y(n).wait_send()
                copy_yx(n).wait_send()
                for i in range(1, depth):
                    copy_yz(n, i).wait_send()
            write(n).wait()
        yield True


class Back:
    def __init__(self, ys, weight, rest=None, factor=1.0):
        self.count, self.has_rest, self.factor = len(ys), rest is not None, factor
        self.ins = [*ys, weight] + ([rest] if self.has_rest else [])
        self.specs = [VMEM] * self.count + [ANY] + [VMEM] * self.has_rest
        n, (t, d, c) = ys[0].shape[0], weight.shape
        self.blocks = t
        self.out_shape = [jax.ShapeDtypeStruct((n, d), jnp.float32)]
        self.scratch = [
            pltpu.VMEM((2, d, c), jnp.bfloat16),
            pltpu.VMEM((n, d), jnp.float32),
            pltpu.SemaphoreType.DMA((3,)),
        ]

    def steps(self, place, ins, outs, scratch):
        held, total, sem = scratch
        ys, weight = ins[: self.count], ins[self.count]
        width = held.shape[2] // self.count

        def load(i):
            return pltpu.make_async_copy(weight.at[i], held.at[i % 2], sem.at[i % 2])

        load(0).start()
        for i in range(self.blocks):
            load(i).wait()
            if i + 1 < self.blocks:
                load(i + 1).start()
            y = [y_ref[:, i * width : i * width + width] for y_ref in ys]
            term = dot(jnp.concatenate(y, 1) if len(y) > 1 else y[0], held[i % 2], NT)
            if i:
                total[...] += term
            else:
                total[...] = term + self.factor * ins[-1][...] if self.has_rest else term
            yield True
        out = pltpu.make_async_copy(total, outs[0], sem.at[2])
        out.start()
        out.wait()
        yield True


class Total:
    def __init__(self, value, t):
        self.depth = t // 2
        rows, dma = value.shape[0], pltpu.SemaphoreType.DMA
        self.ins, self.specs = [value], [ANY]
        self.out_shape = [jax.ShapeDtypeStruct(value.shape, jnp.float32)]
        self.scratch = [
            pltpu.VMEM((self.depth, rows, LANES), jnp.float32),
            pltpu.VMEM((3, 2, rows, LANES), jnp.float32),
            dma((self.depth + 3,)),
            dma((self.depth + 3,)),
            dma((2,)),
        ]

    def steps(self, place, ins, outs, scratch):
        along, pair, send, recv, local = scratch
        depth = self.depth

        def z_copy(i):
            return remote(ins[0], along.at[place.line], send.at[i], recv.at[i], place.z_mate(i))

        def swap_copy(k):
            device = (place.y_mate, place.x_mate, place.sibling)[k]
            return remote(pair.at[k, 0], pair.at[k, 1], send.at[depth + k], recv.at[depth + k], device)

        own = pltpu.make_async_copy(ins[0], along.at[place.line], local.at[0])
        own.start()
        for i in range(1, depth):
            z_copy(i).start()
        yield True
        own.wait()
        for i in range(1, depth):
            landed(along.at[place.line_at(depth - i)], recv.at[i])
        total = along[0]
        for i in range(1, depth):
            total = total + along[i]
        for k in range(3):
            pair[k, 0] = total
            swap_copy(k).start()
            yield True
            swap_copy(k).wait_recv()
            total = pair[k, 0] + pair[k, 1]
        for i in range(1, depth):
            z_copy(i).wait_send()
        for k in range(3):
            swap_copy(k).wait_send()
        pair[0, 0] = total
        out = pltpu.make_async_copy(pair.at[0, 0], outs[0], local.at[1])
        out.start()
        out.wait()
        yield True


class Together:
    def __init__(self, *jobs):
        self.jobs = jobs
        self.ins = [a for j in jobs for a in j.ins]
        self.specs = [a for j in jobs for a in j.specs]
        self.out_shape = [a for j in jobs for a in j.out_shape]
        self.scratch = [a for j in jobs for a in j.scratch]

    def steps(self, place, ins, outs, scratch):
        ins, outs, scratch, running = list(ins), list(outs), list(scratch), []
        for j in self.jobs:
            a, b, c = len(j.ins), len(j.out_shape), len(j.scratch)
            running.append(j.steps(place, ins[:a], outs[:b], scratch[:c]))
            ins, outs, scratch = ins[a:], outs[b:], scratch[c:]
        while running:
            running = [g for g in running if next(g, None) is not None]
            yield True


class Nothing:
    ins, specs, out_shape, scratch = [], [], [], []

    def steps(self, place, ins, outs, scratch):
        yield from ()


ANY = pl.BlockSpec(memory_space=pl.ANY)
VMEM = pl.BlockSpec(memory_space=pltpu.VMEM)


def communicate(body, out_shape, ins, in_specs, out_specs, scratch, cid):
    return pl.pallas_call(
        body,
        out_shape=out_shape,
        in_specs=in_specs,
        out_specs=out_specs,
        scratch_shapes=scratch,
        compiler_params=pltpu.CompilerParams(collective_id=cid, has_side_effects=True, vmem_limit_bytes=58 << 20),
    )(*ins)


def jobs_kernel(jobs, t, cid):
    counts = [len(j.ins) for j in jobs]
    gives = [len(j.out_shape) for j in jobs]
    sizes = [len(j.scratch) for j in jobs]

    def body(*refs):
        place = Place(t)
        place.greet()
        refs = list(refs)
        ins = [[refs.pop(0) for _ in range(c)] for c in counts]
        outs = [[refs.pop(0) for _ in range(c)] for c in gives]
        scratch = [[refs.pop(0) for _ in range(c)] for c in sizes]
        running = [j.steps(place, i, o, s) for j, i, o, s in zip(jobs, ins, outs, scratch)]
        while running:
            running = [g for g in running if next(g, None) is not None]

    return communicate(
        body,
        [s for j in jobs for s in j.out_shape],
        [a for j in jobs for a in j.ins],
        [a for j in jobs for a in j.specs],
        [ANY] * sum(gives),
        [s for j in jobs for s in j.scratch],
        cid,
    )


def attend(tokens_qkv, t, causal, bq, job, lead, each, cid):
    n, d = tokens_qkv[0].shape
    slots = Slots(t, n, d)
    pairs = slots.pairs
    held = jax.ShapeDtypeStruct((pairs, LEN, LANES), jnp.bfloat16)
    extra, gives = len(job.ins), len(job.out_shape)

    def body(*refs):
        qkv, refs = refs[:3], refs[3:]
        job_refs, refs = refs[:extra], refs[extra:]
        out, saved, lse, refs = refs[0], refs[1:5], refs[5], refs[6:]
        job_outs, refs = refs[:gives], refs[gives:]
        here, (hs, hr, ts, tr, keep), refs = refs[:4], refs[4:9], refs[9:]
        place = Place(t)
        place.greet()

        def main():
            move = ToHeads(place, slots, qkv, here[:3], hs, hr)
            back = ToTokens(place, slots, here[3:], [out], ts, tr)
            move.start()
            yield lead
            for slot in range(pairs):
                move.wait_slot(slot)
                for i in range(LEN // bq):
                    attend_block(i, bq, causal, *(r.at[slot] for r in here), lse.at[slot])
                    yield each
                back.start_slot(slot)
            copies = [pltpu.make_async_copy(h, s, keep.at[i]) for i, (h, s) in enumerate(zip(here, saved))]
            for c in copies:
                c.start()
            move.finish()
            yield -1
            back.finish()
            for c in copies:
                c.wait()

        weave(main(), job.steps(place, job_refs, job_outs, refs))

    out = communicate(
        body,
        [jax.ShapeDtypeStruct((n, d), jnp.bfloat16)]
        + [held] * 4
        + [jax.ShapeDtypeStruct((pairs, 8, LEN), jnp.float32)]
        + job.out_shape,
        [*tokens_qkv, *job.ins],
        [ANY] * 3 + job.specs,
        [ANY] * 5 + [VMEM] + [ANY] * gives,
        [pltpu.VMEM(held.shape, held.dtype)] * 4
        + reshard_sems(slots, 3, 1)
        + [pltpu.SemaphoreType.DMA((4,))]
        + job.scratch,
        cid,
    )
    return out[0], out[1:6], out[6:]


def attend_back(grad, saved, t, causal, bq, job, lead, every, cid):
    n, d = grad.shape
    slots = Slots(t, n, d)
    pairs = slots.pairs
    held = pltpu.VMEM((pairs, LEN, LANES), jnp.bfloat16)
    extra, gives = len(job.ins), len(job.out_shape)

    def body(grad_ref, q, k, v, o, lse, *refs):
        job_refs, refs = refs[:extra], refs[extra:]
        outs, refs = refs[:3], refs[3:]
        job_outs, refs = refs[:gives], refs[gives:]
        (do, *made, kt, dk, dv, hs, hr, ts, tr), refs = refs[:11], refs[11:]
        place = Place(t)
        place.greet()

        def main():
            move = ToHeads(place, slots, [grad_ref], [do], hs, hr)
            back = ToTokens(place, slots, made, outs, ts, tr)
            move.start()
            yield lead
            count = 0
            for slot in range(pairs):
                move.wait_slot(slot)
                dk[...] = jnp.zeros_like(dk)
                dv[...] = jnp.zeros_like(dv)
                kt[...] = jnp.transpose(k[slot])
                for i in range(LEN // bq):
                    attend_back_block(
                        i,
                        bq,
                        causal,
                        *(r.at[slot] for r in (q, k, v, o, lse, do, made[0])),
                        kt,
                        dk,
                        dv,
                    )
                    count += 1
                    yield 1 if count % every == 0 else 0
                made[1][slot] = dk[...].astype(jnp.bfloat16)
                made[2][slot] = dv[...].astype(jnp.bfloat16)
                back.start_slot(slot)
            move.finish()
            yield -1
            back.finish()

        weave(main(), job.steps(place, job_refs, job_outs, refs))

    out = communicate(
        body,
        [jax.ShapeDtypeStruct((n, d), jnp.bfloat16)] * 3 + job.out_shape,
        [grad, *saved, *job.ins],
        [ANY] + [VMEM] * 5 + job.specs,
        [ANY] * (3 + gives),
        [held] * 4
        + [pltpu.VMEM((LANES, LEN), jnp.bfloat16)]
        + [pltpu.VMEM((LEN, LANES), jnp.float32)] * 2
        + reshard_sems(slots, 1, 3)
        + job.scratch,
        cid,
    )
    return out[:3], out[3:]


def cols_kernel(count, x_ref, w_ref, *outs):
    out = dot(x_ref[...], w_ref[0], NN)
    width = out.shape[1] // count
    for i, o_ref in enumerate(outs):
        o_ref[...] = out[:, i * width : (i + 1) * width].astype(o_ref.dtype)


def cols_product(x, weight, count, dtype=jnp.bfloat16):
    n, d = x.shape
    t, _, c = weight.shape
    width = c // count
    return pl.pallas_call(
        functools.partial(cols_kernel, count),
        grid=(t,),
        out_shape=[jax.ShapeDtypeStruct((n, t * width), dtype)] * count,
        in_specs=[
            pl.BlockSpec((n, d), lambda i: (0, 0)),
            pl.BlockSpec((1, d, c), lambda i: (i, 0, 0)),
        ],
        out_specs=[pl.BlockSpec((n, width), lambda i: (0, i))] * count,
        compiler_params=pltpu.CompilerParams(vmem_limit_bytes=48 << 20),
        cost_estimate=pl.CostEstimate(
            flops=2 * n * d * t * c, bytes_accessed=2 * (t * d * c + n * d + n * t * c), transcendentals=0
        ),
    )(x, weight)


def back_kernel(count, *refs):
    ys, w_ref, o_ref = refs[:count], refs[count], refs[count + 1]
    y = jnp.concatenate([y_ref[...] for y_ref in ys], 1) if count > 1 else ys[0][...]
    term = dot(y, w_ref[0], NT)

    @pl.when(pl.program_id(0) == 0)
    def _():
        o_ref[...] = term

    @pl.when(pl.program_id(0) != 0)
    def _():
        o_ref[...] += term


def back_product(ys, weight):
    count = len(ys)
    n = ys[0].shape[0]
    t, d, c = weight.shape
    width = c // count
    return pl.pallas_call(
        functools.partial(back_kernel, count),
        grid=(t,),
        out_shape=jax.ShapeDtypeStruct((n, d), jnp.float32),
        in_specs=[pl.BlockSpec((n, width), lambda i: (0, i))] * count
        + [pl.BlockSpec((1, d, c), lambda i: (i, 0, 0))],
        out_specs=pl.BlockSpec((n, d), lambda i: (0, 0)),
        compiler_params=pltpu.CompilerParams(vmem_limit_bytes=48 << 20),
        cost_estimate=pl.CostEstimate(
            flops=2 * n * d * t * c, bytes_accessed=2 * (t * d * c + 2 * n * d + n * t * c), transcendentals=0
        ),
    )(*ys, weight)


def forward_kernel(x_ref, w_ref, b_ref, v_ref, act_ref, slope_ref, o_ref):
    v = dot(x_ref[...], w_ref[0], NN) + b_ref[...].astype(jnp.float32)
    square = v * v
    th = jnp.tanh(math.sqrt(2 / math.pi) * v * (1 + 0.044715 * square))
    half = 0.5 * (1 + th)
    act = (v * half).astype(jnp.bfloat16)
    act_ref[...] = act
    inner = math.sqrt(2 / math.pi) * (1 + 3 * 0.044715 * square)
    slope_ref[...] = (half + 0.5 * v * (1 - th * th) * inner).astype(jnp.bfloat16)
    term = dot(act, v_ref[0], NN)

    @pl.when(pl.program_id(0) == 0)
    def _():
        o_ref[...] = term

    @pl.when(pl.program_id(0) != 0)
    def _():
        o_ref[...] += term


def forward_hidden(x, w_hid, bias, w_out):
    n, d = x.shape
    t, _, c = w_hid.shape
    low = jax.ShapeDtypeStruct((n, t * c), jnp.bfloat16)
    part = pl.BlockSpec((n, c), lambda i: (0, i))
    whole = pl.BlockSpec((n, d), lambda i: (0, 0))
    return pl.pallas_call(
        forward_kernel,
        grid=(t,),
        out_shape=[low, low, jax.ShapeDtypeStruct((n, d), jnp.float32)],
        in_specs=[
            whole,
            pl.BlockSpec((1, d, c), lambda i: (i, 0, 0)),
            pl.BlockSpec((1, c), lambda i: (0, i)),
            pl.BlockSpec((1, c, d), lambda i: (i, 0, 0)),
        ],
        out_specs=[part, part, whole],
        compiler_params=pltpu.CompilerParams(vmem_limit_bytes=48 << 20),
        cost_estimate=pl.CostEstimate(
            flops=4 * n * d * t * c, bytes_accessed=4 * t * d * c + 4 * n * t * c, transcendentals=n * t * c
        ),
    )(x, w_hid, bias, w_out)


def backward_kernel(g_ref, v_ref, slope_ref, w_ref, gh_ref, sum_ref, o_ref):
    grad = dot(g_ref[...], v_ref[0], NT) * slope_ref[...].astype(jnp.float32)
    grad = grad.astype(jnp.bfloat16)
    gh_ref[...] = grad
    sum_ref[...] = jnp.sum(grad.astype(jnp.float32), axis=0, keepdims=True)
    term = dot(grad, w_ref[0], NT)

    @pl.when(pl.program_id(0) == 0)
    def _():
        o_ref[...] = term

    @pl.when(pl.program_id(0) != 0)
    def _():
        o_ref[...] += term


def backward_hidden(grad, w_out, slopes, w_hid):
    n, d = grad.shape
    t, _, c = w_hid.shape
    part = pl.BlockSpec((n, c), lambda i: (0, i))
    whole = pl.BlockSpec((n, d), lambda i: (0, 0))
    return pl.pallas_call(
        backward_kernel,
        grid=(t,),
        out_shape=[
            jax.ShapeDtypeStruct((n, t * c), jnp.bfloat16),
            jax.ShapeDtypeStruct((1, t * c), jnp.float32),
            jax.ShapeDtypeStruct((n, d), jnp.float32),
        ],
        in_specs=[
            whole,
            pl.BlockSpec((1, c, d), lambda i: (i, 0, 0)),
            part,
            pl.BlockSpec((1, d, c), lambda i: (i, 0, 0)),
        ],
        out_specs=[part, pl.BlockSpec((1, c), lambda i: (0, i)), whole],
        compiler_params=pltpu.CompilerParams(vmem_limit_bytes=48 << 20),
        cost_estimate=pl.CostEstimate(
            flops=4 * n * d * t * c, bytes_accessed=4 * t * d * c + 4 * n * t * c, transcendentals=0
        ),
    )(grad, w_out, slopes, w_hid)


def cols_weight(x, ys, t):
    return Weight(x, ys, True, t)


def rows_weight(x, y, t):
    return Weight(x, [y], False, t)


def cols_result(total, count, d, width):
    total = total.astype(jnp.float32)
    if width < LANES:
        parts = total.reshape(count, d // 2, 2, width).transpose(2, 1, 0, 3)
        return parts.reshape(d, count * width)
    return total.reshape(-1, d, LANES).transpose(1, 0, 2).reshape(d, count * width)


def rows_grad_kernel(x_ref, y_ref, o_ref):
    out = dot(jnp.transpose(x_ref[...]), y_ref[...], NN).astype(o_ref.dtype)
    r = out.shape[0]
    for j in range(out.shape[1] // LANES):
        o_ref[0, 0, j * r : j * r + r, :] = out[:, j * LANES : j * LANES + LANES]


def rows_grad(x, y, t):
    n, d = y.shape
    blocks = min(t, x.shape[1] // LANES)
    r = x.shape[1] // blocks
    whole = blocks == t
    size = d // LANES * r
    out = pl.pallas_call(
        rows_grad_kernel,
        grid=(blocks,),
        out_shape=jax.ShapeDtypeStruct((2, t // 2, size, LANES) if whole else (blocks, 1, size, LANES), jnp.bfloat16),
        in_specs=[pl.BlockSpec((n, r), lambda i: (0, i)), pl.BlockSpec((n, d), lambda i: (0, 0))],
        out_specs=pl.BlockSpec(
            (1, 1, size, LANES), (lambda i: (i % 2, i // 2, 0, 0)) if whole else (lambda i: (i, 0, 0, 0))
        ),
        compiler_params=pltpu.CompilerParams(vmem_limit_bytes=48 << 20),
        cost_estimate=pl.CostEstimate(
            flops=2 * n * d * blocks * r, bytes_accessed=2 * (blocks * d * r + n * d + n * blocks * r), transcendentals=0
        ),
    )(x, y)
    if whole:
        return out
    m = t // blocks
    parts = out.reshape(blocks, d // LANES, m, r // m, LANES).transpose(0, 2, 1, 3, 4)
    return by_side(parts.reshape(t, size // m, LANES), t)


def rows_result(total, r, d):
    return total.astype(jnp.float32).reshape(d // LANES, r, LANES).transpose(1, 0, 2).reshape(r, d)


def gather_weight(weight):
    dp, t = lax.axis_size("dp"), lax.axis_size("tensor")
    rows = weight.shape[0] // dp
    share = lax.dynamic_slice_in_dim(weight, lax.axis_index("dp") * rows, rows, 0)
    whole = lax.all_gather(share, ("tensor", "dp"), axis=0, tiled=True)
    return whole.reshape(t, weight.shape[0], weight.shape[1])


def widen(weight, count):
    t, r, c = weight.shape
    width = c // count
    if width % LANES == 0:
        return weight
    m = LANES // width
    parts = weight.reshape(t // m, m, r, count, width).transpose(0, 2, 3, 1, 4)
    return parts.reshape(t // m, r, count * LANES)


def swap(value, axis, bit):
    size = lax.axis_size(axis)
    return lax.ppermute(value, axis, [(i, i ^ bit) for i in range(size)])


def settle(total):
    bit = 4
    while bit < lax.axis_size("dp"):
        total = total + swap(total, "dp", bit)
        bit *= 2
    return total


def normalize(rows_in, gain_row, shift_row):
    row_mean = jnp.mean(rows_in, axis=-1, keepdims=True)
    centered = rows_in - row_mean
    variance = jnp.mean(centered * centered, axis=-1, keepdims=True)
    return centered * lax.rsqrt(variance + norm_eps) * gain_row + shift_row


def gelu_tanh(values):
    return jax.nn.gelu(values, approximate=True)


def product(values, weight):
    return jnp.dot(values, weight, preferred_element_type=jnp.float32)


def per_device(
    tokens,
    memory,
    self_qkv,
    self_out,
    cross_q,
    cross_kv,
    cross_out,
    hidden_weight,
    hidden_bias,
    output_weight,
    output_bias,
    norm_gain,
    norm_shift,
    grad_output,
):
    low = jnp.bfloat16
    t = lax.axis_size("tensor")
    n, d = tokens.shape
    size = LEN * 8 // t
    units = hidden_bias.shape[0]
    bias_block = jnp.pad(hidden_bias, (0, 64 * LANES - units)).reshape(64, LANES)
    first = [self_qkv.reshape(d, -1), bias_block]
    w_qkv, bias_all = jobs_kernel([Gather(first, t, 0.36, 1 << 18)], t, 0)
    w_qkv = widen(w_qkv, 3)
    bias_all = bias_all.reshape(t, -1)[:, :units].reshape(1, -1)

    qkv = cols_product(tokens, w_qkv, 3)
    second = [self_out, cross_q, cross_kv.reshape(d, -1), cross_out]
    self_heads, self_saved, (w_so, w_cq, w_kv, w_co) = attend(
        qkv, t, True, 512, Gather(second, t, 0.36), 4, 1, 1
    )
    w_cq, w_kv = widen(w_cq, 1), widen(w_kv, 2)
    w_so, w_co = w_so.reshape(d, d), w_co.reshape(d, d)
    branch_one = product(self_heads, w_so)
    normed_one, pull_one = jax.vjp(
        normalize, residual_alpha * tokens.astype(jnp.float32) + branch_one, norm_gain[0], norm_shift[0]
    )
    normed_one_low = normed_one.astype(low)
    kv = cols_product(memory, w_kv, 2)
    cq = cols_product(normed_one_low, w_cq, 1)
    third = [hidden_weight, output_weight]
    cross_heads, cross_saved, (w_hid, w_out) = attend([*cq, *kv], t, False, 512, Gather(third, t, 0.36), 4, 1, 2)
    branch_two = product(cross_heads, w_co)
    normed_two, pull_two = jax.vjp(
        normalize, residual_alpha * normed_one + branch_two, norm_gain[1], norm_shift[1]
    )
    normed_two_low = normed_two.astype(low)
    activated, slopes, branch_three = forward_hidden(normed_two_low, w_hid, bias_all, w_out)
    layer_out, pull_three = jax.vjp(
        normalize, residual_alpha * normed_two + branch_three + output_bias, norm_gain[2], norm_shift[2]
    )
    grad_three, gain_three, shift_three = pull_three(grad_output.astype(jnp.float32))
    bias_out_grad = jnp.sum(grad_three, axis=0)
    grad_three_low = grad_three.astype(low)
    grad_hidden, hidden_bias_grad, grad_normed = backward_hidden(grad_three_low, w_out, slopes, w_hid)
    grad_two, gain_two, shift_two = pull_two(
        residual_alpha * grad_three + grad_normed
    )
    grad_two_low = grad_two.astype(low)
    grad_co = lax.dot_general(grad_two_low, w_co, NT, preferred_element_type=jnp.float32).astype(low)
    reduce_ff = Reduce(
        [rows_weight(activated, grad_three_low, t), cols_weight(normed_two_low, [grad_hidden], t)], t, size, 0.25
    )
    (g_cq, g_ck, g_cv), (out_weight_grad, hidden_weight_grad) = attend_back(
        grad_co, cross_saved, t, False, 256, reduce_ff, 2, 2, 3
    )
    grad_one, gain_one, shift_one = pull_one(residual_alpha * grad_two + back_product([g_cq], w_cq))
    grad_one_low = grad_one.astype(low)
    grad_so = lax.dot_general(grad_one_low, w_so, NT, preferred_element_type=jnp.float32).astype(low)
    reduce_cross = Reduce(
        [
            rows_weight(cross_heads, grad_two_low, t),
            cols_weight(normed_one_low, [g_cq], t),
            cols_weight(memory, [g_ck, g_cv], t),
            rows_weight(self_heads, grad_one_low, t),
        ],
        t,
        size,
        0.25,
    )
    beside = Together(reduce_cross, Back([g_ck, g_cv], w_kv))
    g_qkv, (cross_out_grad, cross_q_grad, cross_kv_grad, self_out_grad, grad_memory) = attend_back(
        grad_so, self_saved, t, True, 256, beside, 2, 2, 4
    )
    small = jnp.concatenate(
        [gain_one, gain_two, gain_three, shift_one, shift_two, shift_three, bias_out_grad, hidden_bias_grad[0]]
    ).reshape(-1, LANES)
    self_qkv_grad, small, grad_tokens = jobs_kernel(
        [
            Reduce([cols_weight(tokens, g_qkv, t)], t, size, 0.5),
            Total(small, t),
            Back(g_qkv, w_qkv, grad_one, residual_alpha),
        ],
        t,
        5,
    )
    small = settle(small).reshape(-1)
    gain_total, shift_total = small[: 3 * d].reshape(3, d), small[3 * d : 6 * d].reshape(3, d)
    bias_total = small[6 * d : 7 * d]
    hidden_bias_total = lax.dynamic_slice_in_dim(small, 7 * d + lax.axis_index("tensor") * units, units, 0)
    out_weight_grad = rows_result(settle(out_weight_grad), output_weight.shape[0], d)
    hidden_weight_grad = cols_result(settle(hidden_weight_grad), 1, d, hidden_weight.shape[1])
    cross_out_grad = rows_result(settle(cross_out_grad), cross_out.shape[0], d)
    cross_q_grad = cols_result(settle(cross_q_grad), 1, d, cross_q.shape[1])
    cross_kv_grad = cols_result(settle(cross_kv_grad), 2, d, cross_kv.shape[2]).reshape(cross_kv.shape)
    self_out_grad = rows_result(settle(self_out_grad), self_out.shape[0], d)
    self_qkv_grad = cols_result(settle(self_qkv_grad), 3, d, self_qkv.shape[2]).reshape(self_qkv.shape)
    return (
        layer_out.astype(low),
        grad_tokens,
        grad_memory,
        self_qkv_grad,
        self_out_grad,
        cross_q_grad,
        cross_kv_grad,
        cross_out_grad,
        hidden_weight_grad,
        hidden_bias_total,
        out_weight_grad,
        bias_total,
        gain_total,
        shift_total,
    )


def solution(mesh):
    return jax.shard_map(
        per_device,
        mesh=mesh,
        in_specs=(
            P(("dp", "tensor"), None),
            P(("dp", "tensor"), None),
            P(None, None, "tensor"),
            P("tensor", None),
            P(None, "tensor"),
            P(None, None, "tensor"),
            P("tensor", None),
            P(None, "tensor"),
            P("tensor"),
            P("tensor", None),
            P(),
            P(),
            P(),
            P(("dp", "tensor"), None),
        ),
        out_specs=(
            P(("dp", "tensor"), None),
            P(("dp", "tensor"), None),
            P(("dp", "tensor"), None),
            P(None, None, "tensor"),
            P("tensor", None),
            P(None, "tensor"),
            P(None, None, "tensor"),
            P("tensor", None),
            P(None, "tensor"),
            P("tensor"),
            P("tensor", None),
            P(),
            P(),
            P(),
        ),
        check_vma=False,
    )
```
